32 devices in a mesh: dp: 4 (over x, core), fsdp: 8 (over z, y).
Axes of the slice: x: 2, y: 2, z: 4, core: 2. Of those that a mesh axis runs over, the one named last changes fastest.
Arguments:
- tokens: bfloat16 [192, 296, 512], P(('dp', 'fsdp')), as said below
- cotangent: bfloat16 [192, 296, 512], P(('dp', 'fsdp')), may hold values from -6 to 6
- lengths: int32 [192], P(('dp', 'fsdp')), may hold values from 37 to 296, as said below
- valid_mask: int32 [192, 296], P(('dp', 'fsdp')), may hold values 0 or 1
- action_bins: int32 [192, 296, 11], P(('dp', 'fsdp')), may hold values from 0 to 255
- value_head: bfloat16 [2816, 512], replicated, may hold values from -0.25 to 0.25
- w_triple: float32 [512, 1536], P('fsdp')
- w_mixer: float32 [512, 512], P('fsdp')
- w_expand: float32 [512, 2048], P('fsdp')
- w_reduce: float32 [2048, 512], P('fsdp')
- norm_params: float32 [512, 4], replicated, as said below
- first_triple: float32 [512, 1536], P('fsdp')
- first_mixer: float32 [512, 512], P('fsdp')
- first_expand: float32 [512, 2048], P('fsdp')
- first_reduce: float32 [2048, 512], P('fsdp')
- first_norms: float32 [512, 4], replicated
- second_triple: float32 [512, 1536], P('fsdp'), as said below
- second_mixer: float32 [512, 512], P('fsdp'), as said below
- second_expand: float32 [512, 2048], P('fsdp'), as said below
- second_reduce: float32 [2048, 512], P('fsdp'), as said below
- second_norms: float32 [512, 4], replicated, as said below
Outputs:
- block_out: bfloat16 [192, 296, 512], P(('dp', 'fsdp'))
- input_grad: bfloat16 [192, 296, 512], P(('dp', 'fsdp'))
- new_triple: float32 [512, 1536], P('fsdp')
- new_mixer: float32 [512, 512], P('fsdp')
- new_expand: float32 [512, 2048], P('fsdp')
- new_reduce: float32 [2048, 512], P('fsdp')
- momentum_triple: float32 [512, 1536], P('fsdp')
- momentum_mixer: float32 [512, 512], P('fsdp')
- momentum_expand: float32 [512, 2048], P('fsdp')
- momentum_reduce: float32 [2048, 512], P('fsdp')
- variance_triple: float32 [512, 1536], P('fsdp')
- variance_mixer: float32 [512, 512], P('fsdp')
- variance_expand: float32 [512, 2048], P('fsdp')
- variance_reduce: float32 [2048, 512], P('fsdp')
- new_norms: float32 [512, 4], replicated
- momentum_norms: float32 [512, 4], replicated
- variance_norms: float32 [512, 4], replicated
- norm_table: float32 [2, 8], replicated
- value_mean: float32 [11], replicated
- value_peak: float32 [11], replicated
The draws below stay inside these ranges and needn't reach their ends.
Inputs may be any that keep to these rules, and one draw needn't show every extreme that they name: `lengths`: every episode has at least 37 rows; an episode of the first device has exactly 37 and one of the last device exactly 296. `tokens`: rows of order one. `norm_params`: gains positive. `second_triple`: positive. `second_mixer`: positive. `second_expand`: positive. `second_reduce`: positive. `second_norms`: positive.
All inputs are finite; a program needn't handle non-finite values. No bound on the sum of `valid_mask` on one device may be relied on, other than what follows from the above.
Results may differ from the reference program's by a relative error of at most 0.012.
The reference program's roundings to bfloat16 on the way count: a program that leaves them out, or rounds other values in their place, can miss the bound.
Values may be sent and summed in bfloat16 or wider, within the bound.
No kernel may reach another device: no remote copies, remote signals or barrier semaphores. Data moves between devices by JAX's collectives and lax.ppermute only.
A program may use at most 256 MiB of HBM per device.

```python
import jax
import jax.numpy as jnp
from jax import lax

D = 512
HEADS = 8
HEAD_DIM = 64
FF = 2048
ACT = 11
NBINS = 256
LMAX = 296
EP_DEV = 6
STEP = 5
EPISODES = 192
N_DP = 4
N_FSDP = 8


def row_ramp(rows_count):
    return 0.4 + 1.6 * jnp.arange(rows_count, dtype=jnp.float32) / rows_count


def row_fall(rows_count):
    return 2.0 - 1.6 * jnp.arange(rows_count, dtype=jnp.float32) / rows_count


def base_draw(key, shape):
    return jax.random.normal(key, shape, jnp.float32)


def matrix_draw(key, rows_count, columns_count, fan_count):
    return base_draw(key, (rows_count, columns_count)) * row_ramp(rows_count)[:, None] * fan_count ** (-0.5)


def draw_tokens(key, part):
    key_base = jax.random.fold_in(key, 11)
    key_drift = jax.random.fold_in(key, 12)
    drift = jax.random.normal(key_drift, (D,), jnp.float32)
    slope = -1.5 + 3.0 * jnp.arange(EPISODES, dtype=jnp.float32) / max(EPISODES - 1, 1)
    return (base_draw(key_base, (EPISODES, LMAX, D)) + slope[:, None, None] * drift[None, None, :]).astype(jnp.bfloat16)


def draw_lengths(key, part):
    key_main = jax.random.fold_in(key, 21)
    key_long = jax.random.fold_in(key, 22)
    key_short = jax.random.fold_in(key, 23)
    index_all = jnp.arange(EPISODES)
    device = index_all // EP_DEV
    along_dp = device // N_FSDP
    along_fsdp = device % N_FSDP
    ceiling = 3 * LMAX // 8 + 5 * LMAX // 16 * along_fsdp // max(N_FSDP - 1, 1) + 5 * LMAX // 16 * along_dp // max(N_DP - 1, 1)
    drawn = jax.random.randint(key_main, (EPISODES,), LMAX // 8, ceiling + 1)
    longest = EPISODES - 1 - jax.random.randint(key_long, (), 0, EP_DEV)
    shortest = jax.random.randint(key_short, (), 0, EP_DEV)
    drawn = jnp.where(index_all == longest, LMAX, drawn)
    drawn = jnp.where(index_all == shortest, LMAX // 8, drawn)
    return drawn.astype(jnp.int32)


def draw_w_triple(key, part):
    return matrix_draw(key, D, 3 * D, D)


def draw_w_mixer(key, part):
    return matrix_draw(key, D, D, D) * (0.25 * LMAX ** 0.5)


def draw_w_expand(key, part):
    return matrix_draw(key, D, FF, D)


def draw_w_reduce(key, part):
    return matrix_draw(key, FF, D, FF)


def draw_norm_params(key, part):
    key_gain = jax.random.fold_in(key, 31)
    key_bias = jax.random.fold_in(key, 32)
    slope = 0.5 + jnp.arange(D, dtype=jnp.float32) / D
    gains = slope[:, None] * jax.random.uniform(key_gain, (D, 2), jnp.float32, 0.7, 1.3)
    biases = 0.6 * base_draw(key_bias, (D, 2))
    return jnp.stack([gains[:, 0], biases[:, 0], gains[:, 1], biases[:, 1]], axis=1)


def token_root():
    return (EPISODES * LMAX * 0.41) ** 0.5


def first_of(key, shape, scale_factor):
    return scale_factor * jax.random.normal(key, shape, jnp.float32) / 9.0


def first_matrix(key, shape, scale_factor):
    return first_of(key, shape, scale_factor) * row_fall(shape[0])[:, None]


def second_of(key, shape, scale_factor):
    return scale_factor * scale_factor * 0.001001 * jax.random.uniform(key, shape, jnp.float32, 1.0, 4.0)


def triple_scale():
    columns = jnp.arange(3 * D)
    return jnp.where(columns < 2 * D, 0.1, 0.4)[None, :] * LMAX ** 0.5 * token_root()


def norms_scale():
    return jnp.array([0.5 * LMAX ** 0.5, 0.5 * LMAX ** 0.5, 2.3, 2.3], jnp.float32)[None, :] * token_root()


def draw_first_triple(key, part):
    return first_matrix(key, (D, 3 * D), triple_scale())


def draw_first_mixer(key, part):
    return first_matrix(key, (D, D), 0.3 * token_root())


def draw_first_expand(key, part):
    return first_matrix(key, (D, FF), 0.9 * token_root())


def draw_first_reduce(key, part):
    return first_matrix(key, (FF, D), 0.9 * token_root())


def draw_first_norms(key, part):
    return first_of(key, (D, 4), norms_scale())


def draw_second_triple(key, part):
    return second_of(key, (D, 3 * D), triple_scale())


def draw_second_mixer(key, part):
    return second_of(key, (D, D), 0.3 * token_root())


def draw_second_expand(key, part):
    return second_of(key, (D, FF), 0.9 * token_root())


def draw_second_reduce(key, part):
    return second_of(key, (FF, D), 0.9 * token_root())


def draw_second_norms(key, part):
    return second_of(key, (D, 4), norms_scale())


def touch_ends(values, stream_key, smallest, largest):
    spot = [jax.random.randint(jax.random.fold_in(stream_key, axis), (), 0, length) for axis, length in enumerate(values.shape)]
    main_axis = values.shape.index(max(values.shape))
    neighbour = spot[:main_axis] + [(spot[main_axis] + 1) % values.shape[main_axis]] + spot[main_axis + 1:]
    return values.at[tuple(spot)].set(smallest).at[tuple(neighbour)].set(largest)


def levels(stream_key, extent, shards, least, top_value):
    def one(axis_at, shards_of):
        steps = jax.random.uniform(jax.random.fold_in(jax.random.fold_in(stream_key, 6), axis_at), (shards_of,), jnp.float32, least / len(shards), top_value / len(shards))
        return jnp.repeat(jnp.exp(steps), extent[axis_at] // shards_of).reshape((-1,) + (1,) * (len(extent) - axis_at - 1))

    factor_of = one(*shards[0])
    for cut in shards[1:]:
        factor_of = factor_of * one(*cut)
    return factor_of


def normal_values(stream_key, extent, scale, bound, shards=(), kind=jnp.bfloat16):
    values = jax.random.normal(stream_key, extent, jnp.float32) * scale
    if len(shards) > 0:
        values = levels(stream_key, extent, shards, -0.22, 0.18) * values
    return jnp.clip(values, min=-bound, max=bound).astype(kind)


def setup_inputs(seed: int = 0) -> dict:
    key_of = jax.random.split(jax.random.key(seed), 22)
    return {
        "tokens": draw_tokens(jax.random.fold_in(key_of[21], 71), 0),
        "cotangent": normal_values(key_of[1], (EPISODES, LMAX, D), 1.0, 6.0, ((0, 32),)),
        "lengths": draw_lengths(jax.random.fold_in(key_of[21], 71), 0),
        "valid_mask": touch_ends((jax.random.randint(key_of[3], (EPISODES, LMAX), 0, 4) < 3).astype(jnp.int32), jax.random.fold_in(key_of[3], 1), 0, 1),
        "action_bins": touch_ends(jax.random.randint(key_of[4], (EPISODES, LMAX, ACT), 0, NBINS), jax.random.fold_in(key_of[4], 1), 0, NBINS - 1).astype(jnp.int32),
        "value_head": normal_values(key_of[5], (ACT * NBINS, D), D ** -0.5, 0.25),
        "w_triple": draw_w_triple(jax.random.fold_in(key_of[21], 71), 0),
        "w_mixer": draw_w_mixer(jax.random.fold_in(key_of[21], 71), 0),
        "w_expand": draw_w_expand(jax.random.fold_in(key_of[21], 71), 0),
        "w_reduce": draw_w_reduce(jax.random.fold_in(key_of[21], 71), 0),
        "norm_params": draw_norm_params(jax.random.fold_in(key_of[21], 71), 0),
        "first_triple": draw_first_triple(jax.random.fold_in(key_of[21], 71), 0),
        "first_mixer": draw_first_mixer(jax.random.fold_in(key_of[21], 71), 0),
        "first_expand": draw_first_expand(jax.random.fold_in(key_of[21], 71), 0),
        "first_reduce": draw_first_reduce(jax.random.fold_in(key_of[21], 71), 0),
        "first_norms": draw_first_norms(jax.random.fold_in(key_of[21], 71), 0),
        "second_triple": draw_second_triple(jax.random.fold_in(key_of[21], 71), 0),
        "second_mixer": draw_second_mixer(jax.random.fold_in(key_of[21], 71), 0),
        "second_expand": draw_second_expand(jax.random.fold_in(key_of[21], 71), 0),
        "second_reduce": draw_second_reduce(jax.random.fold_in(key_of[21], 71), 0),
        "second_norms": draw_second_norms(jax.random.fold_in(key_of[21], 71), 0),
    }


@jax.custom_vjp
def low(v):
    return lax.optimization_barrier(v.astype(jnp.bfloat16)).astype(jnp.float32)

@jax.custom_vjp
def low_back(v):
    return v

def low_keep(v):
    return (low(v), None)

def low_pass(kept, grad):
    return (grad,)

def back_keep(v):
    return (v, None)

def back_low(kept, grad):
    return (low(grad),)
low.defvjp(low_keep, low_pass)
low_back.defvjp(back_keep, back_low)
NORM_EPSILON = 1e-05
BETA_FIRST = 0.9
BETA_SECOND = 0.999
ADAM_EPSILON = 1e-06
RATIO_EPSILON = 1e-06
WEIGHT_DECAY = 0.01
LEARNING_RATE = 0.5
MASKED = -1e+30
PRECISE = lax.Precision.HIGHEST

def layer_norm(row_block, gain_vector, bias_vector):
    center = row_block - lax.optimization_barrier(jnp.mean(row_block, axis=-1, keepdims=True))
    spread = lax.optimization_barrier(jnp.mean(center * center, axis=-1, keepdims=True))
    return center * lax.rsqrt(spread + NORM_EPSILON) * gain_vector + bias_vector

def product(left_side, right_side):
    return jnp.dot(left_side, right_side, precision=PRECISE)

def group_forward(inputs, w_triple, w_mixer, w_expand, w_reduce, norm_params, length_block):
    episodes, length_rows, features = inputs.shape
    flattened = inputs.reshape(episodes * length_rows, features)
    normed_one = low(layer_norm(flattened, norm_params[:, 0], norm_params[:, 1]))
    triple = low(low_back(product(normed_one, low(w_triple))))
    triple = triple.reshape(episodes, length_rows, 3, HEADS, HEAD_DIM)
    places = jnp.arange(length_rows)

    def attend_episode(episode_item):
        episode_block, length_limit = episode_item
        queries = episode_block[:, 0].transpose(1, 0, 2)
        key_rows = episode_block[:, 1].transpose(1, 0, 2)
        value_rows = episode_block[:, 2].transpose(1, 0, 2)
        scores = low_back(jnp.einsum('hqd,hkd->hqk', queries, key_rows, precision=PRECISE) * HEAD_DIM ** (-0.5))
        allowed = (places[None, :] <= places[:, None]) & (places[None, :] < length_limit)
        scores = jnp.where(allowed[None], scores, MASKED)
        shifted = jnp.exp(scores - lax.optimization_barrier(jnp.max(scores, axis=-1, keepdims=True)))
        softmax_rows = shifted / lax.optimization_barrier(jnp.sum(shifted, axis=-1, keepdims=True))
        mixture = jnp.einsum('hqk,hkd->qhd', low(softmax_rows), value_rows, precision=PRECISE)
        return mixture.reshape(length_rows, HEADS * HEAD_DIM)
    attended = lax.map(jax.checkpoint(attend_episode), (triple, length_block))
    attended = low(low_back(attended.reshape(episodes * length_rows, features)))
    hidden = flattened + low_back(product(attended, low(w_mixer)))
    normed_two = low(layer_norm(hidden, norm_params[:, 2], norm_params[:, 3]))
    expanded = low_back(product(normed_two, low(w_expand)))
    activated = low(jax.nn.gelu(expanded, approximate=False))
    result = hidden + low_back(product(activated, low(w_reduce)))
    return result.reshape(episodes, length_rows, features)

def lamb_moments(weight, gradient, moment_one, moment_two):
    first_new = BETA_FIRST * moment_one + (1.0 - BETA_FIRST) * gradient
    second_new = BETA_SECOND * moment_two + (1.0 - BETA_SECOND) * gradient * gradient
    update = first_new / (1.0 - BETA_FIRST ** STEP) / (jnp.sqrt(second_new / (1.0 - BETA_SECOND ** STEP)) + ADAM_EPSILON) + WEIGHT_DECAY * weight
    return (first_new, second_new, update)

def reference(tokens, cotangent, lengths, valid_mask, action_bins, value_head, w_triple, w_mixer, w_expand, w_reduce, norm_params, first_triple, first_mixer, first_expand, first_reduce, first_norms, second_triple, second_mixer, second_expand, second_reduce, second_norms):
    groups = N_DP * N_FSDP
    weights = (w_triple, w_mixer, w_expand, w_reduce, norm_params)
    token_groups = tokens.astype(jnp.float32).reshape(groups, EP_DEV, LMAX, D)
    back_groups = cotangent.astype(jnp.float32).reshape(groups, EP_DEV, LMAX, D)
    length_groups = lengths.reshape(groups, EP_DEV)
    mark_groups = valid_mask.reshape(groups, EP_DEV, LMAX)
    bin_groups = action_bins.reshape(groups, EP_DEV, LMAX, ACT)
    places = jnp.arange(LMAX)
    offsets = (jnp.arange(ACT) * NBINS).astype(jnp.int32)

    def one_group(state_carry, group_item):
        gradient_sums, value_sums, value_counts, value_tops = state_carry
        inputs, back_rows, limit_block, mark_block, bin_block = group_item
        inside = places[None, :] < limit_block[:, None]
        live_rows = inside.astype(inputs.dtype)

        def forward(inputs_in, first_in, second_in, third_in, fourth_in, fifth_in):
            return group_forward(inputs_in, first_in, second_in, third_in, fourth_in, fifth_in, limit_block)
        outputs, pullback = jax.vjp(forward, inputs, *weights)
        gradients = pullback(back_rows * live_rows[:, :, None])
        gradient_sums = tuple((running + gradient for running, gradient in zip(gradient_sums, gradients[1:])))
        block_rows = outputs.astype(jnp.bfloat16)
        rows_flat = block_rows.reshape(-1, D).astype(jnp.float32)
        bin_rows = (bin_block.reshape(-1, ACT) + offsets[None, :]).astype(jnp.int32)
        picked = jnp.take(value_head, bin_rows, axis=0).astype(jnp.float32)
        value_scores = jnp.einsum('tad,td->ta', picked, rows_flat, precision=PRECISE)
        counted = ((mark_block == 1) & inside).reshape(-1, 1).astype(jnp.float32)
        value_sums = value_sums + lax.optimization_barrier(jnp.sum(value_scores * counted, axis=0))
        value_counts = value_counts + jnp.sum(counted)
        value_tops = jnp.maximum(value_tops, lax.optimization_barrier(jnp.max(jnp.where(counted > 0, value_scores, MASKED), axis=0)))
        return ((gradient_sums, value_sums, value_counts, value_tops), (block_rows, gradients[0].astype(jnp.bfloat16)))
    start = (tuple((jnp.zeros_like(weight) for weight in weights)), jnp.zeros((ACT,), jnp.float32), jnp.zeros((), jnp.float32), jnp.full((ACT,), MASKED, jnp.float32))
    finals, stacked = lax.scan(one_group, start, (token_groups, back_groups, length_groups, mark_groups, bin_groups))
    gradient_sums, value_sums, value_counts, value_tops = finals
    block_out = stacked[0].reshape(EPISODES, LMAX, D)
    input_grad = stacked[1].reshape(EPISODES, LMAX, D)
    value_mean = value_sums / jnp.maximum(value_counts, 1.0)
    firsts = (first_triple, first_mixer, first_expand, first_reduce)
    seconds = (second_triple, second_mixer, second_expand, second_reduce)
    new_list, first_list, second_list, weight_norms, update_norms = ([], [], [], [], [])
    for index_matrix in range(4):
        weight = weights[index_matrix]
        first_new, second_new, update = lamb_moments(weight, gradient_sums[index_matrix], firsts[index_matrix], seconds[index_matrix])
        weight_norm = jnp.sqrt(jnp.sum(weight * weight))
        update_norm = jnp.sqrt(jnp.sum(update * update))
        new_list.append(weight - LEARNING_RATE * (weight_norm / (update_norm + RATIO_EPSILON)) * update)
        first_list.append(first_new)
        second_list.append(second_new)
        weight_norms.append(weight_norm)
        update_norms.append(update_norm)
    small_first, small_second, small_update = lamb_moments(norm_params, gradient_sums[4], first_norms, second_norms)
    small_weight = jnp.sqrt(lax.optimization_barrier(jnp.sum(norm_params * norm_params, axis=0)))
    small_norm = jnp.sqrt(lax.optimization_barrier(jnp.sum(small_update * small_update, axis=0)))
    new_norms = norm_params - LEARNING_RATE * (small_weight / (small_norm + RATIO_EPSILON))[None, :] * small_update
    norm_table = jnp.stack([jnp.concatenate([jnp.stack(weight_norms), small_weight]), jnp.concatenate([jnp.stack(update_norms), small_norm])])
    return (block_out, input_grad, new_list[0], new_list[1], new_list[2], new_list[3], first_list[0], first_list[1], first_list[2], first_list[3], second_list[0], second_list[1], second_list[2], second_list[3], new_norms, small_first, small_second, norm_table, value_mean, value_tops)
```

```python
import functools

import jax
import jax.numpy as jnp
from jax import lax
from jax.experimental import pallas as pl
from jax.experimental.pallas import tpu as pltpu
from jax.sharding import PartitionSpec as P

HEADS = 8
HEAD_DIM = 64
ACT = 11
NBINS = 256
STEP = 5

NORM_EPSILON = 1e-05
BETA_FIRST = 0.9
BETA_SECOND = 0.999
ADAM_EPSILON = 1e-06
RATIO_EPSILON = 1e-06
WEIGHT_DECAY = 0.01
LEARNING_RATE = 0.5
MASKED = -1e30

D = 512
FF = 2048
QB = 64
QUAD = 256
F32 = jnp.float32
BF16 = jnp.bfloat16
VMEM_LIMIT = 60 * 1024 * 1024

NT = (((1,), (1,)), ((), ()))
NN = (((1,), (0,)), ((), ()))
TN = (((0,), (0,)), ((), ()))


def mm(a, b, dims=NN):
    return lax.dot_general(a, b, dims, preferred_element_type=F32)


def pad_rows(v, rows):
    return jnp.concatenate([v, jnp.zeros((rows - v.shape[0], v.shape[1]), v.dtype)], axis=0)


def ln_parts(x):
    center = x - jnp.mean(x, axis=-1, keepdims=True)
    spread = jnp.mean(center * center, axis=-1, keepdims=True)
    rstd = lax.rsqrt(spread + NORM_EPSILON)
    return center * rstd, rstd


def ln_back(grad, xhat, rstd, gain):
    t = grad * gain
    m1 = jnp.mean(t, axis=-1, keepdims=True)
    m2 = jnp.mean(t * xhat, axis=-1, keepdims=True)
    return rstd * (t - m1 - xhat * m2)


def head_masks():
    lane = lax.broadcasted_iota(jnp.int32, (1, QUAD), 1)
    return [jnp.where(lane // HEAD_DIM == h, 1.0, 0.0).astype(BF16) for h in range(4)]


def stack_heads(block, masks):
    return jnp.concatenate([block * m for m in masks], axis=0)


def pair_rows(t):
    tt = t.T
    lane = lax.broadcasted_iota(jnp.int32, (QB, 2 * HEAD_DIM), 1)
    return jnp.where(lane < HEAD_DIM, tt[:QB], tt[QB:])


def sides(refs, core):
    return [(refs[0], 0)] if len(refs) == 1 else [(refs[0], core), (refs[1], 1 - core)]


def load_triple(refs, dst, sem, me, core, rels, start):
    half = refs[0].shape[1]
    for p, rel in enumerate(rels):
        block = jnp.bitwise_xor(me, rel)
        for src, c in sides(refs, core):
            row = pl.multiple_of(block * (len(refs) * half) + c * half, half)
            copy = pltpu.make_async_copy(src.at[p], dst.at[pl.ds(row, half)], sem)
            copy.start() if start else copy.wait()


def load_rest(refs, wm, we, wr, sem, me, core, rels, start):
    hm = D // len(rels) // len(refs)
    hr = FF // len(rels) // len(refs)
    nc = FF // D
    for p, rel in enumerate(rels):
        block = jnp.bitwise_xor(me, rel)
        for src, c in sides(refs, core):
            row = pl.multiple_of(block * (len(refs) * hm) + c * hm, hm)
            rowr = pl.multiple_of(block * (len(refs) * hr) + c * hr, hr)
            copies = [pltpu.make_async_copy(src.at[p, pl.ds(0, hm)], wm.at[pl.ds(row, hm)], sem)]
            for q in range(nc):
                copies.append(
                    pltpu.make_async_copy(
                        src.at[p, pl.ds(hm * (1 + q), hm)],
                        we.at[pl.ds(row, hm), pl.ds(q * D, D)],
                        sem,
                    )
                )
            copies.append(
                pltpu.make_async_copy(src.at[p, pl.ds(hm * (1 + nc), hr)], wr.at[pl.ds(rowr, hr)], sem)
            )
            for copy in copies:
                copy.start() if start else copy.wait()


def f1_kernel(rels, nh, idx, lens, tok, norm, *refs):
    w_refs, (tri_out, att_out, lse_out, wt, tri, sem) = refs[:nh], refs[nh:]
    e = pl.program_id(0)
    rows = tok.shape[1]
    padded = tri.shape[0]
    rows16 = -(-rows // 16) * 16

    @pl.when(e == 0)
    def _():
        load_triple(w_refs, wt, sem, idx[0], idx[1], rels, True)
        tri[rows16:padded] = jnp.zeros((padded - rows16, 3 * D), BF16)
        load_triple(w_refs, wt, sem, idx[0], idx[1], rels, False)

    x = pad_rows(tok[0].astype(F32), rows16)
    xhat, _ = ln_parts(x)
    n1 = (xhat * norm[0:1] + norm[1:2]).astype(BF16)
    t = mm(n1, wt[...]).astype(BF16)
    tri[0:rows16, 0:D] = t[:, 0:D] * jnp.asarray(HEAD_DIM**-0.5, BF16)
    tri[0:rows16, D:] = t[:, D:]
    tri_out[0] = tri[0:rows]

    length = lens[e]
    masks = head_masks()
    lane = lax.broadcasted_iota(jnp.int32, (1, QUAD), 1) % QB
    blocks = -(-rows // QB)
    for g in range(HEADS // 4):
        gl = g * QUAD
        for j in range(blocks):
            ext = min(QB * (j + 1), rows16)
            q4 = stack_heads(tri[QB * j : QB * (j + 1), gl : gl + QUAD], masks)
            s = mm(tri[0:ext, D + gl : D + gl + QUAD], q4, NT)
            kmax = jnp.minimum(lane + QB * j, length - 1)
            krow = lax.broadcasted_iota(jnp.int32, (ext, QUAD), 0)
            s = jnp.where(krow <= kmax, s, MASKED)
            m = jnp.max(s, axis=0, keepdims=True)
            p = jnp.exp(s - m)
            total = jnp.sum(p, axis=0, keepdims=True)
            lse_out[0, pl.ds(g * blocks + j, 1), :] = m + jnp.log(total)
            pb = (p * (1.0 / total)).astype(BF16)
            live = min(QB, rows - QB * j)
            for t2 in range(2):
                cl = 2 * D + gl + 128 * t2
                o = mm(tri[0:ext, cl : cl + 128], pb[:, 128 * t2 : 128 * t2 + 128], TN)
                o = pair_rows(o).astype(BF16)
                att_out[0, QB * j : QB * j + live, gl + 128 * t2 : gl + 128 * t2 + 128] = o[:live]


def f2_kernel(rels, pos, nh, idx, att_ref, tok, gl_ref, norm, *refs):
    w_refs, refs = refs[:nh], refs[nh:]
    (block_out, gh_out, ga_out), grads, refs = refs[:3], refs[3 : 3 + nh], refs[3 + nh :]
    ln_out, wm, we, wr, acc_m, acc_e, acc_r, sem = refs
    e = pl.program_id(0)
    rows = tok.shape[1]
    rows16 = -(-rows // 16) * 16

    @pl.when(e == 0)
    def _():
        load_rest(w_refs, wm, we, wr, sem, idx[0], idx[1], rels, True)
        acc_m[...] = jnp.zeros_like(acc_m)
        acc_e[...] = jnp.zeros_like(acc_e)
        acc_r[...] = jnp.zeros_like(acc_r)
        ln_out[...] = jnp.zeros_like(ln_out)
        load_rest(w_refs, wm, we, wr, sem, idx[0], idx[1], rels, False)

    gain = norm[2:3]
    att = pad_rows(att_ref[0], rows16)
    glow = pad_rows(gl_ref[0], rows16)
    hidden = pad_rows(tok[0].astype(F32), rows16) + mm(att, wm[...])
    xhat, rstd = ln_parts(hidden)
    n2 = (xhat * gain + norm[3:4]).astype(BF16)
    out = hidden
    g2 = jnp.zeros_like(hidden)
    for c in range(FF // D):
        cs = slice(c * D, c * D + D)
        ex = mm(n2, we[:, cs])
        phi = 0.5 + 0.5 * lax.erf(ex * 0.7071067811865476)
        act = (ex * phi).astype(BF16)
        gp = phi + ex * (jnp.exp(-0.5 * ex * ex) * 0.3989422804014327)
        out = out + mm(act, wr[cs])
        gact = mm(glow, wr[cs], NT)
        ge = (gp * gact).astype(BF16)
        g2 = g2 + mm(ge, we[:, cs], NT)
        acc_r[:, cs] += mm(glow, act, TN)
        acc_e[:, cs] += mm(n2, ge, TN)
    block_out[0] = out[:rows].astype(BF16)
    gh = glow.astype(F32) + ln_back(g2, xhat, rstd, gain)
    ln_out[0:1] += jnp.sum(g2 * xhat, axis=0, keepdims=True)
    ln_out[1:2] += jnp.sum(g2, axis=0, keepdims=True)
    gb = gh.astype(BF16)
    gh_out[0] = gh[:rows]
    acc_m[...] += mm(att, gb, TN)
    ga_out[0] = mm(gb, wm[...], NT)[:rows].astype(BF16)

    @pl.when(e == pl.num_programs(0) - 1)
    def _():
        me, core = idx[0], idx[1]
        hm = D // len(rels) // nh
        hr = FF // len(rels) // nh
        nc = FF // D
        for c in range(nc):
            wr[c * D : c * D + D] = acc_r[:, c * D : c * D + D].T.astype(BF16)
        for p, rel in enumerate(pos):
            block = jnp.bitwise_xor(me, rel)
            for dst, c in sides(grads, core):
                row = pl.multiple_of(block * (nh * hm) + c * hm, hm)
                rowr = pl.multiple_of(block * (nh * hr) + c * hr, hr)
                dst[p, 0:hm] = acc_m[pl.ds(row, hm)].astype(BF16)
                for q in range(nc):
                    dst[p, hm * (1 + q) : hm * (2 + q)] = acc_e[
                        pl.ds(row, hm), q * D : q * D + D
                    ].astype(BF16)
                dst[p, hm * (1 + nc) :] = wr[pl.ds(rowr, hr)]


def b1_kernel(pos, nh, idx, lens, tri_ref, ga_ref, lse, tok, norm, gtri_out, *refs):
    grads, (tri, ga, gtri, dk, dv, acc) = refs[:nh], refs[nh:]
    e = pl.program_id(0)
    rows = tok.shape[1]
    padded = tri.shape[0]
    rows16 = -(-rows // 16) * 16
    rows8 = rows // 16 * 16

    @pl.when(e == 0)
    def _():
        acc[...] = jnp.zeros_like(acc)
        tri[rows8:padded] = jnp.zeros((padded - rows8, 3 * D), BF16)
        ga[rows8:padded] = jnp.zeros((padded - rows8, D), BF16)

    tri[0:rows] = tri_ref[0]
    ga[0:rows] = ga_ref[0]
    dk[...] = jnp.zeros_like(dk)
    dv[...] = jnp.zeros_like(dv)
    gtri[:, 0:D] = jnp.zeros((padded, D), BF16)

    length = lens[e]
    masks = head_masks()
    lane = lax.broadcasted_iota(jnp.int32, (1, QUAD), 1) % QB
    blocks = -(-rows // QB)
    for j in range(blocks):

        @pl.when(length > QB * j)
        def _(j=j):
            ext = min(QB * (j + 1), rows16)
            kmax = jnp.minimum(lane + QB * j, length - 1)
            krow = lax.broadcasted_iota(jnp.int32, (ext, QUAD), 0)
            allowed = krow <= kmax
            for g in range(HEADS // 4):
                gl = g * QUAD
                q4 = stack_heads(tri[QB * j : QB * (j + 1), gl : gl + QUAD], masks)
                do4 = stack_heads(ga[QB * j : QB * (j + 1), gl : gl + QUAD], masks)
                s = mm(tri[0:ext, D + gl : D + gl + QUAD], q4, NT)
                s = jnp.where(allowed, s - lse[0, pl.ds(g * blocks + j, 1), :], MASKED)
                p = jnp.exp(s)
                dp = mm(tri[0:ext, 2 * D + gl : 2 * D + gl + QUAD], do4, NT)
                delta = jnp.sum(p * dp, axis=0, keepdims=True)
                ds = (p * (dp - delta)).astype(BF16)
                dv[0:ext, gl : gl + QUAD] += mm(p.astype(BF16), do4)
                dk[0:ext, gl : gl + QUAD] += mm(ds, q4)
                for t2 in range(2):
                    cl = D + gl + 128 * t2
                    dq = mm(tri[0:ext, cl : cl + 128], ds[:, 128 * t2 : 128 * t2 + 128], TN)
                    dq = pair_rows(dq) * HEAD_DIM**-0.5
                    gtri[QB * j : QB * (j + 1), gl + 128 * t2 : gl + 128 * t2 + 128] = dq.astype(BF16)

    gtri[0:rows16, D : 2 * D] = dk[...].astype(BF16)
    gtri[0:rows16, 2 * D :] = dv[...].astype(BF16)
    gtri_out[0] = gtri[0:rows]
    xhat, _ = ln_parts(pad_rows(tok[0].astype(F32), rows16))
    n1 = (xhat * norm[0:1] + norm[1:2]).astype(BF16)
    acc[...] += mm(n1, gtri[0:rows16], TN)

    @pl.when(e == pl.num_programs(0) - 1)
    def _():
        me, core = idx[0], idx[1]
        hm = D // len(pos) // nh
        for p, rel in enumerate(pos):
            block = jnp.bitwise_xor(me, rel)
            for dst, c in sides(grads, core):
                row = pl.multiple_of(block * (nh * hm) + c * hm, hm)
                for q in range(3):
                    dst[p, hm * q : hm * (q + 1)] = acc[pl.ds(row, hm), q * D : q * D + D].astype(BF16)


def b2_kernel(rels, nh, idx, gtri, tok, gh, norm, *refs):
    w_refs, (ig_out, ln_out, wt, sem) = refs[:nh], refs[nh:]
    e = pl.program_id(0)

    @pl.when(e == 0)
    def _():
        load_triple(w_refs, wt, sem, idx[0], idx[1], rels, True)
        ln_out[...] = jnp.zeros_like(ln_out)
        load_triple(w_refs, wt, sem, idx[0], idx[1], rels, False)

    g1 = mm(gtri[0], wt[...], NT)
    xhat, rstd = ln_parts(tok[0].astype(F32))
    ig_out[0] = (gh[0] + ln_back(g1, xhat, rstd, norm[0:1])).astype(BF16)
    ln_out[0:1] += jnp.sum(g1 * xhat, axis=0, keepdims=True)
    ln_out[1:2] += jnp.sum(g1, axis=0, keepdims=True)


def q_kernel(total_rows, bo, vh, bins, cnt, sum_out, top_out):
    s = pl.program_id(0)
    block = bo.shape[0]

    @pl.when(s == 0)
    def _():
        sum_out[...] = jnp.zeros_like(sum_out)
        top_out[...] = jnp.full_like(top_out, MASKED)

    place = lax.broadcasted_iota(jnp.int32, (1, block), 1) + s * block
    counted = (cnt[...] > 0) & (place < total_rows)
    binrow = lax.broadcasted_iota(jnp.int32, (NBINS, block), 0)
    for a in range(ACT):
        sc = mm(vh[a * NBINS : (a + 1) * NBINS], bo[...], NT)
        picked = jnp.sum(jnp.where(binrow == bins[a : a + 1], sc, 0.0), axis=0, keepdims=True)
        sum_out[a : a + 1] += jnp.where(counted, picked, 0.0)
        top_out[a : a + 1] = jnp.maximum(top_out[a : a + 1], jnp.where(counted, picked, MASKED))


def xor_step(v, axis, size, bit):
    return lax.ppermute(v, axis, [(i, i ^ bit) for i in range(size)])


def axis_bits(size):
    bits = []
    b = 1
    while b < size:
        bits.append(b)
        b *= 2
    return bits


def gather_half(piece, n_f, n_d, order, nh):
    buf, rels = piece[None], [0]
    for b in order:
        buf = jnp.concatenate([buf, xor_step(buf, "fsdp", n_f, b)], axis=0)
        rels = rels + [r ^ b for r in rels]
    if nh == 1:
        return [buf], rels
    return [buf, xor_step(buf, "dp", n_d, 1)], rels


def halving_positions(order):
    rels = [0]
    for b in reversed(order):
        rels = rels + [r ^ b for r in rels]
    return rels


def add_low(a, b):
    return (a.astype(F32) + b.astype(F32)).astype(BF16)


def reduce_halves(parts, n_f, n_d, order):
    total = parts[0]
    if len(parts) == 2:
        total = add_low(total, xor_step(parts[1], "dp", n_d, 1))
    for b in order:
        n = total.shape[0] // 2
        total = add_low(total[:n], xor_step(total[n:], "fsdp", n_f, b))
    total = total[0].astype(F32)
    for b in axis_bits(n_d)[len(parts) - 1 :]:
        total = total + xor_step(total.astype(BF16), "dp", n_d, b).astype(F32)
    return total


def lamb_moments(weight, gradient, moment_one, moment_two):
    first_new = BETA_FIRST * moment_one + (1.0 - BETA_FIRST) * gradient
    second_new = BETA_SECOND * moment_two + (1.0 - BETA_SECOND) * gradient * gradient
    update = (
        first_new
        / (1.0 - BETA_FIRST**STEP)
        / (jnp.sqrt(second_new / (1.0 - BETA_SECOND**STEP)) + ADAM_EPSILON)
        + WEIGHT_DECAY * weight
    )
    return (first_new, second_new, update)


def const_spec(shape):
    return pl.BlockSpec(shape, lambda *a: (0,) * len(shape))


SMEM = pl.BlockSpec(memory_space=pltpu.SMEM)
ANY = pl.BlockSpec(memory_space=pl.ANY)


def params():
    return pltpu.CompilerParams(dimension_semantics=("arbitrary",), vmem_limit_bytes=VMEM_LIMIT)


def body(n_d, n_f, *args):
    (
        tokens, cotangent, lengths, valid_mask, action_bins, value_head,
        w_triple, w_mixer, w_expand, w_reduce, norm_params,
        first_triple, first_mixer, first_expand, first_reduce, first_norms,
        second_triple, second_mixer, second_expand, second_reduce, second_norms,
    ) = args
    ep, rows, _ = tokens.shape
    flat = ep * rows
    rows16 = -(-rows // 16) * 16
    padded = -(-rows // QB) * QB
    blocks = padded // QB
    me = lax.axis_index("fsdp")
    core = lax.axis_index("dp") % 2
    idx = jnp.stack([me, core]).astype(jnp.int32)
    nh = 2 if D // n_f >= 32 else 1
    hm = D // n_f // nh
    hr = FF // n_f // nh
    nc = FF // D

    order_g = list(reversed(axis_bits(n_f)))

    def own_half(w):
        n = w.shape[0] // nh
        return lax.dynamic_slice_in_dim(w, core * n, n, 0) if nh == 2 else w

    own_t = own_half(w_triple).astype(BF16)
    own_m = own_half(w_mixer).astype(BF16)
    own_e = own_half(w_expand).astype(BF16)
    own_r = own_half(w_reduce).astype(BF16)
    own_rest = jnp.concatenate(
        [own_m] + [own_e[:, q * D : (q + 1) * D] for q in range(nc)] + [own_r], axis=0
    )
    t_parts, rels = gather_half(own_t, n_f, n_d, order_g, nh)
    r_parts, _ = gather_half(own_rest, n_f, n_d, order_g, nh)

    norm = jnp.concatenate([norm_params.T, jnp.zeros((4, D), F32)], axis=0)
    places = jnp.arange(rows)
    inside = places[None, :] < lengths[:, None]
    glow = jnp.where(inside[:, :, None], cotangent, jnp.zeros((), BF16))

    ep_block = lambda width: pl.BlockSpec((1, rows, width), lambda e: (e, 0, 0))

    triple, attended, lse = pl.pallas_call(
        functools.partial(f1_kernel, rels, nh),
        grid=(ep,),
        in_specs=[SMEM, SMEM, ep_block(D), const_spec((8, D))] + [ANY] * nh,
        out_specs=[
            ep_block(3 * D), ep_block(D), pl.BlockSpec((1, 16, QUAD), lambda e: (e, 0, 0)),
        ],
        out_shape=[
            jax.ShapeDtypeStruct((ep, rows, 3 * D), BF16),
            jax.ShapeDtypeStruct((ep, rows, D), BF16),
            jax.ShapeDtypeStruct((ep, 16, QUAD), F32),
        ],
        scratch_shapes=[
            pltpu.VMEM((D, 3 * D), BF16), pltpu.VMEM((padded, 3 * D), BF16), pltpu.SemaphoreType.DMA,
        ],
        compiler_params=params(),
        cost_estimate=pl.CostEstimate(flops=20_000_000_000, bytes_accessed=14_000_000, transcendentals=0),
        name="f1",
    )(idx, lengths, tokens, norm, *t_parts)

    order_s = axis_bits(n_f)
    pos = halving_positions(order_s)
    width = hm * (1 + nc) + hr
    block_out, gh, ga, *grads_r, ln2 = pl.pallas_call(
        functools.partial(f2_kernel, rels, pos, nh),
        grid=(ep,),
        in_specs=[SMEM, ep_block(D), ep_block(D), ep_block(D), const_spec((8, D))] + [ANY] * nh,
        out_specs=[
            ep_block(D), ep_block(D), ep_block(D),
            *[const_spec((n_f, width, D))] * nh, const_spec((8, D)),
        ],
        out_shape=[
            jax.ShapeDtypeStruct((ep, rows, D), BF16),
            jax.ShapeDtypeStruct((ep, rows, D), F32),
            jax.ShapeDtypeStruct((ep, rows, D), BF16),
            *[jax.ShapeDtypeStruct((n_f, width, D), BF16)] * nh,
            jax.ShapeDtypeStruct((8, D), F32),
        ],
        scratch_shapes=[
            pltpu.VMEM((D, D), BF16), pltpu.VMEM((D, FF), BF16), pltpu.VMEM((FF, D), BF16),
            pltpu.VMEM((D, D), F32), pltpu.VMEM((D, FF), F32), pltpu.VMEM((D, FF), F32),
            pltpu.SemaphoreType.DMA,
        ],
        compiler_params=params(),
        cost_estimate=pl.CostEstimate(flops=40_000_000_000, bytes_accessed=20_000_000, transcendentals=0),
        name="f2",
    )(idx, attended, tokens, glow, norm, *r_parts)

    gtri, *grads_t = pl.pallas_call(
        functools.partial(b1_kernel, pos, nh),
        grid=(ep,),
        in_specs=[
            SMEM, SMEM, ep_block(3 * D), ep_block(D),
            pl.BlockSpec((1, 16, QUAD), lambda e: (e, 0, 0)), ep_block(D), const_spec((8, D)),
        ],
        out_specs=[ep_block(3 * D)] + [const_spec((n_f, 3 * hm, D))] * nh,
        out_shape=[
            jax.ShapeDtypeStruct((ep, rows, 3 * D), BF16),
            *[jax.ShapeDtypeStruct((n_f, 3 * hm, D), BF16)] * nh,
        ],
        scratch_shapes=[
            pltpu.VMEM((padded, 3 * D), BF16), pltpu.VMEM((padded, D), BF16),
            pltpu.VMEM((padded, 3 * D), BF16), pltpu.VMEM((rows16, D), F32),
            pltpu.VMEM((rows16, D), F32), pltpu.VMEM((D, 3 * D), F32),
        ],
        compiler_params=params(),
        cost_estimate=pl.CostEstimate(flops=25_000_000_000, bytes_accessed=20_000_000, transcendentals=0),
        name="b1",
    )(idx, lengths, triple, ga, lse, tokens, norm)

    input_grad, ln1 = pl.pallas_call(
        functools.partial(b2_kernel, rels, nh),
        grid=(ep,),
        in_specs=[SMEM, ep_block(3 * D), ep_block(D), ep_block(D), const_spec((8, D))] + [ANY] * nh,
        out_specs=[ep_block(D), const_spec((8, D))],
        out_shape=[
            jax.ShapeDtypeStruct((ep, rows, D), BF16),
            jax.ShapeDtypeStruct((8, D), F32),
        ],
        scratch_shapes=[pltpu.VMEM((D, 3 * D), BF16), pltpu.SemaphoreType.DMA],
        compiler_params=params(),
        cost_estimate=pl.CostEstimate(flops=5_000_000_000, bytes_accessed=16_000_000, transcendentals=0),
        name="b2",
    )(idx, gtri, tokens, gh, norm, *t_parts)

    counted = ((valid_mask == 1) & inside).reshape(1, flat)
    bins_t = action_bins.reshape(flat, ACT).T
    qb = 256
    steps = -(-flat // qb)
    q_sum, q_top = pl.pallas_call(
        functools.partial(q_kernel, flat),
        grid=(steps,),
        in_specs=[
            pl.BlockSpec((qb, D), lambda s: (s, 0)), const_spec((ACT * NBINS, D)),
            pl.BlockSpec((ACT, qb), lambda s: (0, s)), pl.BlockSpec((1, qb), lambda s: (0, s)),
        ],
        out_specs=[const_spec((16, qb)), const_spec((16, qb))],
        out_shape=[jax.ShapeDtypeStruct((16, qb), F32), jax.ShapeDtypeStruct((16, qb), F32)],
        compiler_params=params(),
        cost_estimate=pl.CostEstimate(flops=6_000_000_000, bytes_accessed=6_000_000, transcendentals=0),
        name="qstat",
    )(block_out.reshape(flat, D), value_head, bins_t, counted.astype(jnp.int32))
    value_sum = jnp.sum(q_sum[:ACT], axis=1)
    value_top = jnp.max(q_top[:ACT], axis=1)
    value_count = jnp.sum(counted.astype(F32))

    small = jnp.concatenate(
        [ln1[0], ln1[1], ln2[0], ln2[1], value_sum, value_count[None], value_top,
         jnp.zeros((512 - 2 * ACT - 1,), F32)]
    )
    tops_at = 4 * D + ACT + 1
    lane = jnp.arange(small.shape[0])
    is_top = (lane >= tops_at) & (lane < tops_at + ACT)
    for axis, size in (("dp", n_d), ("fsdp", n_f)):
        for b in axis_bits(size):
            other = xor_step(small, axis, size, b)
            small = jnp.where(is_top, jnp.maximum(small, other), small + other)
    norm_grads = small[: 4 * D].reshape(4, D).T
    value_mean = small[4 * D : 4 * D + ACT] / jnp.maximum(small[4 * D + ACT], 1.0)
    value_peak = small[tops_at : tops_at + ACT]

    def both_cores(mine):
        if nh == 1:
            return (mine,)
        theirs = xor_step(mine, "dp", n_d, 1)
        return jnp.where(core == 0, mine, theirs), jnp.where(core == 0, theirs, mine)

    both_r = both_cores(reduce_halves(grads_r, n_f, n_d, order_s))
    both_t = both_cores(reduce_halves(grads_t, n_f, n_d, order_s))

    def columns(v, at, parts):
        return jnp.concatenate([v[at + hm * q : at + hm * (q + 1)] for q in range(parts)], axis=1)

    shard_grads = (
        jnp.concatenate([columns(v, 0, 3) for v in both_t], axis=0),
        jnp.concatenate([v[:hm] for v in both_r], axis=0),
        jnp.concatenate([columns(v, hm, nc) for v in both_r], axis=0),
        jnp.concatenate([v[hm * (1 + nc) :] for v in both_r], axis=0),
    )
    masters = (w_triple, w_mixer, w_expand, w_reduce)
    firsts = (first_triple, first_mixer, first_expand, first_reduce)
    seconds = (second_triple, second_mixer, second_expand, second_reduce)
    results = []
    squares = []
    for master, gradient, moment_one, moment_two in zip(masters, shard_grads, firsts, seconds):
        first_new, second_new, update = lamb_moments(master, gradient, moment_one, moment_two)
        results.append((first_new, second_new, update))
        squares.append(jnp.sum(master * master))
        squares.append(jnp.sum(update * update))
    totals = jnp.stack(squares)
    for b in axis_bits(n_f):
        totals = totals + xor_step(totals, "fsdp", n_f, b)
    roots = jnp.sqrt(totals)
    weight_norms, update_norms = roots[0::2], roots[1::2]
    new_list = []
    for i in range(4):
        ratio = weight_norms[i] / (update_norms[i] + RATIO_EPSILON)
        new_list.append(masters[i] - LEARNING_RATE * ratio * results[i][2])
    small_first, small_second, small_update = lamb_moments(
        norm_params, norm_grads, first_norms, second_norms
    )
    small_weight = jnp.sqrt(jnp.sum(norm_params * norm_params, axis=0))
    small_norm = jnp.sqrt(jnp.sum(small_update * small_update, axis=0))
    new_norms = (
        norm_params
        - LEARNING_RATE * (small_weight / (small_norm + RATIO_EPSILON))[None, :] * small_update
    )
    norm_table = jnp.stack(
        [jnp.concatenate([weight_norms, small_weight]), jnp.concatenate([update_norms, small_norm])]
    )
    return (
        block_out, input_grad,
        new_list[0], new_list[1], new_list[2], new_list[3],
        results[0][0], results[1][0], results[2][0], results[3][0],
        results[0][1], results[1][1], results[2][1], results[3][1],
        new_norms, small_first, small_second, norm_table, value_mean, value_peak,
    )


def solution(mesh):
    n_d, n_f = mesh.shape["dp"], mesh.shape["fsdp"]
    both = ("dp", "fsdp")
    row, rep = P("fsdp", None), P()
    in_specs = (
        P(both, None, None), P(both, None, None), P(both), P(both, None), P(both, None, None), rep,
        row, row, row, row, rep,
        row, row, row, row, rep,
        row, row, row, row, rep,
    )
    out_specs = (
        (P(both, None, None),) * 2 + (row,) * 12 + (rep,) * 6
    )
    return jax.shard_map(
        functools.partial(body, n_d, n_f), mesh=mesh, in_specs=in_specs, out_specs=out_specs,
        check_vma=False,
    )
```

```python
import functools

import jax
import jax.numpy as jnp
from jax import lax
from jax.experimental import pallas as pl
from jax.experimental.pallas import tpu as pltpu
from jax.sharding import PartitionSpec as P

HEADS = 8
HEAD_DIM = 64
ACT = 11
NBINS = 256
STEP = 5

NORM_EPSILON = 1e-05
BETA_FIRST = 0.9
BETA_SECOND = 0.999
ADAM_EPSILON = 1e-06
RATIO_EPSILON = 1e-06
WEIGHT_DECAY = 0.01
LEARNING_RATE = 0.5
MASKED = -1e30

D = 512
FF = 2048
QB = 64
QUAD = 256
F32 = jnp.float32
BF16 = jnp.bfloat16
VMEM_LIMIT = 60 * 1024 * 1024

NT = (((1,), (1,)), ((), ()))
NN = (((1,), (0,)), ((), ()))
TN = (((0,), (0,)), ((), ()))


def mm(a, b, dims=NN):
    return lax.dot_general(a, b, dims, preferred_element_type=F32)


def pad_rows(v, rows):
    return jnp.concatenate([v, jnp.zeros((rows - v.shape[0], v.shape[1]), v.dtype)], axis=0)


def ln_parts(x):
    center = x - jnp.mean(x, axis=-1, keepdims=True)
    spread = jnp.mean(center * center, axis=-1, keepdims=True)
    rstd = lax.rsqrt(spread + NORM_EPSILON)
    return center * rstd, rstd


def ln_back(grad, xhat, rstd, gain):
    t = grad * gain
    m1 = jnp.mean(t, axis=-1, keepdims=True)
    m2 = jnp.mean(t * xhat, axis=-1, keepdims=True)
    return rstd * (t - m1 - xhat * m2)


def head_masks():
    lane = lax.broadcasted_iota(jnp.int32, (1, QUAD), 1)
    return [jnp.where(lane // HEAD_DIM == h, 1.0, 0.0).astype(BF16) for h in range(4)]


def stack_heads(block, masks):
    return jnp.concatenate([block * m for m in masks], axis=0)


def pair_rows(t):
    tt = t.T
    lane = lax.broadcasted_iota(jnp.int32, (QB, 2 * HEAD_DIM), 1)
    return jnp.where(lane < HEAD_DIM, tt[:QB], tt[QB:])


def place(block, size, side, core):
    if side == 0:
        return pl.multiple_of(block * size, size)
    c = core if side == 1 else 1 - core
    return pl.multiple_of(block * (2 * size) + c * size, size)


def run_copies(copies, start):
    for copy in copies:
        copy.start() if start else copy.wait()


def load_triple(refs, plan, dst, sem, me, core, start):
    for ref, (rels, side) in zip(refs, plan):
        half = ref.shape[1]
        for p, rel in enumerate(rels):
            row = place(jnp.bitwise_xor(me, rel), half, side, core)
            run_copies([pltpu.make_async_copy(ref.at[p], dst.at[pl.ds(row, half)], sem)], start)


def load_mixer(refs, plan, wm, sem, me, core, start):
    for ref, (rels, side) in zip(refs, plan):
        hm = D // wm_blocks(plan) // (1 if side == 0 else 2)
        for p, rel in enumerate(rels):
            row = place(jnp.bitwise_xor(me, rel), hm, side, core)
            run_copies([pltpu.make_async_copy(ref.at[p, pl.ds(0, hm)], wm.at[pl.ds(row, hm)], sem)], start)


def wm_blocks(plan):
    return sum(len(rels) for rels, side in plan if side != 2)


def load_ff(refs, plan, at_mixer, we, wr, sem, me, core, start):
    for ref, (rels, side) in zip(refs, plan):
        halves = 1 if side == 0 else 2
        hm = D // wm_blocks(plan) // halves
        hr = wr.shape[0] // wm_blocks(plan) // halves
        nc = we.shape[1] // D
        at = hm if at_mixer else 0
        for p, rel in enumerate(rels):
            block = jnp.bitwise_xor(me, rel)
            row, rowr = place(block, hm, side, core), place(block, hr, side, core)
            copies = []
            for q in range(nc):
                copies.append(
                    pltpu.make_async_copy(
                        ref.at[p, pl.ds(at + hm * q, hm)],
                        we.at[pl.ds(row, hm), pl.ds(q * D, D)],
                        sem,
                    )
                )
            copies.append(
                pltpu.make_async_copy(ref.at[p, pl.ds(at + hm * nc, hr)], wr.at[pl.ds(rowr, hr)], sem)
            )
            run_copies(copies, start)


def load_ff_true(ref, n_f, parts, we, wr, sem, start):
    hm = D // n_f // parts
    hr = wr.shape[0] // n_f // parts
    nc = we.shape[1] // D
    for d in range(parts):
        for i in range(n_f):
            row, rowr = (i * parts + d) * hm, (i * parts + d) * hr
            src = ref.at[d * n_f + i]
            copies = [
                pltpu.make_async_copy(
                    src.at[pl.ds(hm * q, hm)], we.at[pl.ds(row, hm), pl.ds(q * D, D)], sem
                )
                for q in range(nc)
            ]
            copies.append(pltpu.make_async_copy(src.at[pl.ds(hm * nc, hr)], wr.at[pl.ds(rowr, hr)], sem))
            run_copies(copies, start)


def f1_kernel(plan, nw, idx, lens, tok, norm, *refs):
    w_refs, (tri_out, n1_out, att_out, lse_out, wt, tri, sem) = refs[:nw], refs[nw:]
    e = pl.program_id(0)
    rows = tok.shape[1]
    padded = tri.shape[0]
    rows16 = -(-rows // 16) * 16

    @pl.when(e == 0)
    def _():
        load_triple(w_refs, plan, wt, sem, idx[0], idx[1], True)
        tri[rows16:padded] = jnp.zeros((padded - rows16, 3 * D), BF16)
        load_triple(w_refs, plan, wt, sem, idx[0], idx[1], False)

    xhat, _ = ln_parts(pad_rows(tok[0].astype(F32), rows16))
    n1 = (xhat * norm[0:1] + norm[1:2]).astype(BF16)
    n1_out[0] = n1[:rows]
    t = mm(n1, wt[...]).astype(BF16)
    tri[0:rows16, 0:D] = t[:, 0:D] * jnp.asarray(HEAD_DIM**-0.5, BF16)
    tri[0:rows16, D:] = t[:, D:]
    tri_out[0] = tri[0:rows]

    length = lens[e]
    masks = head_masks()
    lane = lax.broadcasted_iota(jnp.int32, (1, QUAD), 1) % QB
    blocks = -(-rows // QB)
    for g in range(HEADS // 4):
        gl = g * QUAD
        for j in range(blocks):
            ext = min(QB * (j + 1), rows16)
            q4 = stack_heads(tri[QB * j : QB * (j + 1), gl : gl + QUAD], masks)
            s = mm(tri[0:ext, D + gl : D + gl + QUAD], q4, NT)
            kmax = jnp.minimum(lane + QB * j, length - 1)
            krow = lax.broadcasted_iota(jnp.int32, (ext, QUAD), 0)
            s = jnp.where(krow <= kmax, s, MASKED)
            m = jnp.max(s, axis=0, keepdims=True)
            p = jnp.exp(s - m)
            total = jnp.sum(p, axis=0, keepdims=True)
            lse_out[0, pl.ds(g * blocks + j, 1), :] = m + jnp.log(total)
            pb = (p * (1.0 / total)).astype(BF16)
            live = min(QB, rows - QB * j)
            for t2 in range(2):
                cl = 2 * D + gl + 128 * t2
                o = mm(tri[0:ext, cl : cl + 128], pb[:, 128 * t2 : 128 * t2 + 128], TN)
                o = pair_rows(o).astype(BF16)
                att_out[0, QB * j : QB * j + live, gl + 128 * t2 : gl + 128 * t2 + 128] = o[:live]


def put_rows(dst, p, at, src, row, rows):
    for q in range(src.shape[1] // QUAD):
        dst[p, at : at + rows] = src[pl.ds(row, rows), q * QUAD : (q + 1) * QUAD].astype(BF16)
        at += rows
    return at


def grad_sides(refs):
    return [(refs[0], 0)] if len(refs) == 1 else [(refs[0], 1), (refs[1], 2)]


def put_ff_grads(grads, pos, idx, acc_e, acc_r, wr, acc_m=None):
    halves = len(grads)
    hm = D // len(pos) // halves
    hr = wr.shape[0] // len(pos) // halves
    for c in range(wr.shape[0] // D):
        wr[c * D : c * D + D] = acc_r[:, c * D : c * D + D].T.astype(BF16)
    for p, rel in enumerate(pos):
        block = jnp.bitwise_xor(idx[0], rel)
        for dst, side in grad_sides(grads):
            row, rowr = place(block, hm, side, idx[1]), place(block, hr, side, idx[1])
            at = put_rows(dst, p, 0, acc_e, row, hm)
            at = put_rows(dst, p, at, wr, rowr, hr)
            if acc_m is not None:
                put_rows(dst, p, at, acc_m, row, hm)


def ff_chunks(n2, glow, out, g2, we, wr, acc_e, acc_r):
    for c in range(we.shape[1] // D):
        cs = slice(c * D, c * D + D)
        ex = mm(n2, we[:, cs])
        phi = 0.5 + 0.5 * lax.erf(ex * 0.7071067811865476)
        act = (ex * phi).astype(BF16)
        gp = phi + ex * (jnp.exp(-0.5 * ex * ex) * 0.3989422804014327)
        out = out + mm(act, wr[cs])
        gact = mm(glow, wr[cs], NT)
        ge = (gp * gact).astype(BF16)
        g2 = g2 + mm(ge, we[:, cs], NT)
        acc_r[:, cs] += mm(glow, act, TN)
        acc_e[:, cs] += mm(n2, ge, TN)
    return out, g2


def f2a_kernel(plan, nw, pos, nh, idx, att_ref, tok, gl_ref, norm, *refs):
    w_refs, refs = refs[:nw], refs[nw:]
    (hid_out, out_out, g2_out, n2_out), grads, refs = refs[:4], refs[4 : 4 + nh], refs[4 + nh :]
    wm, we, wr, acc_e, acc_r, sem = refs
    e = pl.program_id(0)
    rows = tok.shape[1]
    rows16 = -(-rows // 16) * 16

    @pl.when(e == 0)
    def _():
        load_mixer(w_refs, plan, wm, sem, idx[0], idx[1], True)
        load_ff(w_refs, plan, True, we, wr, sem, idx[0], idx[1], True)
        acc_e[...] = jnp.zeros_like(acc_e)
        acc_r[...] = jnp.zeros_like(acc_r)
        load_mixer(w_refs, plan, wm, sem, idx[0], idx[1], False)
        load_ff(w_refs, plan, True, we, wr, sem, idx[0], idx[1], False)

    att = pad_rows(att_ref[0], rows16)
    glow = pad_rows(gl_ref[0], rows16)
    hidden = pad_rows(tok[0].astype(F32), rows16) + mm(att, wm[...])
    xhat, _ = ln_parts(hidden)
    n2 = (xhat * norm[2:3] + norm[3:4]).astype(BF16)
    hid_out[0] = hidden[:rows]
    n2_out[0] = n2[:rows]
    out, g2 = ff_chunks(n2, glow, hidden, jnp.zeros_like(hidden), we, wr, acc_e, acc_r)
    out_out[0] = out[:rows]
    g2_out[0] = g2[:rows]

    @pl.when(e == pl.num_programs(0) - 1)
    def _():
        put_ff_grads(grads, pos, idx, acc_e, acc_r, wr)


def f2b_kernel(plan, nw, parts, pos, nh, idx, att_ref, hid, out_ref, g2_ref, n2_ref, gl_ref, norm, wb, *refs):
    w_refs, refs = refs[:nw], refs[nw:]
    (block_out, gh_out, ga_out), grads, refs = refs[:3], refs[3 : 3 + nh], refs[3 + nh :]
    ln_out, wm, we, wr, acc_e, acc_r, acc_m, sem = refs
    e = pl.program_id(0)
    rows = hid.shape[1]
    rows16 = -(-rows // 16) * 16

    @pl.when(e == 0)
    def _():
        load_mixer(w_refs, plan, wm, sem, idx[0], idx[1], True)
        load_ff_true(wb, len(pos), parts, we, wr, sem, True)
        acc_e[...] = jnp.zeros_like(acc_e)
        acc_r[...] = jnp.zeros_like(acc_r)
        acc_m[...] = jnp.zeros_like(acc_m)
        ln_out[...] = jnp.zeros_like(ln_out)
        load_mixer(w_refs, plan, wm, sem, idx[0], idx[1], False)
        load_ff_true(wb, len(pos), parts, we, wr, sem, False)

    gain = norm[2:3]
    att = pad_rows(att_ref[0], rows16)
    glow = pad_rows(gl_ref[0], rows16)
    n2 = pad_rows(n2_ref[0], rows16)
    xhat, rstd = ln_parts(pad_rows(hid[0], rows16))
    out, g2 = ff_chunks(
        n2, glow, pad_rows(out_ref[0], rows16), pad_rows(g2_ref[0], rows16), we, wr, acc_e, acc_r
    )
    block_out[0] = out[:rows].astype(BF16)
    gh = glow.astype(F32) + ln_back(g2, xhat, rstd, gain)
    ln_out[0:1] += jnp.sum(g2 * xhat, axis=0, keepdims=True)
    ln_out[1:2] += jnp.sum(g2, axis=0, keepdims=True)
    gb = gh.astype(BF16)
    gh_out[0] = gh[:rows]
    acc_m[...] += mm(att, gb, TN)
    ga_out[0] = mm(gb, wm[...], NT)[:rows].astype(BF16)

    @pl.when(e == pl.num_programs(0) - 1)
    def _():
        put_ff_grads(grads, pos, idx, acc_e, acc_r, wr, acc_m)


def b1_kernel(pos, nh, idx, lens, tri_ref, ga_ref, lse, n1, gtri_out, *refs):
    grads, (tri, ga, gtri, dk, dv, acc) = refs[:nh], refs[nh:]
    e = pl.program_id(0)
    rows = n1.shape[1]
    padded = tri.shape[0]
    rows16 = -(-rows // 16) * 16
    low16 = rows // 16 * 16

    @pl.when(e == 0)
    def _():
        acc[...] = jnp.zeros_like(acc)
        tri[low16:padded] = jnp.zeros((padded - low16, 3 * D), BF16)
        ga[low16:padded] = jnp.zeros((padded - low16, D), BF16)

    tri[0:rows] = tri_ref[0]
    ga[0:rows] = ga_ref[0]
    dk[...] = jnp.zeros_like(dk)
    dv[...] = jnp.zeros_like(dv)
    gtri[:, 0:D] = jnp.zeros((padded, D), BF16)

    length = lens[e]
    masks = head_masks()
    lane = lax.broadcasted_iota(jnp.int32, (1, QUAD), 1) % QB
    blocks = -(-rows // QB)
    for j in range(blocks):

        @pl.when(length > QB * j)
        def _(j=j):
            ext = min(QB * (j + 1), rows16)
            kmax = jnp.minimum(lane + QB * j, length - 1)
            krow = lax.broadcasted_iota(jnp.int32, (ext, QUAD), 0)
            for g in range(HEADS // 4):
                gl = g * QUAD
                gs = slice(gl, gl + QUAD)
                q4 = stack_heads(tri[QB * j : QB * (j + 1), gs], masks)
                do4 = stack_heads(ga[QB * j : QB * (j + 1), gs], masks)
                s = mm(tri[0:ext, D + gl : D + gl + QUAD], q4, NT)
                s = jnp.where(krow <= kmax, s - lse[0, pl.ds(g * blocks + j, 1), :], MASKED)
                p = jnp.exp(s)
                dp = mm(tri[0:ext, 2 * D + gl : 2 * D + gl + QUAD], do4, NT)
                delta = jnp.sum(p * dp, axis=0, keepdims=True)
                ds = (p * (dp - delta)).astype(BF16)
                dv[0:ext, gs] += mm(p.astype(BF16), do4)
                dk[0:ext, gs] += mm(ds, q4)
                for t2 in range(2):
                    cl = D + gl + 128 * t2
                    dq = mm(tri[0:ext, cl : cl + 128], ds[:, 128 * t2 : 128 * t2 + 128], TN)
                    dq = pair_rows(dq) * HEAD_DIM**-0.5
                    gtri[QB * j : QB * (j + 1), gl + 128 * t2 : gl + 128 * t2 + 128] = dq.astype(BF16)

    gtri[0:rows16, D : 2 * D] = dk[...].astype(BF16)
    gtri[0:rows16, 2 * D :] = dv[...].astype(BF16)
    gtri_out[0] = gtri[0:rows]
    acc[...] += mm(pad_rows(n1[0], rows16), gtri[0:rows16], TN)

    @pl.when(e == pl.num_programs(0) - 1)
    def _():
        hm = D // len(pos) // nh
        for p, rel in enumerate(pos):
            block = jnp.bitwise_xor(idx[0], rel)
            for dst, side in grad_sides(grads):
                put_rows(dst, p, 0, acc, place(block, hm, side, idx[1]), hm)


def b2_kernel(plan, nw, idx, gtri, tok, gh, norm, ln2, q_sum, q_top, *refs):
    w_refs, (ig_out, ln_out, wt, sem) = refs[:nw], refs[nw:]
    e = pl.program_id(0)

    @pl.when(e == 0)
    def _():
        load_triple(w_refs, plan, wt, sem, idx[0], idx[1], True)
        ln_out[...] = jnp.zeros_like(ln_out)
        load_triple(w_refs, plan, wt, sem, idx[0], idx[1], False)

    g1 = mm(gtri[0], wt[...], NT)
    xhat, rstd = ln_parts(tok[0].astype(F32))
    ig_out[0] = (gh[0] + ln_back(g1, xhat, rstd, norm[0:1])).astype(BF16)
    ln_out[0:1] += jnp.sum(g1 * xhat, axis=0, keepdims=True)
    ln_out[1:2] += jnp.sum(g1, axis=0, keepdims=True)

    @pl.when(e == pl.num_programs(0) - 1)
    def _():
        ln_out[2:4] = ln2[0:2]
        ln_out[4:5, 0:16] = jnp.sum(q_sum[...].T, axis=0, keepdims=True)
        ln_out[5:6, 0:16] = jnp.max(q_top[...].T, axis=0, keepdims=True)


def q_kernel(total_rows, bo, vh, bins, cnt, sum_out, top_out):
    s = pl.program_id(0)
    block = bo.shape[0]

    @pl.when(s == 0)
    def _():
        sum_out[...] = jnp.zeros_like(sum_out)
        top_out[...] = jnp.full_like(top_out, MASKED)

    place = lax.broadcasted_iota(jnp.int32, (1, block), 1) + s * block
    counted = (cnt[...] > 0) & (place < total_rows)
    binrow = lax.broadcasted_iota(jnp.int32, (NBINS, block), 0)
    for a in range(ACT):
        sc = mm(vh[a * NBINS : (a + 1) * NBINS], bo[...], NT)
        picked = jnp.sum(jnp.where(binrow == bins[a : a + 1], sc, 0.0), axis=0, keepdims=True)
        sum_out[a : a + 1] += jnp.where(counted, picked, 0.0)
        top_out[a : a + 1] = jnp.maximum(top_out[a : a + 1], jnp.where(counted, picked, MASKED))
    sum_out[ACT : ACT + 1] += jnp.where(counted, 1.0, 0.0)


def lamb_moments(weight, gradient, moment_one, moment_two):
    first_new = BETA_FIRST * moment_one + (1.0 - BETA_FIRST) * gradient
    second_new = BETA_SECOND * moment_two + (1.0 - BETA_SECOND) * gradient * gradient
    update = (
        first_new
        * (1.0 / (1.0 - BETA_FIRST**STEP))
        / (jnp.sqrt(second_new * (1.0 / (1.0 - BETA_SECOND**STEP))) + ADAM_EPSILON)
        + WEIGHT_DECAY * weight
    )
    return (first_new, second_new, update)


class Squares:
    def __init__(self):
        self.total = jnp.zeros((8, 128), F32)

    def add(self, lane, weight, update):
        rows = lax.broadcasted_iota(jnp.int32, (8, 128), 0)
        lanes = lax.broadcasted_iota(jnp.int32, (8, 128), 1)
        for row, v in ((6, weight), (7, update)):
            one = jnp.sum(jnp.sum(v * v, axis=0, keepdims=True), axis=1, keepdims=True)
            self.total = self.total + jnp.where((rows == row) & (lanes == lane), one, 0.0)


def lamb_piece(state, outs, grad, rows, cols, squares, lane):
    weight = state[0][rows, cols]
    first_new, second_new, update = lamb_moments(weight, grad, state[1][rows, cols], state[2][rows, cols])
    for out, v in zip(outs, (first_new, second_new, update)):
        out[rows, cols] = v
    squares.add(lane, weight, update)


def core_halves(idx, parts):
    if len(parts) == 1:
        return [lambda rows: parts[0][rows]]
    own = idx[1] == 0
    return [
        lambda rows: jnp.where(own, parts[0][rows], parts[1][rows]),
        lambda rows: jnp.where(own, parts[1][rows], parts[0][rows]),
    ]


def lamb_mlp_kernel(n_f, nh, rows_a, idx, *refs):
    parts, refs = refs[:nh], refs[nh:]
    states = [refs[3 * i : 3 * i + 3] for i in range(3)]
    outs = [refs[9 + 3 * i : 12 + 3 * i] for i in range(3)]
    sq_out = refs[18]
    hm = D // n_f // nh
    h2 = FF // n_f // 2
    hr = h2 // nh
    ne, nd = FF // 2 // QUAD, D // QUAD
    squares = Squares()
    for c, take in enumerate(core_halves(idx, parts)):
        rows = slice(c * hm, c * hm + hm)
        for q in range(nd):
            at = 2 * rows_a + hm * q
            grad = take(slice(at, at + hm))
            lamb_piece(states[0], outs[0], grad, rows, slice(q * QUAD, (q + 1) * QUAD), squares, 1)
        for h in range(2):
            for q in range(ne):
                at = rows_a * h + hm * q
                grad = take(slice(at, at + hm))
                for k in range(QUAD // h2):
                    i = q * (QUAD // h2) + k
                    col = (2 * i + h) * h2
                    lamb_piece(
                        states[1], outs[1], grad[:, k * h2 : (k + 1) * h2], rows,
                        slice(col, col + h2), squares, 2,
                    )
            for q in range(nd):
                at = rows_a * h + hm * ne + hr * q
                grad = take(slice(at, at + hr))
                row = h * h2 + c * hr
                lamb_piece(
                    states[2], outs[2], grad, slice(row, row + hr),
                    slice(q * QUAD, (q + 1) * QUAD), squares, 3,
                )
    sq_out[...] = squares.total


def lamb_triple_kernel(n_f, nh, idx, *refs):
    parts, refs = refs[:nh], refs[nh:]
    sq_in, state, outs, sq_out = refs[0], refs[1:4], refs[4:7], refs[7]
    hm = D // n_f // nh
    squares = Squares()
    for c, take in enumerate(core_halves(idx, parts)):
        for q in range(3 * D // QUAD):
            lamb_piece(
                state, outs, take(slice(hm * q, hm * q + hm)), slice(c * hm, c * hm + hm),
                slice(q * QUAD, (q + 1) * QUAD), squares, 0,
            )
    sq_out[...] = squares.total + sq_in[...]


def merge_small(mine, other):
    row = lax.broadcasted_iota(jnp.int32, mine.shape, 0)
    return jnp.where(row == 5, jnp.maximum(mine, other), mine + other)


def final_kernel(one, two, norms, firsts, seconds, *refs):
    masters, updates, news = refs[:4], refs[4:8], refs[8:12]
    norms_out, first_out, second_out, table_out, mean_out, peak_out = refs[12:]
    small = merge_small(one[...], two[...])
    roots = jnp.sqrt(small[6:8, 0:128])
    for i in range(4):
        ratio = roots[0:1, i : i + 1] / (roots[1:2, i : i + 1] + RATIO_EPSILON)
        news[i][...] = masters[i][...] - LEARNING_RATE * ratio * updates[i][...]
    weight = norms[...]
    first_new, second_new, update = lamb_moments(weight, small[0:4], firsts[...], seconds[...])
    weight_norm = jnp.sqrt(jnp.sum(weight * weight, axis=1, keepdims=True))
    update_norm = jnp.sqrt(jnp.sum(update * update, axis=1, keepdims=True))
    norms_out[...] = weight - LEARNING_RATE * (weight_norm / (update_norm + RATIO_EPSILON)) * update
    first_out[...] = first_new
    second_out[...] = second_new
    row = lax.broadcasted_iota(jnp.int32, (4, 128), 0)
    lane = lax.broadcasted_iota(jnp.int32, (4, 128), 1)
    low = lax.broadcasted_iota(jnp.int32, (1, 128), 1) < 4
    for k, v in enumerate((weight_norm, update_norm)):
        spread = jnp.sum(jnp.where(lane == row + 4, v, 0.0), axis=0, keepdims=True)
        table_out[k : k + 1] = jnp.where(low, roots[k : k + 1], spread)[:, 0:8]
    sums = small[4:5, 0:128]
    mean_out[...] = (sums / jnp.maximum(sums[:, ACT : ACT + 1], 1.0))[:, 0:ACT]
    peak_out[...] = small[5:6, 0:ACT]


def xor_step(v, axis, size, bit):
    return lax.ppermute(v, axis, [(i, i ^ bit) for i in range(size)])


def axis_bits(size):
    bits = []
    b = 1
    while b < size:
        bits.append(b)
        b *= 2
    return bits


def sync(*vs):
    return lax.optimization_barrier(vs)


def halving_positions(order):
    rels = [0]
    for b in reversed(order):
        rels = rels + [r ^ b for r in rels]
    return rels


def add_low(a, b):
    return (a.astype(F32) + b.astype(F32)).astype(BF16)


def const_spec(shape):
    return pl.BlockSpec(shape, lambda *a: (0,) * len(shape))


SMEM = pl.BlockSpec(memory_space=pltpu.SMEM)
ANY = pl.BlockSpec(memory_space=pl.ANY)


def kernel_call(kernel, name, grid, in_specs, out, scratch, us, args, **more):
    return pl.pallas_call(
        kernel,
        grid=grid,
        in_specs=in_specs,
        out_specs=[spec for spec, _ in out],
        out_shape=[shape for _, shape in out],
        scratch_shapes=scratch,
        compiler_params=pltpu.CompilerParams(
            dimension_semantics=("arbitrary",) * len(grid), vmem_limit_bytes=VMEM_LIMIT
        ),
        cost_estimate=pl.CostEstimate(
            flops=us * 300_000_000, bytes_accessed=us * 300_000, transcendentals=0
        ),
        name=name,
        **more,
    )(*args)


def body(n_d, n_f, *args):
    (
        tokens, cotangent, lengths, valid_mask, action_bins, value_head,
        w_triple, w_mixer, w_expand, w_reduce, norm_params,
        first_triple, first_mixer, first_expand, first_reduce, first_norms,
        second_triple, second_mixer, second_expand, second_reduce, second_norms,
    ) = args
    ep, rows, _ = tokens.shape
    flat = ep * rows
    rows16 = -(-rows // 16) * 16
    padded = -(-rows // QB) * QB
    blocks = padded // QB
    me = lax.axis_index("fsdp")
    dp = lax.axis_index("dp")
    core = dp % 2
    idx = jnp.stack([me, core]).astype(jnp.int32)
    shard = D // n_f
    h2 = FF // n_f // 2
    half_ff = FF // 2
    nh = 2 if shard >= 32 else 1
    parts = n_d if shard // n_d >= 16 else 1
    f_bits, d_bits = axis_bits(n_f), axis_bits(n_d)
    steps_f = lambda v, b: xor_step(v, "fsdp", n_f, b)
    steps_d = lambda v, b: xor_step(v, "dp", n_d, b)

    def own_half(w):
        n = w.shape[0] // nh
        return lax.dynamic_slice_in_dim(w, core * n, n, 0) if nh == 2 else w

    def own_part(w):
        n = w.shape[0] // parts
        return lax.dynamic_slice_in_dim(w, dp * n, n, 0) if parts > 1 else w

    def ff_half(w, h):
        return jnp.concatenate([w[:, (2 * i + h) * h2 : (2 * i + h + 1) * h2] for i in range(n_f)], axis=1)

    def under(w):
        return [w[:, q * D : (q + 1) * D] for q in range(w.shape[1] // D)]

    own_t = own_half(w_triple).astype(BF16)
    near, rest_bits = f_bits[0], f_bits[1:]
    rels_a = [0]
    for b in rest_bits:
        rels_a = rels_a + [r ^ b for r in rels_a]
    t_one = jnp.stack([own_t] + [steps_f(own_t, r) for r in rels_a[1:]])
    rels_b = [r ^ near for r in rels_a]

    own_e = w_expand.astype(BF16)
    own_r = w_reduce.astype(BF16)
    own_a = jnp.concatenate(
        [own_half(w_mixer).astype(BF16)]
        + under(own_half(ff_half(own_e, 0)))
        + [own_half(own_r[:h2])],
        axis=0,
    )
    own_b = jnp.concatenate(under(own_part(ff_half(own_e, 1))) + [own_part(own_r[h2:])], axis=0)
    norm_t = norm_params.T
    norm = jnp.concatenate([norm_t, jnp.zeros((4, D), F32)], axis=0)
    places = jnp.arange(rows)
    inside = places[None, :] < lengths[:, None]
    glow = jnp.where(inside[:, :, None], cotangent, jnp.zeros((), BF16))
    counted = ((valid_mask == 1) & inside).astype(jnp.int32).reshape(1, flat)
    bins_t = action_bins.reshape(flat, ACT).T

    ep_block = lambda width: pl.BlockSpec((1, rows, width), lambda e: (e, 0, 0))
    ep_shape = lambda width, dtype: jax.ShapeDtypeStruct((ep, rows, width), dtype)
    low = lambda width: (ep_block(width), ep_shape(width, BF16))
    wide = lambda width: (ep_block(width), ep_shape(width, F32))
    whole = lambda shape: (const_spec(shape), jax.ShapeDtypeStruct(shape, F32))
    norm_spec = const_spec((8, D))
    lse_spec = pl.BlockSpec((1, 16, QUAD), lambda e: (e, 0, 0))
    dma = pltpu.SemaphoreType.DMA
    wt_scratch = pltpu.VMEM((D, 3 * D), BF16)

    waves = list(reversed(f_bits))
    a_buf, a_rels = own_a[None], [0]
    a_buf, own_b, t_one = sync(a_buf, own_b, t_one)
    b_all = lax.all_gather(own_b, ("dp", "fsdp") if parts > 1 else "fsdp", axis=0)
    t_refs, t_plan = [t_one, steps_f(t_one, near)], [(rels_a, nh - 1), (rels_b, nh - 1)]
    got = steps_f(a_buf, waves[0])
    if nh == 2:
        t_refs.append(steps_d(t_one, 1))
        t_plan.append((rels_a, 2))
    a_buf, got, *t_refs = sync(a_buf, got, *t_refs)
    if nh == 2:
        t_refs.append(steps_d(t_refs[1], 1))
        t_plan.append((rels_b, 2))
    nw = len(t_refs)
    a_buf, a_rels = jnp.concatenate([a_buf, got], axis=0), a_rels + [r ^ waves[0] for r in a_rels]
    for b in waves[1:-1]:
        a_buf = jnp.concatenate([a_buf, steps_f(a_buf, b)], axis=0)
        a_rels = a_rels + [r ^ b for r in a_rels]
    glow, bins_t, counted, norm, a_buf, *t_refs = sync(glow, bins_t, counted, norm, a_buf, *t_refs)

    last = waves[-1]
    a_two = steps_f(a_buf, last)
    a_refs, a_plan = [a_buf, a_two], [(a_rels, nh - 1), ([r ^ last for r in a_rels], nh - 1)]
    if nh == 2:
        a_refs.append(steps_d(a_buf, 1))
        a_plan.append((a_rels, 2))
    triple, n1, attended, lse = kernel_call(
        functools.partial(f1_kernel, t_plan, nw), "f1", (ep,),
        [SMEM, SMEM, ep_block(D), norm_spec] + [ANY] * nw,
        [low(3 * D), low(D), low(D), (lse_spec, jax.ShapeDtypeStruct((ep, 16, QUAD), F32))],
        [wt_scratch, pltpu.VMEM((padded, 3 * D), BF16), dma], 23,
        (idx, lengths, tokens, norm, *t_refs),
    )
    attended, *a_refs = sync(attended, *a_refs)
    if nh == 2:
        a_refs.append(steps_d(a_refs[1], 1))
        a_plan.append((a_plan[1][0], 2))
    na = len(a_refs)

    order = f_bits[1:2] + f_bits[:1] + f_bits[2:]
    pos = halving_positions(order)
    hm, hr = shard // nh, h2 // nh
    rows_a = hm * (half_ff // QUAD) + hr * (D // QUAD)
    rows_b = rows_a + hm * (D // QUAD)
    rows_t = 6 * hm
    half = n_f // 2
    grad_out = lambda n: [(const_spec((n_f, n, QUAD)), jax.ShapeDtypeStruct((n_f, n, QUAD), BF16))] * nh
    ff_scratch = [
        pltpu.VMEM((D, D), BF16), pltpu.VMEM((D, half_ff), BF16), pltpu.VMEM((half_ff, D), BF16),
        pltpu.VMEM((D, half_ff), F32), pltpu.VMEM((D, half_ff), F32),
    ]
    hidden, out_part, g2_part, n2, *grads_a = kernel_call(
        functools.partial(f2a_kernel, a_plan, na, pos, nh), "f2a", (ep,),
        [SMEM, ep_block(D), ep_block(D), ep_block(D), norm_spec] + [ANY] * na,
        [wide(D), wide(D), wide(D), low(D)] + grad_out(rows_a),
        ff_scratch + [dma], 25, (idx, attended, tokens, glow, norm, *a_refs),
    )

    def chip_halves(grads, other):
        if nh == 1:
            return grads[0][:half], grads[0][half:]
        return add_low(grads[0][:half], other[:half]), add_low(grads[0][half:], other[half:])

    def other_core(grads):
        return steps_d(grads[1], 1) if nh == 2 else grads[0]

    def halves(keep, got):
        n = keep.shape[0] // 2
        return add_low(keep[:n], got[:n]), add_low(keep[n:], got[n:])

    n2, *grads_a = sync(n2, *grads_a)
    other_a = other_core(grads_a)
    block_out, gh, ga, *rest = kernel_call(
        functools.partial(f2b_kernel, a_plan, na, parts, pos, nh), "f2b", (ep,),
        [SMEM] + [ep_block(D)] * 6 + [norm_spec, ANY] + [ANY] * na,
        [low(D), wide(D), low(D)] + grad_out(rows_b) + [whole((8, D))],
        ff_scratch + [pltpu.VMEM((D, D), F32), dma], 27,
        (idx, attended, hidden, out_part, g2_part, n2, glow, norm, b_all, *a_refs),
    )
    grads_b, ln2 = rest[:nh], rest[nh]
    ga, other_a, *grads_b = sync(ga, other_a, *grads_b)
    other_b = other_core(grads_b)
    keep_a, send_a = chip_halves(grads_a, other_a)
    keep_b, send_b = chip_halves(grads_b, other_b)
    send = jnp.concatenate([send_a, send_b], axis=1)
    keep = jnp.concatenate([keep_a, keep_b], axis=1)
    ga, send, keep = sync(ga, send, keep)

    got = steps_f(send, order[0])
    gtri, *grads_t = kernel_call(
        functools.partial(b1_kernel, pos, nh), "b1", (ep,),
        [SMEM, SMEM, ep_block(3 * D), ep_block(D), lse_spec, ep_block(D)],
        [low(3 * D)] + grad_out(rows_t),
        [
            pltpu.VMEM((padded, 3 * D), BF16), pltpu.VMEM((padded, D), BF16),
            pltpu.VMEM((padded, 3 * D), BF16), pltpu.VMEM((rows16, D), F32),
            pltpu.VMEM((rows16, D), F32), pltpu.VMEM((D, 3 * D), F32),
        ],
        27, (idx, lengths, triple, ga, lse, n1),
    )
    gtri, keep, got, *grads_t = sync(gtri, keep, got, *grads_t)
    other_t = other_core(grads_t)
    keep, send = halves(keep, got)
    keep_t, send_t = chip_halves(grads_t, other_t)
    block_out, keep, send, keep_t, send_t = sync(block_out, keep, send, keep_t, send_t)

    got_t, got = steps_f(send_t, order[0]), steps_f(send, order[1])
    qb = 256
    steps = -(-flat // qb)
    q_sum, q_top = kernel_call(
        functools.partial(q_kernel, flat), "qstat", (steps,),
        [
            pl.BlockSpec((qb, D), lambda s: (s, 0)), const_spec((ACT * NBINS, D)),
            pl.BlockSpec((ACT, qb), lambda s: (0, s)), pl.BlockSpec((1, qb), lambda s: (0, s)),
        ],
        [whole((16, qb))] * 2, [], 10, (block_out.reshape(flat, D), value_head, bins_t, counted),
    )
    gtri, q_sum, keep, got, keep_t, got_t = sync(gtri, q_sum, keep, got, keep_t, got_t)

    late = order[2:]
    keep_t, send_t = halves(keep_t, got_t)
    if late:
        keep, send = halves(keep, got)
    else:
        keep = add_low(keep, got)
    gtri, keep, keep_t, send_t = sync(gtri, keep, keep_t, send_t)
    got_t = steps_f(send_t, order[1])
    if late:
        got = steps_f(send, late[0])
    input_grad, small = kernel_call(
        functools.partial(b2_kernel, t_plan, nw), "b2", (ep,),
        [SMEM, ep_block(3 * D), ep_block(D), ep_block(D), norm_spec]
        + [const_spec((8, D)), const_spec((16, qb)), const_spec((16, qb))] + [ANY] * nw,
        [low(D), whole((8, D))], [wt_scratch, dma], 11,
        (idx, gtri, tokens, gh, norm, ln2, q_sum, q_top, *t_refs),
    )
    small, keep, got, keep_t, got_t = sync(small, keep, got, keep_t, got_t)

    x_bits = d_bits[nh - 1 :]
    if late:
        keep_t, send_t = halves(keep_t, got_t)
        keep = add_low(keep, got)
    else:
        keep_t = add_low(keep_t, got_t)
    for b in late[1:]:
        n = keep.shape[0] // 2
        keep = add_low(keep[:n], steps_f(keep[n:], b))
    red = keep[0]
    for b in x_bits[:-1]:
        red = add_low(red, steps_d(red, b))
    small, red, keep_t = sync(small, red, keep_t)
    if late:
        got_t = steps_f(send_t, late[0])
    got_red = steps_d(red, x_bits[-1])
    small = merge_small(small, steps_d(small, d_bits[0]))
    small, red, got_red, keep_t, got_t = sync(small, red, got_red, keep_t, got_t)
    red = red.astype(F32) + got_red.astype(F32)
    if late:
        keep_t = add_low(keep_t, got_t)
    for b in late[1:]:
        n = keep_t.shape[0] // 2
        keep_t = add_low(keep_t[:n], steps_f(keep_t[n:], b))
    red_t = keep_t[0]
    for b in x_bits[:-1]:
        red_t = add_low(red_t, steps_d(red_t, b))
    red, red_t, small = sync(red, red_t, small)
    got_rt = steps_d(red_t, x_bits[-1])
    for b in d_bits[1:]:
        small = merge_small(small, steps_d(small, b))
    red_parts = [red] + ([steps_d(red, 1)] if nh == 2 else [])

    like = lambda w: whole(w.shape)
    full = lambda *ws: [const_spec(w.shape) for w in ws]
    mlp_state = (
        w_mixer, first_mixer, second_mixer, w_expand, first_expand, second_expand,
        w_reduce, first_reduce, second_reduce,
    )
    *mlp_out, sq_mlp = kernel_call(
        functools.partial(lamb_mlp_kernel, n_f, nh, rows_a), "lamb_mlp", (1,),
        [SMEM] + full(*red_parts, *mlp_state),
        [like(w) for w in (w_mixer, w_expand, w_reduce) for _ in range(3)] + [whole((8, 128))],
        [], 4, (idx, *red_parts, *mlp_state),
    )
    small, sq_mlp, red_t, got_rt = sync(small, sq_mlp, red_t, got_rt)
    red_t = red_t.astype(F32) + got_rt.astype(F32)
    parts_t = [red_t] + ([steps_d(red_t, 1)] if nh == 2 else [])
    tri_state = (w_triple, first_triple, second_triple)
    *tri_out, squares = kernel_call(
        functools.partial(lamb_triple_kernel, n_f, nh), "lamb_triple", (1,),
        [SMEM] + full(*parts_t, sq_mlp, *tri_state),
        [like(w_triple)] * 3 + [whole((8, 128))],
        [], 2, (idx, *parts_t, sq_mlp, *tri_state),
    )

    small = small + jnp.pad(squares, ((0, 0), (0, D - 128)))
    for b in f_bits[:-1]:
        small = merge_small(small, steps_f(small, b))
    small_two = steps_f(small, f_bits[-1])
    masters = (w_triple, w_mixer, w_expand, w_reduce)
    updates = (tri_out[2], mlp_out[2], mlp_out[5], mlp_out[8])
    firsts_t, seconds_t = first_norms.T, second_norms.T
    *news, norms_out, first_out, second_out, norm_table, mean, peak = kernel_call(
        final_kernel, "final", (1,),
        full(small, small_two, norm_t, firsts_t, seconds_t, *masters, *updates),
        [like(w) for w in masters]
        + [whole((4, D))] * 3 + [whole((2, 8)), whole((1, ACT)), whole((1, ACT))],
        [], 3, (small, small_two, norm_t, firsts_t, seconds_t, *masters, *updates),
    )
    return (
        block_out, input_grad, *news,
        tri_out[0], mlp_out[0], mlp_out[3], mlp_out[6],
        tri_out[1], mlp_out[1], mlp_out[4], mlp_out[7],
        norms_out.T, first_out.T, second_out.T, norm_table, mean.reshape(ACT), peak.reshape(ACT),
    )


def solution(mesh):
    n_d, n_f = mesh.shape["dp"], mesh.shape["fsdp"]
    both = ("dp", "fsdp")
    row, rep = P("fsdp", None), P()
    in_specs = (
        P(both, None, None), P(both, None, None), P(both), P(both, None), P(both, None, None), rep,
        row, row, row, row, rep,
        row, row, row, row, rep,
        row, row, row, row, rep,
    )
    out_specs = (
        (P(both, None, None),) * 2 + (row,) * 12 + (rep,) * 6
    )
    return jax.shard_map(
        functools.partial(body, n_d, n_f), mesh=mesh, in_specs=in_specs, out_specs=out_specs,
        check_vma=False,
    )
```

```python
import functools

import jax
import jax.numpy as jnp
from jax import lax
from jax.experimental import pallas as pl
from jax.experimental.pallas import tpu as pltpu
from jax.sharding import PartitionSpec as P

HEADS = 8
HEAD_DIM = 64
ACT = 11
NBINS = 256
STEP = 5

NORM_EPSILON = 1e-05
BETA_FIRST = 0.9
BETA_SECOND = 0.999
ADAM_EPSILON = 1e-06
RATIO_EPSILON = 1e-06
WEIGHT_DECAY = 0.01
LEARNING_RATE = 0.5
MASKED = -1e30

D = 512
FF = 2048
QB = 64
PACK = 256
QUAD = 256
F32 = jnp.float32
BF16 = jnp.bfloat16
VMEM_LIMIT = 60 * 1024 * 1024

NT = (((1,), (1,)), ((), ()))
NN = (((1,), (0,)), ((), ()))
TN = (((0,), (0,)), ((), ()))


def mm(a, b, dims=NN):
    return lax.dot_general(a, b, dims, preferred_element_type=F32)


def pad_rows(v, rows):
    if v.shape[0] == rows:
        return v
    return jnp.concatenate([v, jnp.zeros((rows - v.shape[0], v.shape[1]), v.dtype)], axis=0)


def ln_parts(x):
    center = x - jnp.mean(x, axis=-1, keepdims=True)
    spread = jnp.mean(center * center, axis=-1, keepdims=True)
    rstd = lax.rsqrt(spread + NORM_EPSILON)
    return center * rstd, rstd


def ln_back(grad, xhat, rstd, gain):
    t = grad * gain
    m1 = jnp.mean(t, axis=-1, keepdims=True)
    m2 = jnp.mean(t * xhat, axis=-1, keepdims=True)
    return rstd * (t - m1 - xhat * m2)


def head_masks():
    lane = lax.broadcasted_iota(jnp.int32, (1, QUAD), 1)
    return [jnp.where(lane // HEAD_DIM == h, 1.0, 0.0).astype(BF16) for h in range(4)]


def stack_heads(block, masks):
    return jnp.concatenate([block * m for m in masks], axis=0)


def own_lanes(t):
    head = lax.broadcasted_iota(jnp.int32, (QB, QUAD), 1) // HEAD_DIM
    out = t[0:QB]
    for h in range(1, 4):
        out = jnp.where(head == h, t[QB * h : QB * (h + 1)], out)
    return out


def place(block, size, side, core):
    if side == 0:
        return pl.multiple_of(block * size, size)
    c = core if side == 1 else 1 - core
    return pl.multiple_of(block * (2 * size) + c * size, size)


def run_copies(copies, start):
    for copy in copies:
        copy.start() if start else copy.wait()


def load_triple(refs, plan, dst, sem, me, core, start):
    for ref, (rels, side) in zip(refs, plan):
        half = ref.shape[1]
        for p, rel in enumerate(rels):
            row = place(jnp.bitwise_xor(me, rel), half, side, core)
            run_copies([pltpu.make_async_copy(ref.at[p], dst.at[pl.ds(row, half)], sem)], start)


def load_mixer(refs, plan, wm, sem, me, core, start):
    for ref, (rels, side) in zip(refs, plan):
        hm = D // wm_blocks(plan) // (1 if side == 0 else 2)
        for p, rel in enumerate(rels):
            row = place(jnp.bitwise_xor(me, rel), hm, side, core)
            run_copies([pltpu.make_async_copy(ref.at[p, pl.ds(0, hm)], wm.at[pl.ds(row, hm)], sem)], start)


def wm_blocks(plan):
    return sum(len(rels) for rels, side in plan if side != 2)


def load_ff(refs, plan, at_mixer, we, wr, sem, me, core, start):
    for ref, (rels, side) in zip(refs, plan):
        halves = 1 if side == 0 else 2
        hm = D // wm_blocks(plan) // halves
        hr = wr.shape[0] // wm_blocks(plan) // halves
        nc = we.shape[1] // D
        at = hm if at_mixer else 0
        for p, rel in enumerate(rels):
            block = jnp.bitwise_xor(me, rel)
            row, rowr = place(block, hm, side, core), place(block, hr, side, core)
            copies = []
            for q in range(nc):
                copies.append(
                    pltpu.make_async_copy(
                        ref.at[p, pl.ds(at + hm * q, hm)],
                        we.at[pl.ds(row, hm), pl.ds(q * D, D)],
                        sem,
                    )
                )
            copies.append(
                pltpu.make_async_copy(ref.at[p, pl.ds(at + hm * nc, hr)], wr.at[pl.ds(rowr, hr)], sem)
            )
            run_copies(copies, start)


def f1_kernel(plan, nw, idx, lens, tok, norm, *refs):
    w_refs, (tri_out, n1_out, att_out, lse_out, wt, tri, sem) = refs[:nw], refs[nw:]
    e = pl.program_id(0)
    rows = tok.shape[1]
    padded = tri.shape[0]
    rows16 = -(-rows // 16) * 16

    @pl.when(e == 0)
    def _():
        load_triple(w_refs, plan, wt, sem, idx[0], idx[1], True)
        tri[rows16:padded] = jnp.zeros((padded - rows16, 3 * D), BF16)
        load_triple(w_refs, plan, wt, sem, idx[0], idx[1], False)

    xhat, _ = ln_parts(pad_rows(tok[0].astype(F32), rows16))
    n1 = (xhat * norm[0:1] + norm[1:2]).astype(BF16)
    n1_out[0] = n1[:rows]
    t = mm(n1, wt[...]).astype(BF16)
    tri[0:rows16, 0:D] = t[:, 0:D] * jnp.asarray(HEAD_DIM**-0.5, BF16)
    tri[0:rows16, D:] = t[:, D:]
    tri_out[0] = tri[0:rows]

    length = lens[e]
    masks = head_masks()
    lane = lax.broadcasted_iota(jnp.int32, (1, QUAD), 1) % QB
    blocks = -(-rows // QB)
    for g in range(HEADS // 4):
        gl = g * QUAD
        for j in range(blocks):
            ext = min(QB * (j + 1), rows16)
            q4 = stack_heads(tri[QB * j : QB * (j + 1), gl : gl + QUAD], masks)
            s = mm(tri[0:ext, D + gl : D + gl + QUAD], q4, NT)
            kmax = jnp.minimum(lane + QB * j, length - 1)
            krow = lax.broadcasted_iota(jnp.int32, (ext, QUAD), 0)
            s = jnp.where(krow <= kmax, s, MASKED)
            m = jnp.max(s, axis=0, keepdims=True)
            p = jnp.exp(s - m)
            total = jnp.sum(p, axis=0, keepdims=True)
            lse_out[0, pl.ds(g * blocks + j, 1), :] = m + jnp.log(total)
            pb = (p * (1.0 / total)).astype(BF16)
            live = min(QB, rows - QB * j)
            o = own_lanes(mm(pb, tri[0:ext, 2 * D + gl : 2 * D + gl + QUAD], TN)).astype(BF16)
            att_out[0, QB * j : QB * j + live, gl : gl + QUAD] = o[:live]


def put_rows(dst, at_index, at, src, row, rows):
    for q in range(src.shape[1] // QUAD):
        dst[(*at_index, slice(at, at + rows))] = src[pl.ds(row, rows), q * QUAD : (q + 1) * QUAD].astype(BF16)
        at += rows
    return at


def put_ff_grads(keep, send, pos, idx, acc_e, acc_r, wr, acc_m=None):
    halves, count = keep.shape[:2]
    hm = D // len(pos) // halves
    hr = wr.shape[0] // len(pos) // halves
    for c in range(wr.shape[0] // D):
        wr[c * D : c * D + D] = acc_r[:, c * D : c * D + D].T.astype(BF16)
    for p, rel in enumerate(pos):
        block = jnp.bitwise_xor(idx[0], rel)
        dst = keep if p < count else send
        for c in range(halves):
            side = 0 if halves == 1 else c + 1
            row, rowr = place(block, hm, side, idx[1]), place(block, hr, side, idx[1])
            at = put_rows(dst, (c, p % count), 0, acc_e, row, hm)
            at = put_rows(dst, (c, p % count), at, wr, rowr, hr)
            if acc_m is not None:
                put_rows(dst, (c, p % count), at, acc_m, row, hm)


def ff_chunks(n2, glow, out, g2, we, wr, acc_e, acc_r):
    for c in range(we.shape[1] // D):
        cs = slice(c * D, c * D + D)
        ex = mm(n2, we[:, cs])
        phi = 0.5 + 0.5 * lax.erf(ex * 0.7071067811865476)
        act = (ex * phi).astype(BF16)
        gp = phi + ex * (jnp.exp(-0.5 * ex * ex) * 0.3989422804014327)
        out = out + mm(act, wr[cs])
        gact = mm(glow, wr[cs], NT)
        ge = (gp * gact).astype(BF16)
        back = mm(ge, we[:, cs], NT)
        g2 = back if g2 is None else g2 + back
        acc_r[:, cs] += mm(glow, act, TN)
        acc_e[:, cs] += mm(n2, ge, TN)
    return out, g2


def f2a_kernel(plan, nw, pos, idx, att_ref, tok, gl_ref, norm, *refs):
    w_refs, refs = refs[:nw], refs[nw:]
    hid_out, out_out, g2_out, n2_out, keep, send, wm, we, wr, acc_e, acc_r, sem = refs
    s = pl.program_id(0)

    @pl.when(s == 0)
    def _():
        load_mixer(w_refs, plan, wm, sem, idx[0], idx[1], True)
        load_ff(w_refs, plan, True, we, wr, sem, idx[0], idx[1], True)
        acc_e[...] = jnp.zeros_like(acc_e)
        acc_r[...] = jnp.zeros_like(acc_r)
        load_mixer(w_refs, plan, wm, sem, idx[0], idx[1], False)
        load_ff(w_refs, plan, True, we, wr, sem, idx[0], idx[1], False)

    glow = gl_ref[...]
    hidden = tok[...].astype(F32) + mm(att_ref[...], wm[...])
    xhat, _ = ln_parts(hidden)
    n2 = (xhat * norm[2:3] + norm[3:4]).astype(BF16)
    hid_out[...] = hidden
    n2_out[...] = n2
    out, g2 = ff_chunks(n2, glow, hidden, None, we, wr, acc_e, acc_r)
    out_out[...] = out
    g2_out[...] = g2

    @pl.when(s == pl.num_programs(0) - 1)
    def _():
        put_ff_grads(keep, send, pos, idx, acc_e, acc_r, wr)


def f2b_kernel(plan, nw, pos, idx, att_ref, hid, out_ref, g2_ref, n2_ref, gl_ref, norm, *refs):
    w_refs, b_refs, refs = refs[:nw], refs[nw : 2 * nw], refs[2 * nw :]
    block_out, gh_out, ga_out, keep, send, ln_out, wm, we, wr, acc_e, acc_r, acc_m, sem = refs
    s = pl.program_id(0)

    @pl.when(s == 0)
    def _():
        load_mixer(w_refs, plan, wm, sem, idx[0], idx[1], True)
        load_ff(b_refs, plan, False, we, wr, sem, idx[0], idx[1], True)
        acc_e[...] = jnp.zeros_like(acc_e)
        acc_r[...] = jnp.zeros_like(acc_r)
        acc_m[...] = jnp.zeros_like(acc_m)
        ln_out[...] = jnp.zeros_like(ln_out)
        load_mixer(w_refs, plan, wm, sem, idx[0], idx[1], False)
        load_ff(b_refs, plan, False, we, wr, sem, idx[0], idx[1], False)

    gain = norm[2:3]
    glow = gl_ref[...]
    out, g2 = ff_chunks(n2_ref[...], glow, out_ref[...], g2_ref[...], we, wr, acc_e, acc_r)
    block_out[...] = out.astype(BF16)
    xhat, rstd = ln_parts(hid[...])
    gh = glow.astype(F32) + ln_back(g2, xhat, rstd, gain)
    ln_out[0:1] += jnp.sum(g2 * xhat, axis=0, keepdims=True)
    ln_out[1:2] += jnp.sum(g2, axis=0, keepdims=True)
    gb = gh.astype(BF16)
    gh_out[...] = gh
    acc_m[...] += mm(att_ref[...], gb, TN)
    ga_out[...] = mm(gb, wm[...], NT).astype(BF16)

    @pl.when(s == pl.num_programs(0) - 1)
    def _():
        put_ff_grads(keep, send, pos, idx, acc_e, acc_r, wr, acc_m)


def b1_kernel(pos, nh, idx, lens, tri_ref, ga_ref, lse, n1, gtri_out, *refs):
    grads, (tri, ga, gtri, dk, dv, acc, n1p, gtp) = refs[:nh], refs[nh:]
    e = pl.program_id(0)
    last = pl.num_programs(0) - 1
    rows = n1.shape[1]
    padded = tri.shape[0]
    rows16 = -(-rows // 16) * 16
    low16 = rows // 16 * 16

    @pl.when(e == 0)
    def _():
        acc[...] = jnp.zeros_like(acc)
        tri[low16:padded] = jnp.zeros((padded - low16, 3 * D), BF16)
        ga[low16:padded] = jnp.zeros((padded - low16, D), BF16)

    tri[0:rows] = tri_ref[0]
    ga[0:rows] = ga_ref[0]
    dk[...] = jnp.zeros_like(dk)
    dv[...] = jnp.zeros_like(dv)
    gtri[:, 0:D] = jnp.zeros((padded, D), BF16)

    length = lens[e]
    masks = head_masks()
    lane = lax.broadcasted_iota(jnp.int32, (1, QUAD), 1) % QB
    blocks = -(-rows // QB)
    for j in range(blocks):

        @pl.when(length > QB * j)
        def _(j=j):
            ext = min(QB * (j + 1), rows16)
            kmax = jnp.minimum(lane + QB * j, length - 1)
            krow = lax.broadcasted_iota(jnp.int32, (ext, QUAD), 0)
            for g in range(HEADS // 4):
                gl = g * QUAD
                gs = slice(gl, gl + QUAD)
                q4 = stack_heads(tri[QB * j : QB * (j + 1), gs], masks)
                do4 = stack_heads(ga[QB * j : QB * (j + 1), gs], masks)
                s = mm(tri[0:ext, D + gl : D + gl + QUAD], q4, NT)
                s = jnp.where(krow <= kmax, s - lse[0, pl.ds(g * blocks + j, 1), :], MASKED)
                p = jnp.exp(s)
                dp = mm(tri[0:ext, 2 * D + gl : 2 * D + gl + QUAD], do4, NT)
                delta = jnp.sum(p * dp, axis=0, keepdims=True)
                ds = (p * (dp - delta)).astype(BF16)
                dv[0:ext, gs] += mm(p.astype(BF16), do4)
                dk[0:ext, gs] += mm(ds, q4)
                dq = own_lanes(mm(ds, tri[0:ext, D + gl : D + gl + QUAD], TN)) * HEAD_DIM**-0.5
                gtri[QB * j : QB * (j + 1), gs] = dq.astype(BF16)

    gtri[0:rows16, D : 2 * D] = dk[...].astype(BF16)
    gtri[0:rows16, 2 * D :] = dv[...].astype(BF16)
    gtri_out[0] = gtri[0:rows]
    start = jnp.int32(0)
    for i in range(lens.shape[0] - 1):
        start = start + jnp.where(i < e, (lens[i] + 15) // 16, 0)
    at = pl.multiple_of(start * 16, 16)
    n1p[pl.ds(at, rows16)] = pad_rows(n1[0], rows16)
    gtp[pl.ds(at, rows16)] = gtri[0:rows16]

    @pl.when(e == last)
    def _():
        end = pl.multiple_of(at + rows16, 16)
        n1p[pl.ds(end, PACK)] = jnp.zeros((PACK, D), BF16)
        gtp[pl.ds(end, PACK)] = jnp.zeros((PACK, 3 * D), BF16)

        def chunk(i, carry):
            row = pl.multiple_of(i * PACK, PACK)
            acc[...] += mm(n1p[pl.ds(row, PACK)], gtp[pl.ds(row, PACK)], TN)
            return carry

        lax.fori_loop(0, (at + length + PACK - 1) // PACK, chunk, 0)
        hm = D // len(pos) // nh
        for p, rel in enumerate(pos):
            block = jnp.bitwise_xor(idx[0], rel)
            for c in range(nh):
                side = 0 if nh == 1 else c + 1
                put_rows(grads[c], (p,), 0, acc, place(block, hm, side, idx[1]), hm)


def b2_kernel(plan, nw, first, idx, gtri, tok, gh, norm, *refs):
    w_refs, refs = refs[:nw], refs[nw:]
    if first:
        ig_out, ln_out, wt, sem = refs
    else:
        _, ln1_a, ln2, q_sum, q_top, ig_out, ln_out, wt, sem = refs
    s = pl.program_id(0)

    @pl.when(s == 0)
    def _():
        load_triple(w_refs, plan, wt, sem, idx[0], idx[1], True)
        ln_out[...] = jnp.zeros_like(ln_out)
        load_triple(w_refs, plan, wt, sem, idx[0], idx[1], False)

    g1 = mm(gtri[...], wt[...], NT)
    xhat, rstd = ln_parts(tok[...].astype(F32))
    ig_out[...] = (gh[...] + ln_back(g1, xhat, rstd, norm[0:1])).astype(BF16)
    ln_out[0:1] += jnp.sum(g1 * xhat, axis=0, keepdims=True)
    ln_out[1:2] += jnp.sum(g1, axis=0, keepdims=True)

    if not first:

        @pl.when(s == pl.num_programs(0) - 1)
        def _():
            ln_out[0:2] += ln1_a[0:2]
            ln_out[2:4] = ln2[0:2]
            ln_out[4:5, 0:16] = jnp.sum(q_sum[...].T, axis=0, keepdims=True)
            ln_out[5:6, 0:16] = jnp.max(q_top[...].T, axis=0, keepdims=True)


def q_kernel(total_rows, bo, vh, bins, cnt, sum_out, top_out):
    s = pl.program_id(0)
    block = bo.shape[0]

    @pl.when(s == 0)
    def _():
        sum_out[...] = jnp.zeros_like(sum_out)
        top_out[...] = jnp.full_like(top_out, MASKED)

    place = lax.broadcasted_iota(jnp.int32, (1, block), 1) + s * block
    counted = (cnt[...] > 0) & (place < total_rows)
    binrow = lax.broadcasted_iota(jnp.int32, (NBINS, block), 0)
    for a in range(ACT):
        sc = mm(vh[a * NBINS : (a + 1) * NBINS], bo[...], NT)
        picked = jnp.sum(jnp.where(binrow == bins[a : a + 1], sc, 0.0), axis=0, keepdims=True)
        sum_out[a : a + 1] += jnp.where(counted, picked, 0.0)
        top_out[a : a + 1] = jnp.maximum(top_out[a : a + 1], jnp.where(counted, picked, MASKED))
    sum_out[ACT : ACT + 1] += jnp.where(counted, 1.0, 0.0)


def lamb_moments(weight, gradient, moment_one, moment_two):
    first_new = BETA_FIRST * moment_one + (1.0 - BETA_FIRST) * gradient
    second_new = BETA_SECOND * moment_two + (1.0 - BETA_SECOND) * gradient * gradient
    update = (
        first_new
        * (1.0 / (1.0 - BETA_FIRST**STEP))
        / (jnp.sqrt(second_new * (1.0 / (1.0 - BETA_SECOND**STEP))) + ADAM_EPSILON)
        + WEIGHT_DECAY * weight
    )
    return (first_new, second_new, update)


class Squares:
    def __init__(self):
        self.total = jnp.zeros((8, 128), F32)

    def add(self, lane, weight, update):
        rows = lax.broadcasted_iota(jnp.int32, (8, 128), 0)
        lanes = lax.broadcasted_iota(jnp.int32, (8, 128), 1)
        for row, v in ((6, weight), (7, update)):
            one = jnp.sum(jnp.sum(v * v, axis=0, keepdims=True), axis=1, keepdims=True)
            self.total = self.total + jnp.where((rows == row) & (lanes == lane), one, 0.0)


def lamb_piece(state, outs, grad, rows, cols, squares, lane):
    weight = state[0][rows, cols]
    first_new, second_new, update = lamb_moments(weight, grad, state[1][rows, cols], state[2][rows, cols])
    for out, v in zip(outs, (first_new, second_new, update)):
        out[rows, cols] = v
    squares.add(lane, weight, update)


def core_halves(idx, parts):
    if len(parts) == 1:
        return [lambda rows: parts[0][rows]]
    own = idx[1] == 0
    return [
        lambda rows: jnp.where(own, parts[0][rows], parts[1][rows]),
        lambda rows: jnp.where(own, parts[1][rows], parts[0][rows]),
    ]


def lamb_mlp_kernel(n_f, nh, rows_a, idx, *refs):
    parts, refs = refs[:nh], refs[nh:]
    states = [refs[3 * i : 3 * i + 3] for i in range(3)]
    outs = [refs[9 + 3 * i : 12 + 3 * i] for i in range(3)]
    sq_out = refs[18]
    hm = D // n_f // nh
    h2 = FF // n_f // 2
    hr = h2 // nh
    ne, nd = FF // 2 // QUAD, D // QUAD
    squares = Squares()
    for c, take in enumerate(core_halves(idx, parts)):
        rows = slice(c * hm, c * hm + hm)
        for q in range(nd):
            at = 2 * rows_a + hm * q
            grad = take(slice(at, at + hm))
            lamb_piece(states[0], outs[0], grad, rows, slice(q * QUAD, (q + 1) * QUAD), squares, 1)
        for h in range(2):
            for q in range(ne):
                at = rows_a * h + hm * q
                grad = take(slice(at, at + hm))
                for k in range(QUAD // h2):
                    i = q * (QUAD // h2) + k
                    col = (2 * i + h) * h2
                    lamb_piece(
                        states[1], outs[1], grad[:, k * h2 : (k + 1) * h2], rows,
                        slice(col, col + h2), squares, 2,
                    )
            for q in range(nd):
                at = rows_a * h + hm * ne + hr * q
                grad = take(slice(at, at + hr))
                row = h * h2 + c * hr
                lamb_piece(
                    states[2], outs[2], grad, slice(row, row + hr),
                    slice(q * QUAD, (q + 1) * QUAD), squares, 3,
                )
    sq_out[...] = squares.total


def lamb_triple_kernel(n_f, nh, idx, *refs):
    parts, refs = refs[:nh], refs[nh:]
    sq_in, state, outs, sq_out = refs[0], refs[1:4], refs[4:7], refs[7]
    hm = D // n_f // nh
    squares = Squares()
    for c, take in enumerate(core_halves(idx, parts)):
        for q in range(3 * D // QUAD):
            lamb_piece(
                state, outs, take(slice(hm * q, hm * q + hm)), slice(c * hm, c * hm + hm),
                slice(q * QUAD, (q + 1) * QUAD), squares, 0,
            )
    sq_out[...] = squares.total + sq_in[...]


def merge_small(mine, other):
    row = lax.broadcasted_iota(jnp.int32, mine.shape, 0)
    return jnp.where(row == 5, jnp.maximum(mine, other), mine + other)


def final_kernel(one, two, norms, firsts, seconds, *refs):
    masters, updates, news = refs[:4], refs[4:8], refs[8:12]
    norms_out, first_out, second_out, table_out, mean_out, peak_out = refs[12:]
    small = merge_small(one[...], two[...])
    roots = jnp.sqrt(small[6:8, 0:128])
    for i in range(4):
        ratio = roots[0:1, i : i + 1] / (roots[1:2, i : i + 1] + RATIO_EPSILON)
        news[i][...] = masters[i][...] - LEARNING_RATE * ratio * updates[i][...]
    weight = norms[...]
    first_new, second_new, update = lamb_moments(weight, small[0:4], firsts[...], seconds[...])
    weight_norm = jnp.sqrt(jnp.sum(weight * weight, axis=1, keepdims=True))
    update_norm = jnp.sqrt(jnp.sum(update * update, axis=1, keepdims=True))
    norms_out[...] = weight - LEARNING_RATE * (weight_norm / (update_norm + RATIO_EPSILON)) * update
    first_out[...] = first_new
    second_out[...] = second_new
    row = lax.broadcasted_iota(jnp.int32, (4, 128), 0)
    lane = lax.broadcasted_iota(jnp.int32, (4, 128), 1)
    low = lax.broadcasted_iota(jnp.int32, (1, 128), 1) < 4
    for k, v in enumerate((weight_norm, update_norm)):
        spread = jnp.sum(jnp.where(lane == row + 4, v, 0.0), axis=0, keepdims=True)
        table_out[k : k + 1] = jnp.where(low, roots[k : k + 1], spread)[:, 0:8]
    sums = small[4:5, 0:128]
    mean_out[...] = (sums / jnp.maximum(sums[:, ACT : ACT + 1], 1.0))[:, 0:ACT]
    peak_out[...] = small[5:6, 0:ACT]


def xor_step(v, axis, size, bit):
    return lax.ppermute(v, axis, [(i, i ^ bit) for i in range(size)])


def axis_bits(size):
    bits = []
    b = 1
    while b < size:
        bits.append(b)
        b *= 2
    return bits


def sync(*vs):
    return lax.optimization_barrier(vs)


def halving_positions(order):
    rels = [0]
    for b in reversed(order):
        rels = rels + [r ^ b for r in rels]
    return rels


def add_low(a, b):
    return (a.astype(F32) + b.astype(F32)).astype(BF16)


def const_spec(shape):
    return pl.BlockSpec(shape, lambda *a: (0,) * len(shape))


SMEM = pl.BlockSpec(memory_space=pltpu.SMEM)
ANY = pl.BlockSpec(memory_space=pl.ANY)


def kernel_call(kernel, name, grid, in_specs, out, scratch, us, args, **more):
    return pl.pallas_call(
        kernel,
        grid=grid,
        in_specs=in_specs,
        out_specs=[spec for spec, _ in out],
        out_shape=[shape for _, shape in out],
        scratch_shapes=scratch,
        compiler_params=pltpu.CompilerParams(
            dimension_semantics=("arbitrary",) * len(grid), vmem_limit_bytes=VMEM_LIMIT
        ),
        cost_estimate=pl.CostEstimate(
            flops=us * 20_000_000, bytes_accessed=us * 20_000, transcendentals=0
        ),
        name=name,
        **more,
    )(*args)


def body(n_d, n_f, *args):
    (
        tokens, cotangent, lengths, valid_mask, action_bins, value_head,
        w_triple, w_mixer, w_expand, w_reduce, norm_params,
        first_triple, first_mixer, first_expand, first_reduce, first_norms,
        second_triple, second_mixer, second_expand, second_reduce, second_norms,
    ) = args
    ep, rows, _ = tokens.shape
    flat = ep * rows
    rows16 = -(-rows // 16) * 16
    padded = -(-rows // QB) * QB
    blocks = padded // QB
    me = lax.axis_index("fsdp")
    dp = lax.axis_index("dp")
    core = dp % 2
    idx = jnp.stack([me, core]).astype(jnp.int32)
    shard = D // n_f
    h2 = FF // n_f // 2
    half_ff = FF // 2
    nh = 2 if shard >= 32 else 1
    f_bits, d_bits = axis_bits(n_f), axis_bits(n_d)
    steps_f = lambda v, b: xor_step(v, "fsdp", n_f, b)
    steps_d = lambda v, b: xor_step(v, "dp", n_d, b)

    def own_half(w):
        n = w.shape[0] // nh
        return lax.dynamic_slice_in_dim(w, core * n, n, 0) if nh == 2 else w

    def ff_half(w, h):
        return jnp.concatenate([w[:, (2 * i + h) * h2 : (2 * i + h + 1) * h2] for i in range(n_f)], axis=1)

    def under(w):
        return [w[:, q * D : (q + 1) * D] for q in range(w.shape[1] // D)]

    own_t = own_half(w_triple).astype(BF16)

    def own_piece(expand, reduce, h, first):
        rows_h = slice(h * h2, (h + 1) * h2)
        return jnp.concatenate(
            first + under(ff_half(own_half(expand), h).astype(BF16)) + [own_half(reduce[rows_h]).astype(BF16)],
            axis=0,
        )

    norm_t = norm_params.T
    norm = jnp.concatenate([norm_t, jnp.zeros((4, D), F32)], axis=0)
    ep_block = lambda width: pl.BlockSpec((1, rows, width), lambda e: (e, 0, 0))
    ep_shape = lambda width, dtype: jax.ShapeDtypeStruct((ep, rows, width), dtype)
    low = lambda width: (ep_block(width), ep_shape(width, BF16))
    wide = lambda width: (ep_block(width), ep_shape(width, F32))
    whole = lambda shape: (const_spec(shape), jax.ShapeDtypeStruct(shape, F32))
    norm_spec = const_spec((8, D))
    lse_spec = pl.BlockSpec((1, 16, QUAD), lambda e: (e, 0, 0))
    dma = pltpu.SemaphoreType.DMA
    wt_scratch = pltpu.VMEM((D, 3 * D), BF16)

    near = f_bits[0]
    rels_a = [0]
    for b in f_bits[1:]:
        rels_a = rels_a + [r ^ b for r in rels_a]
    rels_b = [r ^ near for r in rels_a]
    own_t, w_mixer_0, w_expand_0, w_reduce_0 = sync(own_t, w_mixer, w_expand, w_reduce)
    t_got = [steps_f(own_t, r) for r in rels_a[1:]]
    own_a = own_piece(w_expand_0, w_reduce_0, 0, [own_half(w_mixer_0).astype(BF16)])
    t_one = jnp.stack([own_t, *t_got])
    t_one, own_a, cotangent, valid_mask, action_bins, w_expand_1, w_reduce_1 = sync(
        t_one, own_a, cotangent, valid_mask, action_bins, w_expand, w_reduce
    )
    t_two = steps_f(t_one, near)
    t_refs, t_plan = [t_one], [(rels_a, nh - 1)]
    if nh == 2:
        t_refs.append(steps_d(t_one, 1))
        t_plan.append((rels_a, 2))
    a_one = [own_a] + [steps_f(own_a, r) for r in rels_a[1:]]
    own_b = own_piece(w_expand_1, w_reduce_1, 1, [])
    b_one = [own_b] + [steps_f(own_b, r) for r in rels_a[1:]]
    t_refs.append(t_two)
    t_plan.append((rels_b, nh - 1))
    if nh == 2:
        t_refs.append(steps_d(t_two, 1))
        t_plan.append((rels_b, 2))
    nw = len(t_refs)
    places = jnp.arange(rows)
    inside = places[None, :] < lengths[:, None]
    glow = jnp.where(inside[:, :, None], cotangent, jnp.zeros((), BF16))
    counted = ((valid_mask == 1) & inside).astype(jnp.int32).reshape(1, flat)
    bins_t = action_bins.reshape(flat, ACT).T
    a_one = jnp.stack(a_one)
    glow, bins_t, counted, norm, a_one, *t_refs = sync(glow, bins_t, counted, norm, a_one, *t_refs)
    a_two = steps_f(a_one, near)
    a_refs, a_plan = [a_one], [(rels_a, nh - 1)]
    if nh == 2:
        a_refs.append(steps_d(a_one, 1))
        a_plan.append((rels_a, 2))
    triple, n1, attended, lse = kernel_call(
        functools.partial(f1_kernel, t_plan, nw), "f1", (ep,),
        [SMEM, SMEM, ep_block(D), norm_spec] + [ANY] * nw,
        [low(3 * D), low(D), low(D), (lse_spec, jax.ShapeDtypeStruct((ep, 16, QUAD), F32))],
        [wt_scratch, pltpu.VMEM((padded, 3 * D), BF16), dma], 18,
        (idx, lengths, tokens, norm, *t_refs),
    )
    attended, a_two, *b_one = sync(attended, a_two, *b_one)
    a_refs.append(a_two)
    a_plan.append((rels_b, nh - 1))
    if nh == 2:
        a_refs.append(steps_d(a_two, 1))
        a_plan.append((rels_b, 2))
    na = len(a_refs)
    b_one = jnp.stack(b_one)
    attended, b_one, *a_refs = sync(attended, b_one, *a_refs)
    b_two = steps_f(b_one, near)
    b_refs = [b_one] + ([steps_d(b_one, 1)] if nh == 2 else [])

    order = f_bits[1:2] + f_bits[:1] + f_bits[2:]
    late = order[2:]
    pos = halving_positions(order)
    hm, hr = shard // nh, h2 // nh
    rows_a = hm * (half_ff // QUAD) + hr * (D // QUAD)
    rows_b = rows_a + hm * (D // QUAD)
    rows_t = 6 * hm
    half = n_f // 2
    low_out = lambda *shape: (const_spec(shape), jax.ShapeDtypeStruct(shape, BF16))
    ff_scratch = [
        pltpu.VMEM((D, D), BF16), pltpu.VMEM((D, half_ff), BF16), pltpu.VMEM((half_ff, D), BF16),
        pltpu.VMEM((D, half_ff), F32), pltpu.VMEM((D, half_ff), F32),
    ]
    fl = flat // 3 if flat % 48 == 0 else rows
    fl_steps = flat // fl
    fl_block = lambda width, at=0: pl.BlockSpec((fl, width), lambda i: (i + at, 0))
    fl_low = lambda width: (fl_block(width), jax.ShapeDtypeStruct((flat, width), BF16))
    fl_wide = lambda width: (fl_block(width), jax.ShapeDtypeStruct((flat, width), F32))
    tok_flat = tokens.reshape(flat, D)
    glow = glow.reshape(flat, D)
    attended = attended.reshape(flat, D)
    hidden, out_part, g2_part, n2, keep_a, send_a = kernel_call(
        functools.partial(f2a_kernel, a_plan, na, pos), "f2a", (fl_steps,),
        [SMEM] + [fl_block(D)] * 3 + [norm_spec] + [ANY] * na,
        [fl_wide(D)] * 3 + [fl_low(D)] + [low_out(nh, half, rows_a, QUAD)] * 2,
        ff_scratch + [dma], 22, (idx, attended, tok_flat, glow, norm, *a_refs),
    )

    def halves(keep, got):
        n = keep.shape[-3] // 2
        return add_low(keep[..., :n, :, :], got[..., :n, :, :]), add_low(keep[..., n:, :, :], got[..., n:, :, :])

    def core_pair(total):
        return (total[0], steps_d(total[1], 1)) if nh == 2 else (total[0], None)

    def core_halves_of(pair):
        mine, other = pair
        n = mine.shape[0] // 2
        return halves(mine, other) if other is not None else (mine[:n], mine[n:])

    def core_add(pair):
        return add_low(*pair) if pair[1] is not None else pair[0]

    n2, keep_a, send_a, b_two, *b_refs = sync(n2, keep_a, send_a, b_two, *b_refs)
    b_refs += [b_two] + ([steps_d(b_two, 1)] if nh == 2 else [])
    n2, keep_a, send_a, *b_refs = sync(n2, keep_a, send_a, *b_refs)
    got_a = steps_f(send_a, order[0])
    block_out, gh, ga, keep_b, send_b, ln2 = kernel_call(
        functools.partial(f2b_kernel, a_plan, na, pos), "f2b", (fl_steps,),
        [SMEM] + [fl_block(D)] * 6 + [norm_spec] + [ANY] * (2 * na),
        [fl_low(D), fl_wide(D), fl_low(D)] + [low_out(nh, half, rows_b, QUAD)] * 2 + [whole((8, D))],
        ff_scratch + [pltpu.VMEM((D, D), F32), dma], 24,
        (idx, attended, hidden, out_part, g2_part, n2, glow, norm, *a_refs, *b_refs),
    )
    ga, keep_a, got_a, keep_b, send_b = sync(ga, keep_a, got_a, keep_b, send_b)
    keep_a, send_a = halves(keep_a, got_a)
    ga, keep_a, send_a, keep_b, send_b = sync(ga, keep_a, send_a, keep_b, send_b)

    got_b = steps_f(send_b, order[0])
    got_a = steps_f(send_a, order[1])
    pack_rows = ep * rows16 + PACK
    gtri, *grads_t = kernel_call(
        functools.partial(b1_kernel, pos, nh), "b1", (ep,),
        [SMEM, SMEM, ep_block(3 * D), ep_block(D), lse_spec, ep_block(D)],
        [low(3 * D)] + [low_out(n_f, rows_t, QUAD)] * nh,
        [
            pltpu.VMEM((padded, 3 * D), BF16), pltpu.VMEM((padded, D), BF16),
            pltpu.VMEM((padded, 3 * D), BF16), pltpu.VMEM((rows16, D), F32),
            pltpu.VMEM((rows16, D), F32), pltpu.VMEM((D, 3 * D), F32),
            pltpu.VMEM((pack_rows, D), BF16), pltpu.VMEM((pack_rows, 3 * D), BF16),
        ],
        25, (idx, lengths, triple, ga.reshape(ep, rows, D), lse, n1),
    )
    gtri, keep_a, got_a, keep_b, got_b, *grads_t = sync(gtri, keep_a, got_a, keep_b, got_b, *grads_t)

    mine_t, other_t = core_pair(grads_t)
    sum_a = add_low(keep_a, got_a)
    sum_b = add_low(keep_b, got_b)
    mine_t, other_t, sum_a, sum_b = sync(mine_t, other_t, sum_a, sum_b)
    keep_t, send_t = core_halves_of((mine_t, other_t))
    keep_t, send_t, sum_a, sum_b = sync(keep_t, send_t, sum_a, sum_b)
    got_t = steps_f(send_t, order[0])
    pair_b, pair_a = core_pair(sum_b), core_pair(sum_a)
    keep_b, send_b = core_halves_of(pair_b)
    block_out, keep_b, send_b = sync(block_out, keep_b, send_b)
    got_b = steps_f(send_b, order[1])

    qb = 256
    steps = -(-flat // qb)
    q_sum, q_top = kernel_call(
        functools.partial(q_kernel, flat), "qstat", (steps,),
        [
            pl.BlockSpec((qb, D), lambda i: (i, 0)), const_spec((ACT * NBINS, D)),
            pl.BlockSpec((ACT, qb), lambda i: (0, i)), pl.BlockSpec((1, qb), lambda i: (0, i)),
        ],
        [whole((16, qb))] * 2, [], 10, (block_out, value_head, bins_t, counted),
    )
    gtri, q_sum, keep_t, got_t, keep_b, got_b = sync(gtri, q_sum, keep_t, got_t, keep_b, got_b)
    pair_a = sync(*pair_a, q_sum)[:2] if nh == 2 else pair_a

    def b2_call(at, n, gtri, prior, more_in):
        extra = [] if prior is None else [prior, *more_in]
        specs = [] if prior is None else [ANY] + [const_spec(v.shape) for v in more_in]
        more = {} if prior is None else {"input_output_aliases": {5 + nw: 0}}
        return kernel_call(
            functools.partial(b2_kernel, t_plan, nw, prior is None), "b2", (n,),
            [SMEM, fl_block(3 * D, at), fl_block(D, at), fl_block(D, at), norm_spec] + [ANY] * nw + specs,
            [(fl_block(D, at), jax.ShapeDtypeStruct((flat, D), BF16)), whole((8, D))],
            [wt_scratch, dma], 6, (idx, gtri, tok_flat, gh, norm, *t_refs, *extra), **more,
        )

    keep_t, send_t = halves(keep_t, got_t)
    if late:
        keep_b, send_b = halves(keep_b, got_b)
        keep_a, send_a = core_halves_of(pair_a)
        keep_ab = jnp.concatenate([keep_a, keep_b], axis=1)
        send_ab = jnp.concatenate([send_a, send_b], axis=1)
    else:
        keep_ab = jnp.concatenate([core_add(pair_a), add_low(keep_b, got_b)], axis=1)
        send_ab = keep_ab
    gtri_flat = gtri.reshape(flat, 3 * D)
    gtri_flat, keep_t, send_t, keep_ab, send_ab = sync(gtri_flat, keep_t, send_t, keep_ab, send_ab)
    got_t = steps_f(send_t, order[1])
    if late:
        got_ab = steps_f(send_ab, late[0])
    cut = (fl_steps + 1) // 2
    ig_part, ln1_a = b2_call(0, cut, gtri_flat, None, ())
    ig_part, keep_t, got_t = sync(ig_part, keep_t, got_t)

    def finish(keep, bits):
        for b in bits:
            n = keep.shape[0] // 2
            keep = add_low(keep[:n], steps_f(keep[n:], b))
        return keep[0]

    if late:
        keep_t, send_t = halves(keep_t, got_t)
        keep_t, send_t, keep_ab, got_ab, ig_part = sync(keep_t, send_t, keep_ab, got_ab, ig_part)
        got_t = steps_f(send_t, late[0])
        keep_ab = add_low(keep_ab, got_ab)
    else:
        keep_t = add_low(keep_t, got_t)
    x_bits = d_bits[nh - 1 :]
    red = finish(keep_ab, late[1:])
    for b in x_bits[:-1]:
        red = add_low(red, steps_d(red, b))
    red, ig_part = sync(red, ig_part)
    got_red = steps_d(red, x_bits[-1])
    input_grad, small = b2_call(cut, fl_steps - cut, gtri_flat, ig_part, (ln1_a, ln2, q_sum, q_top))
    small, red, got_red, keep_t, *got_t = sync(small, red, got_red, keep_t, *([got_t] if late else []))

    red_t = finish(add_low(keep_t, got_t[0]) if late else keep_t, late[1:])
    for b in x_bits[:-1]:
        red_t = add_low(red_t, steps_d(red_t, b))
    got_rt = steps_d(red_t, x_bits[-1])
    red = red.astype(F32) + got_red.astype(F32)
    red_parts = [red] + ([steps_d(red, 1)] if nh == 2 else [])
    small = merge_small(small, steps_d(small, d_bits[0]))
    small, red_t, *red_parts = sync(small, red_t, *red_parts)
    for b in d_bits[1:]:
        small = merge_small(small, steps_d(small, b))
    like = lambda w: whole(w.shape)
    full = lambda *ws: [const_spec(w.shape) for w in ws]
    mlp_state = (
        w_mixer, first_mixer, second_mixer, w_expand, first_expand, second_expand,
        w_reduce, first_reduce, second_reduce,
    )
    *mlp_out, sq_mlp = kernel_call(
        functools.partial(lamb_mlp_kernel, n_f, nh, rows_a), "lamb_mlp", (1,),
        [SMEM] + full(*red_parts, *mlp_state),
        [like(w) for w in (w_mixer, w_expand, w_reduce) for _ in range(3)] + [whole((8, 128))],
        [], 4, (idx, *red_parts, *mlp_state),
    )
    small, sq_mlp, red_t, got_rt = sync(small, sq_mlp, red_t, got_rt)
    red_t = red_t.astype(F32) + got_rt.astype(F32)
    parts_t = [red_t] + ([steps_d(red_t, 1)] if nh == 2 else [])
    tri_state = (w_triple, first_triple, second_triple)
    *tri_out, squares = kernel_call(
        functools.partial(lamb_triple_kernel, n_f, nh), "lamb_triple", (1,),
        [SMEM] + full(*parts_t, sq_mlp, *tri_state),
        [like(w_triple)] * 3 + [whole((8, 128))],
        [], 2, (idx, *parts_t, sq_mlp, *tri_state),
    )

    small = small + jnp.pad(squares, ((0, 0), (0, D - 128)))
    for b in f_bits[:-1]:
        small = merge_small(small, steps_f(small, b))
    small_two = steps_f(small, f_bits[-1])
    masters = (w_triple, w_mixer, w_expand, w_reduce)
    updates = (tri_out[2], mlp_out[2], mlp_out[5], mlp_out[8])
    firsts_t, seconds_t = first_norms.T, second_norms.T
    *news, norms_out, first_out, second_out, norm_table, mean, peak = kernel_call(
        final_kernel, "final", (1,),
        full(small, small_two, norm_t, firsts_t, seconds_t, *masters, *updates),
        [like(w) for w in masters]
        + [whole((4, D))] * 3 + [whole((2, 8)), whole((1, ACT)), whole((1, ACT))],
        [], 3, (small, small_two, norm_t, firsts_t, seconds_t, *masters, *updates),
    )
    return (
        block_out.reshape(ep, rows, D), input_grad.reshape(ep, rows, D), *news,
        tri_out[0], mlp_out[0], mlp_out[3], mlp_out[6],
        tri_out[1], mlp_out[1], mlp_out[4], mlp_out[7],
        norms_out.T, first_out.T, second_out.T, norm_table, mean.reshape(ACT), peak.reshape(ACT),
    )


def solution(mesh):
    n_d, n_f = mesh.shape["dp"], mesh.shape["fsdp"]
    both = ("dp", "fsdp")
    row, rep = P("fsdp", None), P()
    in_specs = (
        P(both, None, None), P(both, None, None), P(both), P(both, None), P(both, None, None), rep,
        row, row, row, row, rep,
        row, row, row, row, rep,
        row, row, row, row, rep,
    )
    out_specs = (
        (P(both, None, None),) * 2 + (row,) * 12 + (rep,) * 6
    )
    return jax.shard_map(
        functools.partial(body, n_d, n_f), mesh=mesh, in_specs=in_specs, out_specs=out_specs,
        check_vma=False,
    )
```

```python
import functools

import jax
import jax.numpy as jnp
from jax import lax
from jax.experimental import pallas as pl
from jax.experimental.pallas import tpu as pltpu
from jax.sharding import PartitionSpec as P

HEADS = 8
HEAD_DIM = 64
ACT = 11
NBINS = 256
STEP = 5

NORM_EPSILON = 1e-05
BETA_FIRST = 0.9
BETA_SECOND = 0.999
ADAM_EPSILON = 1e-06
RATIO_EPSILON = 1e-06
WEIGHT_DECAY = 0.01
LEARNING_RATE = 0.5
MASKED = -1e30

D = 512
FF = 2048
QB = 64
PACK = 256
QUAD = 256
F32 = jnp.float32
BF16 = jnp.bfloat16
VMEM_LIMIT = 60 * 1024 * 1024

NT = (((1,), (1,)), ((), ()))
NN = (((1,), (0,)), ((), ()))
TN = (((0,), (0,)), ((), ()))


def mm(a, b, dims=NN):
    return lax.dot_general(a, b, dims, preferred_element_type=F32)


def pad_rows(v, rows):
    if v.shape[0] == rows:
        return v
    return jnp.concatenate([v, jnp.zeros((rows - v.shape[0], v.shape[1]), v.dtype)], axis=0)


def ln_parts(x):
    center = x - jnp.mean(x, axis=-1, keepdims=True)
    spread = jnp.mean(center * center, axis=-1, keepdims=True)
    rstd = lax.rsqrt(spread + NORM_EPSILON)
    return center * rstd, rstd


def ln_back(grad, xhat, rstd, gain):
    t = grad * gain
    m1 = jnp.mean(t, axis=-1, keepdims=True)
    m2 = jnp.mean(t * xhat, axis=-1, keepdims=True)
    return rstd * (t - m1 - xhat * m2)


def head_masks():
    lane = lax.broadcasted_iota(jnp.int32, (1, QUAD), 1)
    return [jnp.where(lane // HEAD_DIM == h, 1.0, 0.0).astype(BF16) for h in range(4)]


def stack_heads(block, masks):
    return jnp.concatenate([block * m for m in masks], axis=0)


def own_lanes(t):
    head = lax.broadcasted_iota(jnp.int32, (QB, QUAD), 1) // HEAD_DIM
    out = t[0:QB]
    for h in range(1, 4):
        out = jnp.where(head == h, t[QB * h : QB * (h + 1)], out)
    return out


def place(block, size, side, core):
    if side == 0:
        return pl.multiple_of(block * size, size)
    c = core if side == 1 else 1 - core
    return pl.multiple_of(block * (2 * size) + c * size, size)


def run_copies(copies, start):
    for copy in copies:
        copy.start() if start else copy.wait()


def load_triple(refs, plan, dst, sem, me, core, start):
    for ref, (rels, side) in zip(refs, plan):
        half = ref.shape[1]
        for p, rel in enumerate(rels):
            row = place(jnp.bitwise_xor(me, rel), half, side, core)
            run_copies([pltpu.make_async_copy(ref.at[p], dst.at[pl.ds(row, half)], sem)], start)


def load_mixer(refs, plan, wm, sem, me, core, start):
    for ref, (rels, side) in zip(refs, plan):
        hm = D // wm_blocks(plan) // (1 if side == 0 else 2)
        for p, rel in enumerate(rels):
            row = place(jnp.bitwise_xor(me, rel), hm, side, core)
            run_copies([pltpu.make_async_copy(ref.at[p, pl.ds(0, hm)], wm.at[pl.ds(row, hm)], sem)], start)


def wm_blocks(plan):
    return sum(len(rels) for rels, side in plan if side != 2)


def load_ff(refs, plan, at_mixer, we, wr, sem, me, core, start):
    for ref, (rels, side) in zip(refs, plan):
        halves = 1 if side == 0 else 2
        hm = D // wm_blocks(plan) // halves
        hr = wr.shape[0] // wm_blocks(plan) // halves
        nc = we.shape[1] // D
        at = hm if at_mixer else 0
        for p, rel in enumerate(rels):
            block = jnp.bitwise_xor(me, rel)
            row, rowr = place(block, hm, side, core), place(block, hr, side, core)
            copies = []
            for q in range(nc):
                copies.append(
                    pltpu.make_async_copy(
                        ref.at[p, pl.ds(at + hm * q, hm)],
                        we.at[pl.ds(row, hm), pl.ds(q * D, D)],
                        sem,
                    )
                )
            copies.append(
                pltpu.make_async_copy(ref.at[p, pl.ds(at + hm * nc, hr)], wr.at[pl.ds(rowr, hr)], sem)
            )
            run_copies(copies, start)


def f1_kernel(plan, nw, idx, lens, tok, norm, *refs):
    w_refs, (tri_out, n1_out, att_out, lse_out, wt, tri, sem) = refs[:nw], refs[nw:]
    e = pl.program_id(0)
    rows = tok.shape[1]
    padded = tri.shape[0]
    rows16 = -(-rows // 16) * 16

    @pl.when(e == 0)
    def _():
        load_triple(w_refs, plan, wt, sem, idx[0], idx[1], True)
        tri[rows16:padded] = jnp.zeros((padded - rows16, 3 * D), BF16)
        load_triple(w_refs, plan, wt, sem, idx[0], idx[1], False)

    xhat, _ = ln_parts(pad_rows(tok[0].astype(F32), rows16))
    n1 = (xhat * norm[0:1] + norm[1:2]).astype(BF16)
    n1_out[0] = n1[:rows]
    t = mm(n1, wt[...]).astype(BF16)
    tri[0:rows16, 0:D] = t[:, 0:D] * jnp.asarray(HEAD_DIM**-0.5, BF16)
    tri[0:rows16, D:] = t[:, D:]
    tri_out[0] = tri[0:rows]

    length = lens[e]
    masks = head_masks()
    lane = lax.broadcasted_iota(jnp.int32, (1, QUAD), 1) % QB
    blocks = -(-rows // QB)
    chains = [(j, g * QUAD, g * blocks + j) for j in range(blocks) for g in range(HEADS // 4)]
    exts = [min(QB * (j + 1), rows16) for j, _, _ in chains]
    q4 = [stack_heads(tri[QB * j : QB * (j + 1), gl : gl + QUAD], masks) for j, gl, _ in chains]
    s = [mm(tri[0:x, D + gl : D + gl + QUAD], q, NT) for (_, gl, _), x, q in zip(chains, exts, q4)]
    pb = []
    for (j, _, at), x, v in zip(chains, exts, s):
        kmax = jnp.minimum(lane + QB * j, length - 1)
        krow = lax.broadcasted_iota(jnp.int32, (x, QUAD), 0)
        v = jnp.where(krow <= kmax, v, MASKED)
        m = jnp.max(v, axis=0, keepdims=True)
        p = jnp.exp(v - m)
        total = jnp.sum(p, axis=0, keepdims=True)
        lse_out[0, pl.ds(at, 1), :] = m + jnp.log(total)
        pb.append((p * (1.0 / total)).astype(BF16))
    o = [mm(v, tri[0:x, 2 * D + gl : 2 * D + gl + QUAD], TN) for (_, gl, _), x, v in zip(chains, exts, pb)]
    for (j, gl, _), v in zip(chains, o):
        live = min(QB, rows - QB * j)
        att_out[0, QB * j : QB * j + live, gl : gl + QUAD] = own_lanes(v).astype(BF16)[:live]


def put_rows(dst, at_index, at, src, row, rows):
    for q in range(src.shape[1] // QUAD):
        dst[(*at_index, slice(at, at + rows))] = src[pl.ds(row, rows), q * QUAD : (q + 1) * QUAD].astype(BF16)
        at += rows
    return at


def put_ff_grads(target, halves, pos, idx, acc_e, acc_r, wr, acc_m=None):
    hm = D // len(pos) // halves
    hr = wr.shape[0] // len(pos) // halves
    for c in range(wr.shape[0] // D):
        wr[c * D : c * D + D] = acc_r[:, c * D : c * D + D].T.astype(BF16)
    for p, rel in enumerate(pos):
        block = jnp.bitwise_xor(idx[0], rel)
        for c in range(halves):
            side = 0 if halves == 1 else c + 1
            dst, where = target(c, p)
            row, rowr = place(block, hm, side, idx[1]), place(block, hr, side, idx[1])
            at = put_rows(dst, where, 0, acc_e, row, hm)
            at = put_rows(dst, where, at, wr, rowr, hr)
            if acc_m is not None:
                put_rows(dst, where, at, acc_m, row, hm)


def ff_chunks(n2, glow, out, g2, we, wr, acc_e, acc_r):
    for c in range(we.shape[1] // D):
        cs = slice(c * D, c * D + D)
        ex = mm(n2, we[:, cs])
        phi = 0.5 + 0.5 * lax.erf(ex * 0.7071067811865476)
        act = (ex * phi).astype(BF16)
        gp = phi + ex * (jnp.exp(-0.5 * ex * ex) * 0.3989422804014327)
        out = out + mm(act, wr[cs])
        gact = mm(glow, wr[cs], NT)
        ge = (gp * gact).astype(BF16)
        back = mm(ge, we[:, cs], NT)
        g2 = back if g2 is None else g2 + back
        acc_r[:, cs] += mm(glow, act, TN)
        acc_e[:, cs] += mm(n2, ge, TN)
    return out, g2


def live_rows(cot, lens, rows, step):
    count = cot.shape[0] // rows
    row = lax.broadcasted_iota(jnp.int32, (cot.shape[0], 1), 0)
    live = None
    for i in range(count):
        inside = (row >= i * rows) & (row < i * rows + lens[step * count + i])
        live = inside if live is None else live | inside
    return cot * jnp.where(live, 1.0, 0.0).astype(BF16)


def f2a_kernel(plan, nw, pos, rows, idx, lens, att_ref, tok, cot, norm, *refs):
    w_refs, refs = refs[:nw], refs[nw:]
    hid_out, out_out, g2_out, n2_out, keep, send, wm, we, wr, acc_e, acc_r, sem = refs
    s = pl.program_id(0)

    @pl.when(s == 0)
    def _():
        load_mixer(w_refs, plan, wm, sem.at[0], idx[0], idx[1], True)
        load_ff(w_refs, plan, True, we, wr, sem.at[1], idx[0], idx[1], True)
        acc_e[...] = jnp.zeros_like(acc_e)
        acc_r[...] = jnp.zeros_like(acc_r)
        load_mixer(w_refs, plan, wm, sem.at[0], idx[0], idx[1], False)

    glow = live_rows(cot[...], lens, rows, s)
    hidden = tok[...].astype(F32) + mm(att_ref[...], wm[...])
    xhat, _ = ln_parts(hidden)
    n2 = (xhat * norm[2:3] + norm[3:4]).astype(BF16)
    hid_out[...] = hidden
    n2_out[...] = n2

    @pl.when(s == 0)
    def _():
        load_ff(w_refs, plan, True, we, wr, sem.at[1], idx[0], idx[1], False)

    out, g2 = ff_chunks(n2, glow, hidden, None, we, wr, acc_e, acc_r)
    out_out[...] = out
    g2_out[...] = g2

    @pl.when(s == pl.num_programs(0) - 1)
    def _():
        half = len(pos) // 2
        target = lambda c, p: (keep if p < half else send, (c, p % half))
        put_ff_grads(target, keep.shape[0], pos, idx, acc_e, acc_r, wr)


def f2b_kernel(plan, nw, pos, nh, rows, idx, lens, att_ref, hid, out_ref, g2_ref, n2_ref, cot, norm, *refs):
    w_refs, b_refs, refs = refs[:nw], refs[nw : 2 * nw], refs[2 * nw :]
    (block_out, gh_out, ga_out), grads, refs = refs[:3], refs[3 : 3 + nh], refs[3 + nh :]
    ln_out, wm, we, wr, acc_e, acc_r, acc_m, sem = refs
    s = pl.program_id(0)

    @pl.when(s == 0)
    def _():
        load_ff(b_refs, plan, False, we, wr, sem.at[1], idx[0], idx[1], True)
        load_mixer(w_refs, plan, wm, sem.at[0], idx[0], idx[1], True)
        acc_e[...] = jnp.zeros_like(acc_e)
        acc_r[...] = jnp.zeros_like(acc_r)
        acc_m[...] = jnp.zeros_like(acc_m)
        ln_out[...] = jnp.zeros_like(ln_out)
        load_ff(b_refs, plan, False, we, wr, sem.at[1], idx[0], idx[1], False)

    gain = norm[2:3]
    glow = live_rows(cot[...], lens, rows, s)
    out, g2 = ff_chunks(n2_ref[...], glow, out_ref[...], g2_ref[...], we, wr, acc_e, acc_r)
    block_out[...] = out.astype(BF16)
    xhat, rstd = ln_parts(hid[...])
    gh = glow.astype(F32) + ln_back(g2, xhat, rstd, gain)
    ln_out[0:1] += jnp.sum(g2 * xhat, axis=0, keepdims=True)
    ln_out[1:2] += jnp.sum(g2, axis=0, keepdims=True)

    @pl.when(s == 0)
    def _():
        load_mixer(w_refs, plan, wm, sem.at[0], idx[0], idx[1], False)

    gb = gh.astype(BF16)
    gh_out[...] = gh
    acc_m[...] += mm(att_ref[...], gb, TN)
    ga_out[...] = mm(gb, wm[...], NT).astype(BF16)

    @pl.when(s == pl.num_programs(0) - 1)
    def _():
        put_ff_grads(lambda c, p: (grads[c], (p,)), nh, pos, idx, acc_e, acc_r, wr, acc_m)


def b1_kernel(pos, nh, idx, lens, tri_ref, ga_ref, lse, n1, gtri_out, *refs):
    grads, (tri, ga, gtri, dk, dv, acc, n1p, gtp) = refs[:nh], refs[nh:]
    e = pl.program_id(0)
    last = pl.num_programs(0) - 1
    rows = n1.shape[1]
    padded = tri.shape[0]
    rows16 = -(-rows // 16) * 16
    low16 = rows // 16 * 16

    @pl.when(e == 0)
    def _():
        acc[...] = jnp.zeros_like(acc)
        tri[low16:padded] = jnp.zeros((padded - low16, 3 * D), BF16)
        ga[low16:padded] = jnp.zeros((padded - low16, D), BF16)

    tri[0:rows] = tri_ref[0]
    ga[0:rows] = ga_ref[0]
    dk[...] = jnp.zeros_like(dk)
    dv[...] = jnp.zeros_like(dv)
    gtri[:, 0:D] = jnp.zeros((padded, D), BF16)

    length = lens[e]
    masks = head_masks()
    lane = lax.broadcasted_iota(jnp.int32, (1, QUAD), 1) % QB
    blocks = -(-rows // QB)
    for group in [tuple(range(j, min(j + 2, blocks))) for j in range(0, blocks, 2)]:

        @pl.when(length > QB * group[0])
        def _(group=group):
            chains = [(j, g * QUAD, g * blocks + j) for j in group for g in range(HEADS // 4)]
            exts = [min(QB * (j + 1), rows16) for j, _, _ in chains]
            q4 = [stack_heads(tri[QB * j : QB * (j + 1), gl : gl + QUAD], masks) for j, gl, _ in chains]
            do4 = [stack_heads(ga[QB * j : QB * (j + 1), gl : gl + QUAD], masks) for j, gl, _ in chains]
            s = [mm(tri[0:x, D + gl : D + gl + QUAD], q, NT) for (_, gl, _), x, q in zip(chains, exts, q4)]
            dp = [mm(tri[0:x, 2 * D + gl : 2 * D + gl + QUAD], d, NT) for (_, gl, _), x, d in zip(chains, exts, do4)]
            p = []
            for (j, _, at), x, v in zip(chains, exts, s):
                kmax = jnp.minimum(lane + QB * j, length - 1)
                krow = lax.broadcasted_iota(jnp.int32, (x, QUAD), 0)
                p.append(jnp.exp(jnp.where(krow <= kmax, v - lse[0, pl.ds(at, 1), :], MASKED)))
            ds = []
            for v, w in zip(p, dp):
                delta = jnp.sum(v * w, axis=0, keepdims=True)
                ds.append((v * (w - delta)).astype(BF16))
            for (_, gl, _), x, v, d in zip(chains, exts, p, do4):
                dv[0:x, gl : gl + QUAD] += mm(v.astype(BF16), d)
            dq = [mm(v, tri[0:x, D + gl : D + gl + QUAD], TN) for (_, gl, _), x, v in zip(chains, exts, ds)]
            for (_, gl, _), x, v, q in zip(chains, exts, ds, q4):
                dk[0:x, gl : gl + QUAD] += mm(v, q)
            for (j, gl, _), v in zip(chains, dq):
                gtri[QB * j : QB * (j + 1), gl : gl + QUAD] = (own_lanes(v) * HEAD_DIM**-0.5).astype(BF16)

    gtri[0:rows16, D : 2 * D] = dk[...].astype(BF16)
    gtri[0:rows16, 2 * D :] = dv[...].astype(BF16)
    gtri_out[0] = gtri[0:rows]
    start = jnp.int32(0)
    for i in range(lens.shape[0] - 1):
        start = start + jnp.where(i < e, (lens[i] + 15) // 16, 0)
    at = pl.multiple_of(start * 16, 16)
    n1p[pl.ds(at, rows16)] = pad_rows(n1[0], rows16)
    gtp[pl.ds(at, rows16)] = gtri[0:rows16]

    @pl.when(e == last)
    def _():
        end = pl.multiple_of(at + rows16, 16)
        n1p[pl.ds(end, PACK)] = jnp.zeros((PACK, D), BF16)
        gtp[pl.ds(end, PACK)] = jnp.zeros((PACK, 3 * D), BF16)

        def chunk(i, carry):
            row = pl.multiple_of(i * PACK, PACK)
            acc[...] += mm(n1p[pl.ds(row, PACK)], gtp[pl.ds(row, PACK)], TN)
            return carry

        lax.fori_loop(0, (at + length + PACK - 1) // PACK, chunk, 0)
        hm = D // len(pos) // nh
        for p, rel in enumerate(pos):
            block = jnp.bitwise_xor(idx[0], rel)
            for c in range(nh):
                side = 0 if nh == 1 else c + 1
                put_rows(grads[c], (p,), 0, acc, place(block, hm, side, idx[1]), hm)


def b2_kernel(plan, nw, first, idx, gtri, tok, gh, norm, *refs):
    w_refs, refs = refs[:nw], refs[nw:]
    if first:
        ig_out, ln_out, wt, sem = refs
    else:
        _, ln1_a, ln2, q_sum, q_top, ig_out, ln_out, wt, sem = refs
    s = pl.program_id(0)

    @pl.when(s == 0)
    def _():
        load_triple(w_refs, plan, wt, sem, idx[0], idx[1], True)
        ln_out[...] = jnp.zeros_like(ln_out)
        load_triple(w_refs, plan, wt, sem, idx[0], idx[1], False)

    g1 = mm(gtri[...], wt[...], NT)
    xhat, rstd = ln_parts(tok[...].astype(F32))
    ig_out[...] = (gh[...] + ln_back(g1, xhat, rstd, norm[0:1])).astype(BF16)
    ln_out[0:1] += jnp.sum(g1 * xhat, axis=0, keepdims=True)
    ln_out[1:2] += jnp.sum(g1, axis=0, keepdims=True)

    if not first:

        @pl.when(s == pl.num_programs(0) - 1)
        def _():
            ln_out[0:2] += ln1_a[0:2]
            ln_out[2:4] = ln2[0:2]
            ln_out[4:5, 0:16] = jnp.sum(q_sum[...].T, axis=0, keepdims=True)
            ln_out[5:6, 0:16] = jnp.max(q_top[...].T, axis=0, keepdims=True)


def q_kernel(total_rows, bo, vh, bins, cnt, sum_out, top_out):
    s = pl.program_id(0)
    block = bo.shape[0]

    @pl.when(s == 0)
    def _():
        sum_out[...] = jnp.zeros_like(sum_out)
        top_out[...] = jnp.full_like(top_out, MASKED)

    place = lax.broadcasted_iota(jnp.int32, (1, block), 1) + s * block
    counted = (cnt[...] > 0) & (place < total_rows)
    binrow = lax.broadcasted_iota(jnp.int32, (NBINS, block), 0)
    for a in range(ACT):
        sc = mm(vh[a * NBINS : (a + 1) * NBINS], bo[...], NT)
        picked = jnp.sum(jnp.where(binrow == bins[a : a + 1], sc, 0.0), axis=0, keepdims=True)
        sum_out[a : a + 1] += jnp.where(counted, picked, 0.0)
        top_out[a : a + 1] = jnp.maximum(top_out[a : a + 1], jnp.where(counted, picked, MASKED))
    sum_out[ACT : ACT + 1] += jnp.where(counted, 1.0, 0.0)


def lamb_moments(weight, gradient, moment_one, moment_two):
    first_new = BETA_FIRST * moment_one + (1.0 - BETA_FIRST) * gradient
    second_new = BETA_SECOND * moment_two + (1.0 - BETA_SECOND) * gradient * gradient
    update = (
        first_new
        * (1.0 / (1.0 - BETA_FIRST**STEP))
        / (jnp.sqrt(second_new * (1.0 / (1.0 - BETA_SECOND**STEP))) + ADAM_EPSILON)
        + WEIGHT_DECAY * weight
    )
    return (first_new, second_new, update)


class Squares:
    def __init__(self):
        self.total = jnp.zeros((8, 128), F32)

    def add(self, lane, weight, update):
        rows = lax.broadcasted_iota(jnp.int32, (8, 128), 0)
        lanes = lax.broadcasted_iota(jnp.int32, (8, 128), 1)
        for row, v in ((6, weight), (7, update)):
            one = jnp.sum(jnp.sum(v * v, axis=0, keepdims=True), axis=1, keepdims=True)
            self.total = self.total + jnp.where((rows == row) & (lanes == lane), one, 0.0)


def lamb_piece(state, outs, grad, rows, cols, squares, lane):
    weight = state[0][rows, cols]
    first_new, second_new, update = lamb_moments(weight, grad, state[1][rows, cols], state[2][rows, cols])
    for out, v in zip(outs, (first_new, second_new, update)):
        out[rows, cols] = v
    squares.add(lane, weight, update)


def core_halves(idx, parts):
    if len(parts) == 1:
        return [lambda rows: parts[0][rows]]
    own = idx[1] == 0
    return [
        lambda rows: jnp.where(own, parts[0][rows], parts[1][rows]),
        lambda rows: jnp.where(own, parts[1][rows], parts[0][rows]),
    ]


def lamb_mlp_kernel(n_f, nh, rows_a, idx, *refs):
    parts, refs = refs[:nh], refs[nh:]
    states = [refs[3 * i : 3 * i + 3] for i in range(3)]
    outs = [refs[9 + 3 * i : 12 + 3 * i] for i in range(3)]
    sq_out = refs[18]
    hm = D // n_f // nh
    h2 = FF // n_f // 2
    hr = h2 // nh
    ne, nd = FF // 2 // QUAD, D // QUAD
    squares = Squares()
    for c, take in enumerate(core_halves(idx, parts)):
        rows = slice(c * hm, c * hm + hm)
        for q in range(nd):
            at = 2 * rows_a + hm * q
            grad = take(slice(at, at + hm))
            lamb_piece(states[0], outs[0], grad, rows, slice(q * QUAD, (q + 1) * QUAD), squares, 1)
        for h in range(2):
            for q in range(ne):
                at = rows_a * h + hm * q
                grad = take(slice(at, at + hm))
                for k in range(QUAD // h2):
                    i = q * (QUAD // h2) + k
                    col = (2 * i + h) * h2
                    lamb_piece(
                        states[1], outs[1], grad[:, k * h2 : (k + 1) * h2], rows,
                        slice(col, col + h2), squares, 2,
                    )
            for q in range(nd):
                at = rows_a * h + hm * ne + hr * q
                grad = take(slice(at, at + hr))
                row = h * h2 + c * hr
                lamb_piece(
                    states[2], outs[2], grad, slice(row, row + hr),
                    slice(q * QUAD, (q + 1) * QUAD), squares, 3,
                )
    sq_out[...] = squares.total


def lamb_triple_kernel(n_f, nh, idx, *refs):
    parts, refs = refs[:nh], refs[nh:]
    sq_in, state, outs, sq_out = refs[0], refs[1:4], refs[4:7], refs[7]
    hm = D // n_f // nh
    squares = Squares()
    for c, take in enumerate(core_halves(idx, parts)):
        for q in range(3 * D // QUAD):
            lamb_piece(
                state, outs, take(slice(hm * q, hm * q + hm)), slice(c * hm, c * hm + hm),
                slice(q * QUAD, (q + 1) * QUAD), squares, 0,
            )
    sq_out[...] = squares.total + sq_in[...]


def merge_small(mine, other):
    row = lax.broadcasted_iota(jnp.int32, mine.shape, 0)
    return jnp.where(row == 5, jnp.maximum(mine, other), mine + other)


def final_kernel(one, two, norms, firsts, seconds, *refs):
    masters, updates, news = refs[:4], refs[4:8], refs[8:12]
    norms_out, first_out, second_out, table_out, mean_out, peak_out = refs[12:]
    small = merge_small(one[...], two[...])
    roots = jnp.sqrt(small[6:8, 0:128])
    for i in range(4):
        ratio = roots[0:1, i : i + 1] / (roots[1:2, i : i + 1] + RATIO_EPSILON)
        news[i][...] = masters[i][...] - LEARNING_RATE * ratio * updates[i][...]
    weight = norms[...]
    first_new, second_new, update = lamb_moments(weight, small[0:4], firsts[...], seconds[...])
    weight_norm = jnp.sqrt(jnp.sum(weight * weight, axis=1, keepdims=True))
    update_norm = jnp.sqrt(jnp.sum(update * update, axis=1, keepdims=True))
    norms_out[...] = weight - LEARNING_RATE * (weight_norm / (update_norm + RATIO_EPSILON)) * update
    first_out[...] = first_new
    second_out[...] = second_new
    row = lax.broadcasted_iota(jnp.int32, (4, 128), 0)
    lane = lax.broadcasted_iota(jnp.int32, (4, 128), 1)
    low = lax.broadcasted_iota(jnp.int32, (1, 128), 1) < 4
    for k, v in enumerate((weight_norm, update_norm)):
        spread = jnp.sum(jnp.where(lane == row + 4, v, 0.0), axis=0, keepdims=True)
        table_out[k : k + 1] = jnp.where(low, roots[k : k + 1], spread)[:, 0:8]
    sums = small[4:5, 0:128]
    mean_out[...] = (sums / jnp.maximum(sums[:, ACT : ACT + 1], 1.0))[:, 0:ACT]
    peak_out[...] = small[5:6, 0:ACT]


def xor_step(v, axis, size, bit):
    return lax.ppermute(v, axis, [(i, i ^ bit) for i in range(size)])


def axis_bits(size):
    bits = []
    b = 1
    while b < size:
        bits.append(b)
        b *= 2
    return bits


def sync(*vs):
    return lax.optimization_barrier(vs)


def halving_positions(order):
    rels = [0]
    for b in reversed(order):
        rels = rels + [r ^ b for r in rels]
    return rels


def add_low(a, b):
    return (a.astype(F32) + b.astype(F32)).astype(BF16)


def const_spec(shape):
    return pl.BlockSpec(shape, lambda *a: (0,) * len(shape))


SMEM = pl.BlockSpec(memory_space=pltpu.SMEM)
ANY = pl.BlockSpec(memory_space=pl.ANY)


def kernel_call(kernel, name, grid, in_specs, out, scratch, us, args, **more):
    return pl.pallas_call(
        kernel,
        grid=grid,
        in_specs=in_specs,
        out_specs=[spec for spec, _ in out],
        out_shape=[shape for _, shape in out],
        scratch_shapes=scratch,
        compiler_params=pltpu.CompilerParams(
            dimension_semantics=("arbitrary",) * len(grid), vmem_limit_bytes=VMEM_LIMIT
        ),
        cost_estimate=pl.CostEstimate(
            flops=us, bytes_accessed=us, transcendentals=0
        ),
        name=name,
        **more,
    )(*args)


def body(n_d, n_f, *args):
    (
        tokens, cotangent, lengths, valid_mask, action_bins, value_head,
        w_triple, w_mixer, w_expand, w_reduce, norm_params,
        first_triple, first_mixer, first_expand, first_reduce, first_norms,
        second_triple, second_mixer, second_expand, second_reduce, second_norms,
    ) = args
    ep, rows, _ = tokens.shape
    flat = ep * rows
    rows16 = -(-rows // 16) * 16
    padded = -(-rows // QB) * QB
    blocks = padded // QB
    me = lax.axis_index("fsdp")
    dp = lax.axis_index("dp")
    core = dp % 2
    idx = jnp.stack([me, core]).astype(jnp.int32)
    shard = D // n_f
    h2 = FF // n_f // 2
    half_ff = FF // 2
    nh = 2 if shard >= 32 else 1
    f_bits, d_bits = axis_bits(n_f), axis_bits(n_d)
    steps_f = lambda v, b: xor_step(v, "fsdp", n_f, b)
    steps_d = lambda v, b: xor_step(v, "dp", n_d, b)

    def own_half(w):
        n = w.shape[0] // nh
        return lax.dynamic_slice_in_dim(w, core * n, n, 0) if nh == 2 else w

    def ff_half(w, h):
        return jnp.concatenate([w[:, (2 * i + h) * h2 : (2 * i + h + 1) * h2] for i in range(n_f)], axis=1)

    def under(w):
        return [w[:, q * D : (q + 1) * D] for q in range(w.shape[1] // D)]

    own_t = own_half(w_triple).astype(BF16)

    def own_piece(expand, reduce, h, first):
        rows_h = slice(h * h2, (h + 1) * h2)
        return jnp.concatenate(
            first + under(ff_half(own_half(expand), h).astype(BF16)) + [own_half(reduce[rows_h]).astype(BF16)],
            axis=0,
        )

    norm_t = norm_params.T
    norm = jnp.concatenate([norm_t, jnp.zeros((4, D), F32)], axis=0)
    ep_block = lambda width: pl.BlockSpec((1, rows, width), lambda e: (e, 0, 0))
    ep_shape = lambda width, dtype: jax.ShapeDtypeStruct((ep, rows, width), dtype)
    low = lambda width: (ep_block(width), ep_shape(width, BF16))
    wide = lambda width: (ep_block(width), ep_shape(width, F32))
    whole = lambda shape: (const_spec(shape), jax.ShapeDtypeStruct(shape, F32))
    norm_spec = const_spec((8, D))
    lse_spec = pl.BlockSpec((1, 16, QUAD), lambda e: (e, 0, 0))
    dma = pltpu.SemaphoreType.DMA
    wt_scratch = pltpu.VMEM((D, 3 * D), BF16)

    near = f_bits[0]
    rels_a = [0]
    for b in f_bits[1:]:
        rels_a = rels_a + [r ^ b for r in rels_a]
    rels_b = [r ^ near for r in rels_a]
    own_t, w_mixer_0, w_expand_0, w_reduce_0 = sync(own_t, w_mixer, w_expand, w_reduce)
    t_got = [steps_f(own_t, r) for r in rels_a[1:]]
    own_a = own_piece(w_expand_0, w_reduce_0, 0, [own_half(w_mixer_0).astype(BF16)])
    t_one = jnp.stack([own_t, *t_got])
    a_got = [steps_f(own_a, r) for r in rels_a[1:]]
    t_one, idx, norm, valid_mask, action_bins, w_expand_1, w_reduce_1 = sync(
        t_one, idx, norm, valid_mask, action_bins, w_expand, w_reduce
    )
    t_two = steps_f(t_one, near)
    t_refs, t_plan = [t_one], [(rels_a, nh - 1)]
    if nh == 2:
        t_refs.append(steps_d(t_one, 1))
        t_plan.append((rels_a, 2))
    a_one = [own_a, *a_got]
    own_b = own_piece(w_expand_1, w_reduce_1, 1, [])
    t_two, own_b = sync(t_two, own_b)
    b_one = [own_b] + [steps_f(own_b, r) for r in rels_a[1:]]
    t_refs.append(t_two)
    t_plan.append((rels_b, nh - 1))
    if nh == 2:
        t_refs.append(steps_d(t_two, 1))
        t_plan.append((rels_b, 2))
    nw = len(t_refs)
    places = jnp.arange(rows)
    inside = places[None, :] < lengths[:, None]
    counted = ((valid_mask == 1) & inside).astype(jnp.int32).reshape(1, flat)
    bins_t = action_bins.reshape(flat, ACT).T
    a_one = jnp.stack(a_one)
    bins_t, counted, norm, a_one, *t_refs = sync(bins_t, counted, norm, a_one, *t_refs)
    a_two = steps_f(a_one, near)
    a_refs, a_plan = [a_one], [(rels_a, nh - 1)]
    if nh == 2:
        a_refs.append(steps_d(a_one, 1))
        a_plan.append((rels_a, 2))
    triple, n1, attended, lse = kernel_call(
        functools.partial(f1_kernel, t_plan, nw), "f1", (ep,),
        [SMEM, SMEM, ep_block(D), norm_spec] + [ANY] * nw,
        [low(3 * D), low(D), low(D), (lse_spec, jax.ShapeDtypeStruct((ep, 16, QUAD), F32))],
        [wt_scratch, pltpu.VMEM((padded, 3 * D), BF16), dma], 18,
        (idx, lengths, tokens, norm, *t_refs),
    )
    attended, a_two, *b_one = sync(attended, a_two, *b_one)
    a_refs.append(a_two)
    a_plan.append((rels_b, nh - 1))
    if nh == 2:
        a_refs.append(steps_d(a_two, 1))
        a_plan.append((rels_b, 2))
    na = len(a_refs)
    b_one = jnp.stack(b_one)
    attended, b_one, *a_refs = sync(attended, b_one, *a_refs)
    b_two = steps_f(b_one, near)
    b_refs = [b_one] + ([steps_d(b_one, 1)] if nh == 2 else [])

    order = f_bits[1:2] + f_bits[:1] + f_bits[2:]
    late = order[2:]
    order_a = f_bits[1:3] + f_bits[:1] + f_bits[3:]
    pos, pos_a = halving_positions(order), halving_positions(order_a)
    hm, hr = shard // nh, h2 // nh
    rows_a = hm * (half_ff // QUAD) + hr * (D // QUAD)
    rows_b = rows_a + hm * (D // QUAD)
    rows_t = 6 * hm
    half = n_f // 2
    low_out = lambda *shape: (const_spec(shape), jax.ShapeDtypeStruct(shape, BF16))
    ff_scratch = [
        pltpu.VMEM((D, D), BF16), pltpu.VMEM((D, half_ff), BF16), pltpu.VMEM((half_ff, D), BF16),
        pltpu.VMEM((D, half_ff), F32), pltpu.VMEM((D, half_ff), F32),
    ]
    fl = flat // 3 if flat % 48 == 0 else rows
    fl_steps = flat // fl
    fl_block = lambda width, at=0: pl.BlockSpec((fl, width), lambda i: (i + at, 0))
    fl_low = lambda width: (fl_block(width), jax.ShapeDtypeStruct((flat, width), BF16))
    fl_wide = lambda width: (fl_block(width), jax.ShapeDtypeStruct((flat, width), F32))
    tok_flat = tokens.reshape(flat, D)
    cot_flat = cotangent.reshape(flat, D)
    attended = attended.reshape(flat, D)
    hidden, out_part, g2_part, n2, keep_a, send_a = kernel_call(
        functools.partial(f2a_kernel, a_plan, na, pos_a, rows), "f2a", (fl_steps,),
        [SMEM, SMEM] + [fl_block(D)] * 3 + [norm_spec] + [ANY] * na,
        [fl_wide(D)] * 3 + [fl_low(D)] + [low_out(nh, half, rows_a, QUAD)] * 2,
        ff_scratch + [pltpu.SemaphoreType.DMA((2,))], 22, (idx, lengths, attended, tok_flat, cot_flat, norm, *a_refs),
    )

    def halves(keep, got):
        n = keep.shape[-3] // 2
        return add_low(keep[..., :n, :, :], got[..., :n, :, :]), add_low(keep[..., n:, :, :], got[..., n:, :, :])

    def core_pair(total):
        return (total[0], steps_d(total[1], 1)) if nh == 2 else (total[0], None)

    def core_halves_of(pair):
        mine, other = pair
        n = mine.shape[0] // 2
        return halves(mine, other) if other is not None else (mine[:n], mine[n:])

    def core_add(pair):
        return add_low(*pair) if pair[1] is not None else pair[0]

    n2, keep_a, send_a, b_two, *b_refs = sync(n2, keep_a, send_a, b_two, *b_refs)
    b_refs += [b_two] + ([steps_d(b_two, 1)] if nh == 2 else [])
    n2, keep_a, send_a, *b_refs = sync(n2, keep_a, send_a, *b_refs)
    got_a = steps_f(send_a, order[0])
    block_out, gh, ga, *rest = kernel_call(
        functools.partial(f2b_kernel, a_plan, na, pos, nh, rows), "f2b", (fl_steps,),
        [SMEM, SMEM] + [fl_block(D)] * 6 + [norm_spec] + [ANY] * (2 * na),
        [fl_low(D), fl_wide(D), fl_low(D)] + [low_out(n_f, rows_b, QUAD)] * nh + [whole((8, D))],
        ff_scratch + [pltpu.VMEM((D, D), F32), pltpu.SemaphoreType.DMA((2,))], 24,
        (idx, lengths, attended, hidden, out_part, g2_part, n2, cot_flat, norm, *a_refs, *b_refs),
    )
    grads_b, ln2 = rest[:nh], rest[nh]
    ga, keep_a, got_a, *grads_b = sync(ga, keep_a, got_a, *grads_b)
    pair_b = core_pair(grads_b)
    sum_a = add_low(keep_a, got_a)
    pair_a = core_pair(sum_a)
    keep_b, send_b = core_halves_of(pair_b)
    keep_a, send_a = core_halves_of(pair_a)
    ga, keep_a, send_a, keep_b, send_b = sync(ga, keep_a, send_a, keep_b, send_b)

    got_b = steps_f(send_b, order[0])
    got_a = steps_f(send_a, order_a[1])
    pack_rows = ep * rows16 + PACK
    gtri, *grads_t = kernel_call(
        functools.partial(b1_kernel, pos, nh), "b1", (ep,),
        [SMEM, SMEM, ep_block(3 * D), ep_block(D), lse_spec, ep_block(D)],
        [low(3 * D)] + [low_out(n_f, rows_t, QUAD)] * nh,
        [
            pltpu.VMEM((padded, 3 * D), BF16), pltpu.VMEM((padded, D), BF16),
            pltpu.VMEM((padded, 3 * D), BF16), pltpu.VMEM((rows16, D), F32),
            pltpu.VMEM((rows16, D), F32), pltpu.VMEM((D, 3 * D), F32),
            pltpu.VMEM((pack_rows, D), BF16), pltpu.VMEM((pack_rows, 3 * D), BF16),
        ],
        25, (idx, lengths, triple, ga.reshape(ep, rows, D), lse, n1),
    )
    gtri, keep_a, got_a, keep_b, got_b, *grads_t = sync(gtri, keep_a, got_a, keep_b, got_b, *grads_t)

    mine_t, other_t = core_pair(grads_t)
    late_a = order_a[2:]
    keep_b, send_b = halves(keep_b, got_b)
    if late_a:
        keep_a, send_a = halves(keep_a, got_a)
        send_ab = jnp.concatenate([send_a.reshape(-1, QUAD), send_b.reshape(-1, QUAD)], axis=0)
        keep_ab = jnp.concatenate([keep_a.reshape(-1, QUAD), keep_b.reshape(-1, QUAD)], axis=0)
        cut_a = send_a.size // QUAD
    else:
        keep_a = add_low(keep_a, got_a)
        send_ab, keep_ab = send_b.reshape(-1, QUAD), keep_b.reshape(-1, QUAD)
        cut_a = 0
    mine_t, other_t, keep_ab, send_ab = sync(mine_t, other_t, keep_ab, send_ab)
    keep_t, send_t = core_halves_of((mine_t, other_t))
    block_out, keep_t, send_t, keep_ab, send_ab = sync(block_out, keep_t, send_t, keep_ab, send_ab)
    got_t = steps_f(send_t, order[0])
    got_ab = steps_f(send_ab, near)

    qb = 256
    steps = -(-flat // qb)
    q_sum, q_top = kernel_call(
        functools.partial(q_kernel, flat), "qstat", (steps,),
        [
            pl.BlockSpec((qb, D), lambda i: (i, 0)), const_spec((ACT * NBINS, D)),
            pl.BlockSpec((ACT, qb), lambda i: (0, i)), pl.BlockSpec((1, qb), lambda i: (0, i)),
        ],
        [whole((16, qb))] * 2, [], 10, (block_out, value_head, bins_t, counted),
    )
    gtri, q_sum, keep_t, got_t, keep_ab, got_ab = sync(gtri, q_sum, keep_t, got_t, keep_ab, got_ab)

    def b2_call(at, n, gtri, prior, more_in):
        extra = [] if prior is None else [prior, *more_in]
        specs = [] if prior is None else [ANY] + [const_spec(v.shape) for v in more_in]
        more = {} if prior is None else {"input_output_aliases": {5 + nw: 0}}
        return kernel_call(
            functools.partial(b2_kernel, t_plan, nw, prior is None), "b2", (n,),
            [SMEM, fl_block(3 * D, at), fl_block(D, at), fl_block(D, at), norm_spec] + [ANY] * nw + specs,
            [(fl_block(D, at), jax.ShapeDtypeStruct((flat, D), BF16)), whole((8, D))],
            [wt_scratch, dma], 6, (idx, gtri, tok_flat, gh, norm, *t_refs, *extra), **more,
        )

    keep_t, send_t = halves(keep_t, got_t)
    if late_a:
        keep_a = add_low(keep_ab[:cut_a], got_ab[:cut_a]).reshape(-1, rows_a, QUAD)
    keep_b, got_b = (v[cut_a:].reshape(-1, rows_b, QUAD) for v in (keep_ab, got_ab))
    if late:
        keep_b, send_b = halves(keep_b, got_b)
    else:
        keep_b, send_b = add_low(keep_b, got_b), keep_b
    gtri_flat = gtri.reshape(flat, 3 * D)
    gtri_flat, keep_t, send_t, keep_a, keep_b, send_b = sync(gtri_flat, keep_t, send_t, keep_a, keep_b, send_b)
    got_t = steps_f(send_t, order[1])
    if late:
        got_b = steps_f(send_b, late[0])
    cut = (fl_steps + 1) // 2
    ig_part, ln1_a = b2_call(0, cut, gtri_flat, None, ())
    ig_part, keep_t, got_t, keep_b, *got_b = sync(ig_part, keep_t, got_t, keep_b, *([got_b] if late else []))

    def finish(keep, bits):
        for b in bits:
            n = keep.shape[0] // 2
            keep = add_low(keep[:n], steps_f(keep[n:], b))
        return keep[0]

    x_bits = d_bits[nh - 1 :]
    if late:
        keep_t, send_t = halves(keep_t, got_t)
        keep_b = add_low(keep_b, got_b[0])
    else:
        keep_t = add_low(keep_t, got_t)
    red = jnp.concatenate([finish(keep_a, late_a[1:]), finish(keep_b, late[1:])], axis=0)
    for b in x_bits[:-1]:
        red = add_low(red, steps_d(red, b))
    red, keep_t, ig_part = sync(red, keep_t, ig_part)
    if late:
        got_t = steps_f(send_t, late[0])
    got_red = steps_d(red, x_bits[-1])
    input_grad, small = b2_call(cut, fl_steps - cut, gtri_flat, ig_part, (ln1_a, ln2, q_sum, q_top))
    small, red, got_red, keep_t, *got_t = sync(small, red, got_red, keep_t, *([got_t] if late else []))

    red_t = finish(add_low(keep_t, got_t[0]) if late else keep_t, late[1:])
    for b in x_bits[:-1]:
        red_t = add_low(red_t, steps_d(red_t, b))
    got_rt = steps_d(red_t, x_bits[-1])
    red = red.astype(F32) + got_red.astype(F32)
    red_parts = [red] + ([steps_d(red, 1)] if nh == 2 else [])
    small_core = steps_d(small, d_bits[0])
    red_t, *red_parts = sync(red_t, *red_parts)
    like = lambda w: whole(w.shape)
    full = lambda *ws: [const_spec(w.shape) for w in ws]
    mlp_state = (
        w_mixer, first_mixer, second_mixer, w_expand, first_expand, second_expand,
        w_reduce, first_reduce, second_reduce,
    )
    *mlp_out, sq_mlp = kernel_call(
        functools.partial(lamb_mlp_kernel, n_f, nh, rows_a), "lamb_mlp", (1,),
        [SMEM] + full(*red_parts, *mlp_state),
        [like(w) for w in (w_mixer, w_expand, w_reduce) for _ in range(3)] + [whole((8, 128))],
        [], 4, (idx, *red_parts, *mlp_state),
    )
    small, small_core, sq_mlp, red_t, got_rt = sync(small, small_core, sq_mlp, red_t, got_rt)
    small = merge_small(small, small_core)
    for b in d_bits[1:]:
        small = merge_small(small, steps_d(small, b))
    red_t = red_t.astype(F32) + got_rt.astype(F32)
    parts_t = [red_t] + ([steps_d(red_t, 1)] if nh == 2 else [])
    tri_state = (w_triple, first_triple, second_triple)
    *tri_out, squares = kernel_call(
        functools.partial(lamb_triple_kernel, n_f, nh), "lamb_triple", (1,),
        [SMEM] + full(*parts_t, sq_mlp, *tri_state),
        [like(w_triple)] * 3 + [whole((8, 128))],
        [], 2, (idx, *parts_t, sq_mlp, *tri_state),
    )

    small = small + jnp.pad(squares, ((0, 0), (0, D - 128)))
    for b in f_bits[:-1]:
        small = merge_small(small, steps_f(small, b))
    small_two = steps_f(small, f_bits[-1])
    masters = (w_triple, w_mixer, w_expand, w_reduce)
    updates = (tri_out[2], mlp_out[2], mlp_out[5], mlp_out[8])
    firsts_t, seconds_t = first_norms.T, second_norms.T
    *news, norms_out, first_out, second_out, norm_table, mean, peak = kernel_call(
        final_kernel, "final", (1,),
        full(small, small_two, norm_t, firsts_t, seconds_t, *masters, *updates),
        [like(w) for w in masters]
        + [whole((4, D))] * 3 + [whole((2, 8)), whole((1, ACT)), whole((1, ACT))],
        [], 3, (small, small_two, norm_t, firsts_t, seconds_t, *masters, *updates),
    )
    return (
        block_out.reshape(ep, rows, D), input_grad.reshape(ep, rows, D), *news,
        tri_out[0], mlp_out[0], mlp_out[3], mlp_out[6],
        tri_out[1], mlp_out[1], mlp_out[4], mlp_out[7],
        norms_out.T, first_out.T, second_out.T, norm_table, mean.reshape(ACT), peak.reshape(ACT),
    )


def solution(mesh):
    n_d, n_f = mesh.shape["dp"], mesh.shape["fsdp"]
    both = ("dp", "fsdp")
    row, rep = P("fsdp", None), P()
    in_specs = (
        P(both, None, None), P(both, None, None), P(both), P(both, None), P(both, None, None), rep,
        row, row, row, row, rep,
        row, row, row, row, rep,
        row, row, row, row, rep,
    )
    out_specs = (
        (P(both, None, None),) * 2 + (row,) * 12 + (rep,) * 6
    )
    return jax.shard_map(
        functools.partial(body, n_d, n_f), mesh=mesh, in_specs=in_specs, out_specs=out_specs,
        check_vma=False,
    )
```

```python
import functools

import jax
import jax.numpy as jnp
from jax import lax
from jax.experimental import pallas as pl
from jax.experimental.pallas import tpu as pltpu
from jax.sharding import PartitionSpec as P

HEADS = 8
HEAD_DIM = 64
ACT = 11
NBINS = 256
STEP = 5

NORM_EPSILON = 1e-05
BETA_FIRST = 0.9
BETA_SECOND = 0.999
ADAM_EPSILON = 1e-06
RATIO_EPSILON = 1e-06
WEIGHT_DECAY = 0.01
LEARNING_RATE = 0.5
MASKED = -1e30

D = 512
FF = 2048
QB = 64
PACK = 256
QUAD = 256
F32 = jnp.float32
BF16 = jnp.bfloat16
MIB = 1024 * 1024

NT = (((1,), (1,)), ((), ()))
NN = (((1,), (0,)), ((), ()))
TN = (((0,), (0,)), ((), ()))


def mm(a, b, dims=NN):
    return lax.dot_general(a, b, dims, preferred_element_type=F32)


def pad_rows(v, rows):
    if v.shape[0] == rows:
        return v
    return jnp.concatenate([v, jnp.zeros((rows - v.shape[0], v.shape[1]), v.dtype)], axis=0)


def ln_parts(x):
    center = x - jnp.mean(x, axis=-1, keepdims=True)
    spread = jnp.mean(center * center, axis=-1, keepdims=True)
    rstd = lax.rsqrt(spread + NORM_EPSILON)
    return center * rstd, rstd


def ln_back(grad, xhat, rstd, gain):
    t = grad * gain
    m1 = jnp.mean(t, axis=-1, keepdims=True)
    m2 = jnp.mean(t * xhat, axis=-1, keepdims=True)
    return rstd * (t - m1 - xhat * m2)


def head_masks():
    lane = lax.broadcasted_iota(jnp.int32, (1, QUAD), 1)
    return [jnp.where(lane // HEAD_DIM == h, 1.0, 0.0).astype(BF16) for h in range(4)]


def stack_heads(block, masks):
    return jnp.concatenate([block * m for m in masks], axis=0)


def own_lanes(t):
    head = lax.broadcasted_iota(jnp.int32, (QB, QUAD), 1) // HEAD_DIM
    out = t[0:QB]
    for h in range(1, 4):
        out = jnp.where(head == h, t[QB * h : QB * (h + 1)], out)
    return out


def place(block, size, side, core):
    if side == 0:
        return pl.multiple_of(block * size, size)
    c = core if side == 1 else 1 - core
    return pl.multiple_of(block * (2 * size) + c * size, size)


def run_copies(copies, start):
    for copy in copies:
        copy.start() if start else copy.wait()


def load_triple(refs, plan, dst, sem, me, core, start):
    for ref, (rels, side) in zip(refs, plan):
        half = ref.shape[1]
        for p, rel in enumerate(rels):
            row = place(jnp.bitwise_xor(me, rel), half, side, core)
            run_copies([pltpu.make_async_copy(ref.at[p], dst.at[pl.ds(row, half)], sem)], start)


def load_mixer(refs, plan, wm, sem, me, core, start):
    for ref, (rels, side) in zip(refs, plan):
        hm = D // wm_blocks(plan) // (1 if side == 0 else 2)
        for p, rel in enumerate(rels):
            row = place(jnp.bitwise_xor(me, rel), hm, side, core)
            run_copies([pltpu.make_async_copy(ref.at[p, pl.ds(0, hm)], wm.at[pl.ds(row, hm)], sem)], start)


def wm_blocks(plan):
    return sum(len(rels) for rels, side in plan if side != 2)


def load_ff(refs, plan, at_mixer, we, wr, sem, me, core, start):
    for ref, (rels, side) in zip(refs, plan):
        halves = 1 if side == 0 else 2
        hm = D // wm_blocks(plan) // halves
        hr = wr.shape[0] // wm_blocks(plan) // halves
        nc = we.shape[1] // D
        at = hm if at_mixer else 0
        for p, rel in enumerate(rels):
            block = jnp.bitwise_xor(me, rel)
            row, rowr = place(block, hm, side, core), place(block, hr, side, core)
            copies = []
            for q in range(nc):
                copies.append(
                    pltpu.make_async_copy(
                        ref.at[p, pl.ds(at + hm * q, hm)],
                        we.at[pl.ds(row, hm), pl.ds(q * D, D)],
                        sem,
                    )
                )
            copies.append(
                pltpu.make_async_copy(ref.at[p, pl.ds(at + hm * nc, hr)], wr.at[pl.ds(rowr, hr)], sem)
            )
            run_copies(copies, start)


def f1_kernel(plan, nw, idx, lens, tok, norm, *refs):
    w_refs, (tri_out, n1_out, att_out, lse_out, wt, tri, sem) = refs[:nw], refs[nw:]
    e = pl.program_id(0)
    rows = tok.shape[1]
    padded = tri.shape[0]
    rows16 = -(-rows // 16) * 16

    @pl.when(e == 0)
    def _():
        load_triple(w_refs, plan, wt, sem, idx[0], idx[1], True)
        tri[rows16:padded] = jnp.zeros((padded - rows16, 3 * D), BF16)
        load_triple(w_refs, plan, wt, sem, idx[0], idx[1], False)

    xhat, _ = ln_parts(pad_rows(tok[0].astype(F32), rows16))
    n1 = (xhat * norm[0:1] + norm[1:2]).astype(BF16)
    n1_out[0] = n1[:rows]
    t = mm(n1, wt[...]).astype(BF16)
    tri[0:rows16, 0:D] = t[:, 0:D] * jnp.asarray(HEAD_DIM**-0.5, BF16)
    tri[0:rows16, D:] = t[:, D:]
    tri_out[0] = tri[0:rows]

    length = lens[e]
    masks = head_masks()
    lane = lax.broadcasted_iota(jnp.int32, (1, QUAD), 1) % QB
    blocks = -(-rows // QB)
    chains = [(j, g * QUAD, g * blocks + j) for j in range(blocks) for g in range(HEADS // 4)]
    exts = [min(QB * (j + 1), rows16) for j, _, _ in chains]
    q4 = [stack_heads(tri[QB * j : QB * (j + 1), gl : gl + QUAD], masks) for j, gl, _ in chains]
    s = [mm(tri[0:x, D + gl : D + gl + QUAD], q, NT) for (_, gl, _), x, q in zip(chains, exts, q4)]
    pb = []
    for (j, _, at), x, v in zip(chains, exts, s):
        kmax = jnp.minimum(lane + QB * j, length - 1)
        krow = lax.broadcasted_iota(jnp.int32, (x, QUAD), 0)
        v = jnp.where(krow <= kmax, v, MASKED)
        m = jnp.max(v, axis=0, keepdims=True)
        p = jnp.exp(v - m)
        total = jnp.sum(p, axis=0, keepdims=True)
        lse_out[0, pl.ds(at, 1), :] = m + jnp.log(total)
        pb.append((p * (1.0 / total)).astype(BF16))
    o = [mm(v, tri[0:x, 2 * D + gl : 2 * D + gl + QUAD], TN) for (_, gl, _), x, v in zip(chains, exts, pb)]
    for (j, gl, _), v in zip(chains, o):
        live = min(QB, rows - QB * j)
        att_out[0, QB * j : QB * j + live, gl : gl + QUAD] = own_lanes(v).astype(BF16)[:live]


def put_rows(dst, at_index, at, src, row, rows):
    for q in range(src.shape[1] // QUAD):
        dst[(*at_index, slice(at, at + rows))] = src[pl.ds(row, rows), q * QUAD : (q + 1) * QUAD].astype(BF16)
        at += rows
    return at


def put_ff_grads(target, halves, pos, idx, acc_e, acc_r, wr, acc_m=None):
    hm = D // len(pos) // halves
    hr = wr.shape[0] // len(pos) // halves
    for c in range(wr.shape[0] // D):
        wr[c * D : c * D + D] = acc_r[:, c * D : c * D + D].T.astype(BF16)
    for p, rel in enumerate(pos):
        block = jnp.bitwise_xor(idx[0], rel)
        for c in range(halves):
            side = 0 if halves == 1 else c + 1
            dst, where = target(c, p)
            row, rowr = place(block, hm, side, idx[1]), place(block, hr, side, idx[1])
            at = put_rows(dst, where, 0, acc_e, row, hm)
            at = put_rows(dst, where, at, wr, rowr, hr)
            if acc_m is not None:
                put_rows(dst, where, at, acc_m, row, hm)


def ff_chunks(n2, glow, out, g2, we, wr, acc_e, acc_r):
    for c in range(we.shape[1] // D):
        cs = slice(c * D, c * D + D)
        ex = mm(n2, we[:, cs])
        phi = 0.5 + 0.5 * lax.erf(ex * 0.7071067811865476)
        act = (ex * phi).astype(BF16)
        gp = phi + ex * (jnp.exp(-0.5 * ex * ex) * 0.3989422804014327)
        out = out + mm(act, wr[cs])
        gact = mm(glow, wr[cs], NT)
        ge = (gp * gact).astype(BF16)
        back = mm(ge, we[:, cs], NT)
        g2 = back if g2 is None else g2 + back
        acc_r[:, cs] += mm(glow, act, TN)
        acc_e[:, cs] += mm(n2, ge, TN)
    return out, g2


def live_rows(cot, lens, rows, step):
    count = cot.shape[0] // rows
    row = lax.broadcasted_iota(jnp.int32, (cot.shape[0], 1), 0)
    live = None
    for i in range(count):
        inside = (row >= i * rows) & (row < i * rows + lens[step * count + i])
        live = inside if live is None else live | inside
    return cot * jnp.where(live, 1.0, 0.0).astype(BF16)


def f2a_kernel(plan, nw, pos, rows, idx, lens, att_ref, tok, cot, norm, *refs):
    w_refs, refs = refs[:nw], refs[nw:]
    hid_out, out_out, g2_out, n2_out, keep, send, wm, we, wr, acc_e, acc_r, sem = refs
    s = pl.program_id(0)

    @pl.when(s == 0)
    def _():
        load_mixer(w_refs, plan, wm, sem.at[0], idx[0], idx[1], True)
        load_ff(w_refs, plan, True, we, wr, sem.at[1], idx[0], idx[1], True)
        acc_e[...] = jnp.zeros_like(acc_e)
        acc_r[...] = jnp.zeros_like(acc_r)
        load_mixer(w_refs, plan, wm, sem.at[0], idx[0], idx[1], False)

    glow = live_rows(cot[...], lens, rows, s)
    hidden = tok[...].astype(F32) + mm(att_ref[...], wm[...])
    xhat, _ = ln_parts(hidden)
    n2 = (xhat * norm[2:3] + norm[3:4]).astype(BF16)
    hid_out[...] = hidden
    n2_out[...] = n2

    @pl.when(s == 0)
    def _():
        load_ff(w_refs, plan, True, we, wr, sem.at[1], idx[0], idx[1], False)

    out, g2 = ff_chunks(n2, glow, hidden, None, we, wr, acc_e, acc_r)
    out_out[...] = out
    g2_out[...] = g2

    @pl.when(s == pl.num_programs(0) - 1)
    def _():
        half = len(pos) // 2
        target = lambda c, p: (keep if p < half else send, (c, p % half))
        put_ff_grads(target, keep.shape[0], pos, idx, acc_e, acc_r, wr)


def f2b_kernel(plan, nw, pos, nh, rows, idx, lens, att_ref, hid, out_ref, g2_ref, n2_ref, cot, norm, *refs):
    w_refs, b_refs, refs = refs[:nw], refs[nw : 2 * nw], refs[2 * nw :]
    (block_out, gh_out, ga_out), grads, refs = refs[:3], refs[3 : 3 + nh], refs[3 + nh :]
    ln_out, wm, we, wr, acc_e, acc_r, acc_m, sem = refs
    s = pl.program_id(0)

    @pl.when(s == 0)
    def _():
        load_ff(b_refs, plan, False, we, wr, sem.at[1], idx[0], idx[1], True)
        load_mixer(w_refs, plan, wm, sem.at[0], idx[0], idx[1], True)
        acc_e[...] = jnp.zeros_like(acc_e)
        acc_r[...] = jnp.zeros_like(acc_r)
        acc_m[...] = jnp.zeros_like(acc_m)
        ln_out[...] = jnp.zeros_like(ln_out)
        load_ff(b_refs, plan, False, we, wr, sem.at[1], idx[0], idx[1], False)

    gain = norm[2:3]
    glow = live_rows(cot[...], lens, rows, s)
    out, g2 = ff_chunks(n2_ref[...], glow, out_ref[...], g2_ref[...], we, wr, acc_e, acc_r)
    block_out[...] = out.astype(BF16)
    xhat, rstd = ln_parts(hid[...])
    gh = glow.astype(F32) + ln_back(g2, xhat, rstd, gain)
    ln_out[0:1] += jnp.sum(g2 * xhat, axis=0, keepdims=True)
    ln_out[1:2] += jnp.sum(g2, axis=0, keepdims=True)

    @pl.when(s == 0)
    def _():
        load_mixer(w_refs, plan, wm, sem.at[0], idx[0], idx[1], False)

    gb = gh.astype(BF16)
    gh_out[...] = gh
    acc_m[...] += mm(att_ref[...], gb, TN)
    ga_out[...] = mm(gb, wm[...], NT).astype(BF16)

    @pl.when(s == pl.num_programs(0) - 1)
    def _():
        put_ff_grads(lambda c, p: (grads[c], (p,)), nh, pos, idx, acc_e, acc_r, wr, acc_m)


def b1_kernel(pos, nh, idx, lens, tri_ref, ga_ref, lse, n1, gtri_out, *refs):
    grads, (tri, ga, gtri, dk, dv, acc, n1p, gtp) = refs[:nh], refs[nh:]
    e = pl.program_id(0)
    last = pl.num_programs(0) - 1
    rows = n1.shape[1]
    padded = tri.shape[0]
    rows16 = -(-rows // 16) * 16
    low16 = rows // 16 * 16

    @pl.when(e == 0)
    def _():
        acc[...] = jnp.zeros_like(acc)
        tri[low16:padded] = jnp.zeros((padded - low16, 3 * D), BF16)
        ga[low16:padded] = jnp.zeros((padded - low16, D), BF16)

    tri[0:rows] = tri_ref[0]
    ga[0:rows] = ga_ref[0]
    dk[...] = jnp.zeros_like(dk)
    dv[...] = jnp.zeros_like(dv)
    gtri[:, 0:D] = jnp.zeros((padded, D), BF16)

    length = lens[e]
    masks = head_masks()
    lane = lax.broadcasted_iota(jnp.int32, (1, QUAD), 1) % QB
    blocks = -(-rows // QB)
    for group in [tuple(range(j, min(j + 2, blocks))) for j in range(0, blocks, 2)]:

        @pl.when(length > QB * group[0])
        def _(group=group):
            chains = [(j, g * QUAD, g * blocks + j) for j in group for g in range(HEADS // 4)]
            exts = [min(QB * (j + 1), rows16) for j, _, _ in chains]
            q4 = [stack_heads(tri[QB * j : QB * (j + 1), gl : gl + QUAD], masks) for j, gl, _ in chains]
            do4 = [stack_heads(ga[QB * j : QB * (j + 1), gl : gl + QUAD], masks) for j, gl, _ in chains]
            s = [mm(tri[0:x, D + gl : D + gl + QUAD], q, NT) for (_, gl, _), x, q in zip(chains, exts, q4)]
            dp = [mm(tri[0:x, 2 * D + gl : 2 * D + gl + QUAD], d, NT) for (_, gl, _), x, d in zip(chains, exts, do4)]
            p = []
            for (j, _, at), x, v in zip(chains, exts, s):
                kmax = jnp.minimum(lane + QB * j, length - 1)
                krow = lax.broadcasted_iota(jnp.int32, (x, QUAD), 0)
                p.append(jnp.exp(jnp.where(krow <= kmax, v - lse[0, pl.ds(at, 1), :], MASKED)))
            ds = []
            for v, w in zip(p, dp):
                delta = jnp.sum(v * w, axis=0, keepdims=True)
                ds.append((v * (w - delta)).astype(BF16))
            for (_, gl, _), x, v, d in zip(chains, exts, p, do4):
                dv[0:x, gl : gl + QUAD] += mm(v.astype(BF16), d)
            dq = [mm(v, tri[0:x, D + gl : D + gl + QUAD], TN) for (_, gl, _), x, v in zip(chains, exts, ds)]
            for (_, gl, _), x, v, q in zip(chains, exts, ds, q4):
                dk[0:x, gl : gl + QUAD] += mm(v, q)
            for (j, gl, _), v in zip(chains, dq):
                gtri[QB * j : QB * (j + 1), gl : gl + QUAD] = (own_lanes(v) * HEAD_DIM**-0.5).astype(BF16)

    gtri[0:rows16, D : 2 * D] = dk[...].astype(BF16)
    gtri[0:rows16, 2 * D :] = dv[...].astype(BF16)
    gtri_out[0] = gtri[0:rows]
    start = jnp.int32(0)
    for i in range(lens.shape[0] - 1):
        start = start + jnp.where(i < e, (lens[i] + 15) // 16, 0)
    at = pl.multiple_of(start * 16, 16)
    n1p[pl.ds(at, rows16)] = pad_rows(n1[0], rows16)
    gtp[pl.ds(at, rows16)] = gtri[0:rows16]

    @pl.when(e == last)
    def _():
        end = pl.multiple_of(at + rows16, 16)
        n1p[pl.ds(end, PACK)] = jnp.zeros((PACK, D), BF16)
        gtp[pl.ds(end, PACK)] = jnp.zeros((PACK, 3 * D), BF16)

        def chunk(i, carry):
            row = pl.multiple_of(i * PACK, PACK)
            acc[...] += mm(n1p[pl.ds(row, PACK)], gtp[pl.ds(row, PACK)], TN)
            return carry

        lax.fori_loop(0, (at + length + PACK - 1) // PACK, chunk, 0)
        hm = D // len(pos) // nh
        for p, rel in enumerate(pos):
            block = jnp.bitwise_xor(idx[0], rel)
            for c in range(nh):
                side = 0 if nh == 1 else c + 1
                put_rows(grads[c], (p,), 0, acc, place(block, hm, side, idx[1]), hm)


def b2_kernel(plan, nw, first, idx, gtri, tok, gh, norm, *refs):
    w_refs, refs = refs[:nw], refs[nw:]
    if first:
        ig_out, ln_out, wt, sem = refs
    else:
        _, ln1_a, ln2, q_sum, q_top, ig_out, ln_out, wt, sem = refs
    s = pl.program_id(0)

    @pl.when(s == 0)
    def _():
        load_triple(w_refs, plan, wt, sem, idx[0], idx[1], True)
        ln_out[...] = jnp.zeros_like(ln_out)
        load_triple(w_refs, plan, wt, sem, idx[0], idx[1], False)

    g1 = mm(gtri[...], wt[...], NT)
    xhat, rstd = ln_parts(tok[...].astype(F32))
    ig_out[...] = (gh[...] + ln_back(g1, xhat, rstd, norm[0:1])).astype(BF16)
    ln_out[0:1] += jnp.sum(g1 * xhat, axis=0, keepdims=True)
    ln_out[1:2] += jnp.sum(g1, axis=0, keepdims=True)

    if not first:

        @pl.when(s == pl.num_programs(0) - 1)
        def _():
            ln_out[0:2] += ln1_a[0:2]
            ln_out[2:4] = ln2[0:2]
            ln_out[4:5, 0:16] = jnp.sum(q_sum[...].T, axis=0, keepdims=True)
            ln_out[5:6, 0:16] = jnp.max(q_top[...].T, axis=0, keepdims=True)


def q_kernel(total_rows, bo, vh, bins, cnt, sum_out, top_out):
    s = pl.program_id(0)
    block = bo.shape[0]

    @pl.when(s == 0)
    def _():
        sum_out[...] = jnp.zeros_like(sum_out)
        top_out[...] = jnp.full_like(top_out, MASKED)

    place = lax.broadcasted_iota(jnp.int32, (1, block), 1) + s * block
    counted = (cnt[...] > 0) & (place < total_rows)
    binrow = lax.broadcasted_iota(jnp.int32, (NBINS, block), 0)
    for a in range(ACT):
        sc = mm(vh[a * NBINS : (a + 1) * NBINS], bo[...], NT)
        picked = jnp.sum(jnp.where(binrow == bins[a : a + 1], sc, 0.0), axis=0, keepdims=True)
        sum_out[a : a + 1] += jnp.where(counted, picked, 0.0)
        top_out[a : a + 1] = jnp.maximum(top_out[a : a + 1], jnp.where(counted, picked, MASKED))
    sum_out[ACT : ACT + 1] += jnp.where(counted, 1.0, 0.0)


def lamb_moments(weight, gradient, moment_one, moment_two):
    first_new = BETA_FIRST * moment_one + (1.0 - BETA_FIRST) * gradient
    second_new = BETA_SECOND * moment_two + (1.0 - BETA_SECOND) * gradient * gradient
    update = (
        first_new
        * (1.0 / (1.0 - BETA_FIRST**STEP))
        / (jnp.sqrt(second_new * (1.0 / (1.0 - BETA_SECOND**STEP))) + ADAM_EPSILON)
        + WEIGHT_DECAY * weight
    )
    return (first_new, second_new, update)


class Squares:
    def __init__(self):
        self.total = jnp.zeros((8, 128), F32)

    def add(self, lane, weight, update):
        rows = lax.broadcasted_iota(jnp.int32, (8, 128), 0)
        lanes = lax.broadcasted_iota(jnp.int32, (8, 128), 1)
        for row, v in ((6, weight), (7, update)):
            one = jnp.sum(jnp.sum(v * v, axis=0, keepdims=True), axis=1, keepdims=True)
            self.total = self.total + jnp.where((rows == row) & (lanes == lane), one, 0.0)


def lamb_piece(state, outs, grad, rows, cols, squares, lane):
    weight = state[0][rows, cols]
    first_new, second_new, update = lamb_moments(weight, grad, state[1][rows, cols], state[2][rows, cols])
    for out, v in zip(outs, (first_new, second_new, update)):
        out[rows, cols] = v
    squares.add(lane, weight, update)


def core_halves(idx, parts):
    if len(parts) == 1:
        return [lambda rows: parts[0][rows]]
    own = idx[1] == 0
    return [
        lambda rows: jnp.where(own, parts[0][rows], parts[1][rows]),
        lambda rows: jnp.where(own, parts[1][rows], parts[0][rows]),
    ]


def lamb_mlp_kernel(n_f, nh, rows_a, idx, *refs):
    parts, refs = refs[:nh], refs[nh:]
    states = [refs[3 * i : 3 * i + 3] for i in range(3)]
    outs = [refs[9 + 3 * i : 12 + 3 * i] for i in range(3)]
    sq_out = refs[18]
    hm = D // n_f // nh
    h2 = FF // n_f // 2
    hr = h2 // nh
    ne, nd = FF // 2 // QUAD, D // QUAD
    squares = Squares()
    for c, take in enumerate(core_halves(idx, parts)):
        rows = slice(c * hm, c * hm + hm)
        for q in range(nd):
            at = 2 * rows_a + hm * q
            grad = take(slice(at, at + hm))
            lamb_piece(states[0], outs[0], grad, rows, slice(q * QUAD, (q + 1) * QUAD), squares, 1)
        for h in range(2):
            for q in range(ne):
                at = rows_a * h + hm * q
                grad = take(slice(at, at + hm))
                for k in range(QUAD // h2):
                    i = q * (QUAD // h2) + k
                    col = (2 * i + h) * h2
                    lamb_piece(
                        states[1], outs[1], grad[:, k * h2 : (k + 1) * h2], rows,
                        slice(col, col + h2), squares, 2,
                    )
            for q in range(nd):
                at = rows_a * h + hm * ne + hr * q
                grad = take(slice(at, at + hr))
                row = h * h2 + c * hr
                lamb_piece(
                    states[2], outs[2], grad, slice(row, row + hr),
                    slice(q * QUAD, (q + 1) * QUAD), squares, 3,
                )
    sq_out[...] = squares.total


def lamb_triple_kernel(n_f, nh, idx, *refs):
    parts, refs = refs[:nh], refs[nh:]
    sq_in, state, outs, sq_out = refs[0], refs[1:4], refs[4:7], refs[7]
    hm = D // n_f // nh
    squares = Squares()
    for c, take in enumerate(core_halves(idx, parts)):
        for q in range(3 * D // QUAD):
            lamb_piece(
                state, outs, take(slice(hm * q, hm * q + hm)), slice(c * hm, c * hm + hm),
                slice(q * QUAD, (q + 1) * QUAD), squares, 0,
            )
    sq_out[...] = squares.total + sq_in[...]


def merge_small(mine, other):
    row = lax.broadcasted_iota(jnp.int32, mine.shape, 0)
    return jnp.where(row == 5, jnp.maximum(mine, other), mine + other)


def final_kernel(one, two, norms, firsts, seconds, *refs):
    masters, updates, news = refs[:4], refs[4:8], refs[8:12]
    norms_out, first_out, second_out, table_out, mean_out, peak_out = refs[12:]
    small = merge_small(one[...], two[...])
    roots = jnp.sqrt(small[6:8, 0:128])
    for i in range(4):
        ratio = roots[0:1, i : i + 1] / (roots[1:2, i : i + 1] + RATIO_EPSILON)
        news[i][...] = masters[i][...] - LEARNING_RATE * ratio * updates[i][...]
    weight = norms[...]
    first_new, second_new, update = lamb_moments(weight, small[0:4], firsts[...], seconds[...])
    weight_norm = jnp.sqrt(jnp.sum(weight * weight, axis=1, keepdims=True))
    update_norm = jnp.sqrt(jnp.sum(update * update, axis=1, keepdims=True))
    norms_out[...] = weight - LEARNING_RATE * (weight_norm / (update_norm + RATIO_EPSILON)) * update
    first_out[...] = first_new
    second_out[...] = second_new
    row = lax.broadcasted_iota(jnp.int32, (4, 128), 0)
    lane = lax.broadcasted_iota(jnp.int32, (4, 128), 1)
    low = lax.broadcasted_iota(jnp.int32, (1, 128), 1) < 4
    for k, v in enumerate((weight_norm, update_norm)):
        spread = jnp.sum(jnp.where(lane == row + 4, v, 0.0), axis=0, keepdims=True)
        table_out[k : k + 1] = jnp.where(low, roots[k : k + 1], spread)[:, 0:8]
    sums = small[4:5, 0:128]
    mean_out[...] = (sums / jnp.maximum(sums[:, ACT : ACT + 1], 1.0))[:, 0:ACT]
    peak_out[...] = small[5:6, 0:ACT]


def xor_step(v, axis, size, bit):
    return lax.ppermute(v, axis, [(i, i ^ bit) for i in range(size)])


def axis_bits(size):
    bits = []
    b = 1
    while b < size:
        bits.append(b)
        b *= 2
    return bits


def sync(*vs):
    return lax.optimization_barrier(vs)


def halving_positions(order):
    rels = [0]
    for b in reversed(order):
        rels = rels + [r ^ b for r in rels]
    return rels


def add_low(a, b):
    return (a.astype(F32) + b.astype(F32)).astype(BF16)


def const_spec(shape):
    return pl.BlockSpec(shape, lambda *a: (0,) * len(shape))


SMEM = pl.BlockSpec(memory_space=pltpu.SMEM)
ANY = pl.BlockSpec(memory_space=pl.ANY)


def kernel_call(kernel, name, grid, in_specs, out, scratch, mib, args, **more):
    return pl.pallas_call(
        kernel,
        grid=grid,
        in_specs=in_specs,
        out_specs=[spec for spec, _ in out],
        out_shape=[shape for _, shape in out],
        scratch_shapes=scratch,
        compiler_params=pltpu.CompilerParams(
            dimension_semantics=("arbitrary",) * len(grid), vmem_limit_bytes=mib * MIB
        ),
        cost_estimate=pl.CostEstimate(flops=1, bytes_accessed=1, transcendentals=0),
        name=name,
        **more,
    )(*args)


def body(n_d, n_f, *args):
    (
        tokens, cotangent, lengths, valid_mask, action_bins, value_head,
        w_triple, w_mixer, w_expand, w_reduce, norm_params,
        first_triple, first_mixer, first_expand, first_reduce, first_norms,
        second_triple, second_mixer, second_expand, second_reduce, second_norms,
    ) = args
    ep, rows, _ = tokens.shape
    flat = ep * rows
    rows16 = -(-rows // 16) * 16
    padded = -(-rows // QB) * QB
    blocks = padded // QB
    me = lax.axis_index("fsdp")
    dp = lax.axis_index("dp")
    core = dp % 2
    idx = jnp.stack([me, core]).astype(jnp.int32)
    shard = D // n_f
    h2 = FF // n_f // 2
    half_ff = FF // 2
    nh = 2 if shard >= 32 else 1
    f_bits, d_bits = axis_bits(n_f), axis_bits(n_d)
    steps_f = lambda v, b: xor_step(v, "fsdp", n_f, b)
    steps_d = lambda v, b: xor_step(v, "dp", n_d, b)

    def own_half(w):
        n = w.shape[0] // nh
        return lax.dynamic_slice_in_dim(w, core * n, n, 0) if nh == 2 else w

    def ff_half(w, h):
        return jnp.concatenate([w[:, (2 * i + h) * h2 : (2 * i + h + 1) * h2] for i in range(n_f)], axis=1)

    def under(w):
        return [w[:, q * D : (q + 1) * D] for q in range(w.shape[1] // D)]

    own_t = own_half(w_triple).astype(BF16)

    def own_piece(expand, reduce, h, first):
        rows_h = slice(h * h2, (h + 1) * h2)
        return jnp.concatenate(
            first + under(ff_half(own_half(expand), h).astype(BF16)) + [own_half(reduce[rows_h]).astype(BF16)],
            axis=0,
        )

    norm_t = norm_params.T
    norm = jnp.concatenate([norm_t, jnp.zeros((4, D), F32)], axis=0)
    ep_block = lambda width: pl.BlockSpec((1, rows, width), lambda e: (e, 0, 0))
    ep_shape = lambda width, dtype: jax.ShapeDtypeStruct((ep, rows, width), dtype)
    low = lambda width: (ep_block(width), ep_shape(width, BF16))
    wide = lambda width: (ep_block(width), ep_shape(width, F32))
    whole = lambda shape: (const_spec(shape), jax.ShapeDtypeStruct(shape, F32))
    norm_spec = const_spec((8, D))
    lse_spec = pl.BlockSpec((1, 16, QUAD), lambda e: (e, 0, 0))
    dma = pltpu.SemaphoreType.DMA
    wt_scratch = pltpu.VMEM((D, 3 * D), BF16)

    near = f_bits[0]
    rels_a = [0]
    for b in f_bits[1:]:
        rels_a = rels_a + [r ^ b for r in rels_a]
    rels_b = [r ^ near for r in rels_a]
    own_t, w_mixer_0, w_expand_0, w_reduce_0 = sync(own_t, w_mixer, w_expand, w_reduce)
    t_got = [steps_f(own_t, r) for r in rels_a[1:]]
    own_a = own_piece(w_expand_0, w_reduce_0, 0, [own_half(w_mixer_0).astype(BF16)])
    own_b = own_piece(w_expand_0, w_reduce_0, 1, [])
    a_near = steps_f(own_a, near)
    t_one = jnp.stack([own_t, *t_got])
    t_one, idx, norm, own_a, own_b, a_near = sync(t_one, idx, norm, own_a, own_b, a_near)
    t_two = steps_f(t_one, near)
    t_refs, t_plan = [t_one], [(rels_a, nh - 1)]
    if nh == 2:
        t_refs.append(steps_d(t_one, 1))
        t_plan.append((rels_a, 2))
    t_two, own_b = sync(t_two, own_b)
    b_near = steps_f(own_b, near)
    a_pair, b_pair = jnp.stack([own_a, a_near]), jnp.stack([own_b, b_near])
    a_got = [steps_f(a_pair, r) for r in rels_a[1:]]
    t_refs.append(t_two)
    t_plan.append((rels_b, nh - 1))
    if nh == 2:
        for i, r in enumerate(rels_b):
            t_refs.append(steps_d(t_two[i : i + 1], 1))
            t_plan.append(([r], 2))
    nw = len(t_refs)
    pair_plan = [([0, near], nh - 1)]
    got_plan = [([r, r ^ near], nh - 1) for r in rels_a[1:]]
    a_refs, a_plan = [a_pair], pair_plan + got_plan
    norm, b_pair, *t_refs = sync(norm, b_pair, *t_refs)
    b_refs, b_got = [b_pair], [steps_f(b_pair, r) for r in rels_a[1:]]
    triple, n1, attended, lse = kernel_call(
        functools.partial(f1_kernel, t_plan, nw), "f1", (ep,),
        [SMEM, SMEM, ep_block(D), norm_spec] + [ANY] * nw,
        [low(3 * D), low(D), low(D), (lse_spec, jax.ShapeDtypeStruct((ep, 16, QUAD), F32))],
        [wt_scratch, pltpu.VMEM((padded, 3 * D), BF16), dma], 60,
        (idx, lengths, tokens, norm, *t_refs),
    )
    attended, *a_got = sync(attended, *a_got)
    a_refs += a_got
    if nh == 2:
        a_refs += [steps_d(v, 1) for v in [a_pair, *a_got]]
        a_plan = a_plan + [(rels, 2) for rels, _ in a_plan]
    na = len(a_refs)
    attended, *a_refs = sync(attended, *a_refs)

    order = f_bits[1:2] + f_bits[:1] + f_bits[2:]
    late = order[2:]
    order_a = f_bits[1:3] + f_bits[:1] + f_bits[3:]
    pos, pos_a = halving_positions(order), halving_positions(order_a)
    hm, hr = shard // nh, h2 // nh
    rows_a = hm * (half_ff // QUAD) + hr * (D // QUAD)
    rows_b = rows_a + hm * (D // QUAD)
    rows_t = 6 * hm
    half = n_f // 2
    low_out = lambda *shape: (const_spec(shape), jax.ShapeDtypeStruct(shape, BF16))
    ff_scratch = [
        pltpu.VMEM((D, D), BF16), pltpu.VMEM((D, half_ff), BF16), pltpu.VMEM((half_ff, D), BF16),
        pltpu.VMEM((D, half_ff), F32), pltpu.VMEM((D, half_ff), F32),
    ]
    fl = flat // 3 if flat % 48 == 0 else rows
    fl_steps = flat // fl
    fl_block = lambda width, at=0: pl.BlockSpec((fl, width), lambda i: (i + at, 0))
    fl_low = lambda width: (fl_block(width), jax.ShapeDtypeStruct((flat, width), BF16))
    fl_wide = lambda width: (fl_block(width), jax.ShapeDtypeStruct((flat, width), F32))
    tok_flat = tokens.reshape(flat, D)
    cot_flat = cotangent.reshape(flat, D)
    attended = attended.reshape(flat, D)
    hidden, out_part, g2_part, n2, keep_a, send_a = kernel_call(
        functools.partial(f2a_kernel, a_plan, na, pos_a, rows), "f2a", (fl_steps,),
        [SMEM, SMEM] + [fl_block(D)] * 3 + [norm_spec] + [ANY] * na,
        [fl_wide(D)] * 3 + [fl_low(D)] + [low_out(nh, half, rows_a, QUAD)] * 2,
        ff_scratch + [pltpu.SemaphoreType.DMA((2,))], 50, (idx, lengths, attended, tok_flat, cot_flat, norm, *a_refs),
    )

    def halves(keep, got):
        n = keep.shape[-3] // 2
        return add_low(keep[..., :n, :, :], got[..., :n, :, :]), add_low(keep[..., n:, :, :], got[..., n:, :, :])

    def core_pair(total):
        return (total[0], steps_d(total[1], 1)) if nh == 2 else (total[0], None)

    def core_halves_of(pair):
        mine, other = pair
        n = mine.shape[0] // 2
        return halves(mine, other) if other is not None else (mine[:n], mine[n:])

    def core_add(pair):
        return add_low(*pair) if pair[1] is not None else pair[0]

    n2, keep_a, send_a, *b_got = sync(n2, keep_a, send_a, *b_got)
    b_refs += b_got
    if nh == 2:
        b_refs += [steps_d(v, 1) for v in [b_pair, *b_got]]
    n2, keep_a, send_a, *b_refs = sync(n2, keep_a, send_a, *b_refs)
    got_a = steps_f(send_a, order[0])
    block_out, gh, ga, *rest = kernel_call(
        functools.partial(f2b_kernel, a_plan, na, pos, nh, rows), "f2b", (fl_steps,),
        [SMEM, SMEM] + [fl_block(D)] * 6 + [norm_spec] + [ANY] * (2 * na),
        [fl_low(D), fl_wide(D), fl_low(D)] + [low_out(n_f, rows_b, QUAD)] * nh + [whole((8, D))],
        ff_scratch + [pltpu.VMEM((D, D), F32), pltpu.SemaphoreType.DMA((2,))], 54,
        (idx, lengths, attended, hidden, out_part, g2_part, n2, cot_flat, norm, *a_refs, *b_refs),
    )
    grads_b, ln2 = rest[:nh], rest[nh]
    ga, valid_mask, action_bins, keep_a, got_a, *grads_b = sync(
        ga, valid_mask, action_bins, keep_a, got_a, *grads_b
    )
    pair_b = core_pair(grads_b)
    places = jnp.arange(rows)
    inside = places[None, :] < lengths[:, None]
    counted = ((valid_mask == 1) & inside).astype(jnp.int32).reshape(1, flat)
    bins_t = action_bins.reshape(flat, ACT).T
    sum_a = add_low(keep_a, got_a)
    pair_a = core_pair(sum_a)
    keep_b, send_b = core_halves_of(pair_b)
    keep_a, send_a = core_halves_of(pair_a)
    ga, counted, bins_t, keep_a, send_a, keep_b, send_b = sync(ga, counted, bins_t, keep_a, send_a, keep_b, send_b)

    got_b = steps_f(send_b, order[0])
    got_a = steps_f(send_a, order_a[1])
    pack_rows = ep * rows16 + PACK
    gtri, *grads_t = kernel_call(
        functools.partial(b1_kernel, pos, nh), "b1", (ep,),
        [SMEM, SMEM, ep_block(3 * D), ep_block(D), lse_spec, ep_block(D)],
        [low(3 * D)] + [low_out(n_f, rows_t, QUAD)] * nh,
        [
            pltpu.VMEM((padded, 3 * D), BF16), pltpu.VMEM((padded, D), BF16),
            pltpu.VMEM((padded, 3 * D), BF16), pltpu.VMEM((rows16, D), F32),
            pltpu.VMEM((rows16, D), F32), pltpu.VMEM((D, 3 * D), F32),
            pltpu.VMEM((pack_rows, D), BF16), pltpu.VMEM((pack_rows, 3 * D), BF16),
        ],
        44, (idx, lengths, triple, ga.reshape(ep, rows, D), lse, n1),
    )
    gtri, keep_a, got_a, keep_b, got_b, *grads_t = sync(gtri, keep_a, got_a, keep_b, got_b, *grads_t)

    mine_t, other_t = core_pair(grads_t)
    late_a = order_a[2:]
    keep_b, send_b = halves(keep_b, got_b)
    if late_a:
        keep_a, send_a = halves(keep_a, got_a)
        send_ab = jnp.concatenate([send_a.reshape(-1, QUAD), send_b.reshape(-1, QUAD)], axis=0)
        keep_ab = jnp.concatenate([keep_a.reshape(-1, QUAD), keep_b.reshape(-1, QUAD)], axis=0)
        cut_a = send_a.size // QUAD
    else:
        keep_a = add_low(keep_a, got_a)
        send_ab, keep_ab = send_b.reshape(-1, QUAD), keep_b.reshape(-1, QUAD)
        cut_a = 0
    mine_t, other_t, keep_ab, send_ab = sync(mine_t, other_t, keep_ab, send_ab)
    keep_t, send_t = core_halves_of((mine_t, other_t))
    block_out, keep_t, send_t, keep_ab, send_ab = sync(block_out, keep_t, send_t, keep_ab, send_ab)
    got_t = steps_f(send_t, order[0])
    got_ab = steps_f(send_ab, near)

    qb = 256
    steps = -(-flat // qb)
    q_sum, q_top = kernel_call(
        functools.partial(q_kernel, flat), "qstat", (steps,),
        [
            pl.BlockSpec((qb, D), lambda i: (i, 0)), const_spec((ACT * NBINS, D)),
            pl.BlockSpec((ACT, qb), lambda i: (0, i)), pl.BlockSpec((1, qb), lambda i: (0, i)),
        ],
        [whole((16, qb))] * 2, [], 20, (block_out, value_head, bins_t, counted),
    )
    gtri, q_sum, keep_t, got_t, keep_ab, got_ab = sync(gtri, q_sum, keep_t, got_t, keep_ab, got_ab)

    def b2_call(at, n, gtri, prior, more_in):
        extra = [] if prior is None else [prior, *more_in]
        specs = [] if prior is None else [ANY] + [const_spec(v.shape) for v in more_in]
        more = {} if prior is None else {"input_output_aliases": {5 + nw: 0}}
        return kernel_call(
            functools.partial(b2_kernel, t_plan, nw, prior is None), "b2", (n,),
            [SMEM, fl_block(3 * D, at), fl_block(D, at), fl_block(D, at), norm_spec] + [ANY] * nw + specs,
            [(fl_block(D, at), jax.ShapeDtypeStruct((flat, D), BF16)), whole((8, D))],
            [wt_scratch, dma], 28, (idx, gtri, tok_flat, gh, norm, *t_refs, *extra), **more,
        )

    keep_t, send_t = halves(keep_t, got_t)
    if late_a:
        keep_a = add_low(keep_ab[:cut_a], got_ab[:cut_a]).reshape(-1, rows_a, QUAD)
    keep_b, got_b = (v[cut_a:].reshape(-1, rows_b, QUAD) for v in (keep_ab, got_ab))
    if late:
        keep_b, send_b = halves(keep_b, got_b)
    else:
        keep_b, send_b = add_low(keep_b, got_b), keep_b
    gtri_flat = gtri.reshape(flat, 3 * D)
    gtri_flat, keep_t, send_t, keep_a, keep_b, send_b = sync(gtri_flat, keep_t, send_t, keep_a, keep_b, send_b)
    got_t = steps_f(send_t, order[1])
    if late:
        got_b = steps_f(send_b, late[0])
    cut = (fl_steps + 1) // 2
    ig_part, ln1_a = b2_call(0, cut, gtri_flat, None, ())
    ig_part, keep_t, got_t, keep_b, *got_b = sync(ig_part, keep_t, got_t, keep_b, *([got_b] if late else []))

    def finish(keep, bits):
        for b in bits:
            n = keep.shape[0] // 2
            keep = add_low(keep[:n], steps_f(keep[n:], b))
        return keep[0]

    x_bits = d_bits[nh - 1 :]
    if late:
        keep_t, send_t = halves(keep_t, got_t)
        keep_b = add_low(keep_b, got_b[0])
    else:
        keep_t = add_low(keep_t, got_t)
    red = jnp.concatenate([finish(keep_a, late_a[1:]), finish(keep_b, late[1:])], axis=0)
    for b in x_bits[:-1]:
        red = add_low(red, steps_d(red, b))
    red, keep_t, ig_part = sync(red, keep_t, ig_part)
    if late:
        got_t = steps_f(send_t, late[0])
    got_red = steps_d(red, x_bits[-1])
    input_grad, small = b2_call(cut, fl_steps - cut, gtri_flat, ig_part, (ln1_a, ln2, q_sum, q_top))
    small, red, got_red, keep_t, *got_t = sync(small, red, got_red, keep_t, *([got_t] if late else []))

    red_t = finish(add_low(keep_t, got_t[0]) if late else keep_t, late[1:])
    for b in x_bits[:-1]:
        red_t = add_low(red_t, steps_d(red_t, b))
    got_rt = steps_d(red_t, x_bits[-1])
    red = red.astype(F32) + got_red.astype(F32)
    red_parts = [red] + ([steps_d(red, 1)] if nh == 2 else [])
    small_core = steps_d(small, d_bits[0])
    red_t, *red_parts = sync(red_t, *red_parts)
    like = lambda w: whole(w.shape)
    full = lambda *ws: [pl.BlockSpec(memory_space=pltpu.VMEM)] * len(ws)
    mlp_state = (
        w_mixer, first_mixer, second_mixer, w_expand, first_expand, second_expand,
        w_reduce, first_reduce, second_reduce,
    )
    *mlp_out, sq_mlp = kernel_call(
        functools.partial(lamb_mlp_kernel, n_f, nh, rows_a), "lamb_mlp", (1,),
        [SMEM] + full(*red_parts, *mlp_state),
        [like(w) for w in (w_mixer, w_expand, w_reduce) for _ in range(3)] + [whole((8, 128))],
        [], 20, (idx, *red_parts, *mlp_state),
    )
    small, small_core, sq_mlp, red_t, got_rt = sync(small, small_core, sq_mlp, red_t, got_rt)
    small = merge_small(small, small_core)
    for b in d_bits[1:]:
        small = merge_small(small, steps_d(small, b))
    red_t = red_t.astype(F32) + got_rt.astype(F32)
    parts_t = [red_t] + ([steps_d(red_t, 1)] if nh == 2 else [])
    tri_state = (w_triple, first_triple, second_triple)
    *tri_out, squares = kernel_call(
        functools.partial(lamb_triple_kernel, n_f, nh), "lamb_triple", (1,),
        [SMEM] + full(*parts_t, sq_mlp, *tri_state),
        [like(w_triple)] * 3 + [whole((8, 128))],
        [], 12, (idx, *parts_t, sq_mlp, *tri_state),
    )

    small = small + jnp.pad(squares, ((0, 0), (0, D - 128)))
    for b in f_bits[:-1]:
        small = merge_small(small, steps_f(small, b))
    small_two = steps_f(small, f_bits[-1])
    masters = (w_triple, w_mixer, w_expand, w_reduce)
    updates = (tri_out[2], mlp_out[2], mlp_out[5], mlp_out[8])
    firsts_t, seconds_t = first_norms.T, second_norms.T
    *news, norms_out, first_out, second_out, norm_table, mean, peak = kernel_call(
        final_kernel, "final", (1,),
        full(small, small_two, norm_t, firsts_t, seconds_t, *masters, *updates),
        [like(w) for w in masters]
        + [whole((4, D))] * 3 + [whole((2, 8)), whole((1, ACT)), whole((1, ACT))],
        [], 16, (small, small_two, norm_t, firsts_t, seconds_t, *masters, *updates),
    )
    return (
        block_out.reshape(ep, rows, D), input_grad.reshape(ep, rows, D), *news,
        tri_out[0], mlp_out[0], mlp_out[3], mlp_out[6],
        tri_out[1], mlp_out[1], mlp_out[4], mlp_out[7],
        norms_out.T, first_out.T, second_out.T, norm_table, mean.reshape(ACT), peak.reshape(ACT),
    )


def solution(mesh):
    n_d, n_f = mesh.shape["dp"], mesh.shape["fsdp"]
    both = ("dp", "fsdp")
    row, rep = P("fsdp", None), P()
    in_specs = (
        P(both, None, None), P(both, None, None), P(both), P(both, None), P(both, None, None), rep,
        row, row, row, row, rep,
        row, row, row, row, rep,
        row, row, row, row, rep,
    )
    out_specs = (
        (P(both, None, None),) * 2 + (row,) * 12 + (rep,) * 6
    )
    return jax.shard_map(
        functools.partial(body, n_d, n_f), mesh=mesh, in_specs=in_specs, out_specs=out_specs,
        check_vma=False,
    )
```

```python
import functools

import jax
import jax.numpy as jnp
from jax import lax
from jax.experimental import pallas as pl
from jax.experimental.pallas import tpu as pltpu
from jax.sharding import PartitionSpec as P

HEADS = 8
HEAD_DIM = 64
ACT = 11
NBINS = 256
STEP = 5

NORM_EPSILON = 1e-05
BETA_FIRST = 0.9
BETA_SECOND = 0.999
ADAM_EPSILON = 1e-06
RATIO_EPSILON = 1e-06
WEIGHT_DECAY = 0.01
LEARNING_RATE = 0.5
MASKED = -1e30

D = 512
FF = 2048
QB = 64
PACK = 256
QUAD = 256
F32 = jnp.float32
BF16 = jnp.bfloat16
MIB = 1024 * 1024

NT = (((1,), (1,)), ((), ()))
NN = (((1,), (0,)), ((), ()))
TN = (((0,), (0,)), ((), ()))


def mm(a, b, dims=NN):
    return lax.dot_general(a, b, dims, preferred_element_type=F32)


def pad_rows(v, rows):
    if v.shape[0] == rows:
        return v
    return jnp.concatenate([v, jnp.zeros((rows - v.shape[0], v.shape[1]), v.dtype)], axis=0)


def ln_parts(x):
    center = x - jnp.mean(x, axis=-1, keepdims=True)
    spread = jnp.mean(center * center, axis=-1, keepdims=True)
    rstd = lax.rsqrt(spread + NORM_EPSILON)
    return center * rstd, rstd


def ln_back(grad, xhat, rstd, gain):
    t = grad * gain
    m1 = jnp.mean(t, axis=-1, keepdims=True)
    m2 = jnp.mean(t * xhat, axis=-1, keepdims=True)
    return rstd * (t - m1 - xhat * m2)


def head_masks():
    lane = lax.broadcasted_iota(jnp.int32, (1, QUAD), 1)
    return [jnp.where(lane // HEAD_DIM == h, 1.0, 0.0).astype(BF16) for h in range(4)]


def stack_heads(block, masks):
    return jnp.concatenate([block * m for m in masks], axis=0)


def own_lanes(t):
    head = lax.broadcasted_iota(jnp.int32, (QB, QUAD), 1) // HEAD_DIM
    out = t[0:QB]
    for h in range(1, 4):
        out = jnp.where(head == h, t[QB * h : QB * (h + 1)], out)
    return out


def place(block, size, side, core):
    if side == 0:
        return pl.multiple_of(block * size, size)
    c = core if side == 1 else 1 - core
    return pl.multiple_of(block * (2 * size) + c * size, size)


def run_copies(copies, start):
    for copy in copies:
        copy.start() if start else copy.wait()


def load_triple(refs, plan, dst, sem, me, core, start):
    for ref, (rels, side) in zip(refs, plan):
        half = ref.shape[1]
        for p, rel in enumerate(rels):
            row = place(jnp.bitwise_xor(me, rel), half, side, core)
            run_copies([pltpu.make_async_copy(ref.at[p], dst.at[pl.ds(row, half)], sem)], start)


def load_mixer(refs, plan, wm, sem, me, core, start):
    for ref, (rels, side) in zip(refs, plan):
        hm = D // wm_blocks(plan) // (1 if side == 0 else 2)
        for p, rel in enumerate(rels):
            row = place(jnp.bitwise_xor(me, rel), hm, side, core)
            run_copies([pltpu.make_async_copy(ref.at[p, pl.ds(0, hm)], wm.at[pl.ds(row, hm)], sem)], start)


def wm_blocks(plan):
    return sum(len(rels) for rels, side in plan if side != 2)


def load_ff(refs, plan, at_mixer, we, wr, sem, me, core, start):
    for ref, (rels, side) in zip(refs, plan):
        halves = 1 if side == 0 else 2
        hm = D // wm_blocks(plan) // halves
        hr = wr.shape[0] // wm_blocks(plan) // halves
        nc = we.shape[1] // D
        at = hm if at_mixer else 0
        for p, rel in enumerate(rels):
            block = jnp.bitwise_xor(me, rel)
            row, rowr = place(block, hm, side, core), place(block, hr, side, core)
            copies = []
            for q in range(nc):
                copies.append(
                    pltpu.make_async_copy(
                        ref.at[p, pl.ds(at + hm * q, hm)],
                        we.at[pl.ds(row, hm), pl.ds(q * D, D)],
                        sem,
                    )
                )
            copies.append(
                pltpu.make_async_copy(ref.at[p, pl.ds(at + hm * nc, hr)], wr.at[pl.ds(rowr, hr)], sem)
            )
            run_copies(copies, start)


def f1_kernel(plan, nw, idx, lens, tok, norm, *refs):
    w_refs, (tri_out, n1_out, att_out, lse_out, wt, tri, sem) = refs[:nw], refs[nw:]
    e = pl.program_id(0)
    count, rows = tok.shape[:2]
    padded = tri.shape[1]
    rows16 = -(-rows // 16) * 16

    @pl.when(e == 0)
    def _():
        load_triple(w_refs, plan, wt, sem, idx[0], idx[1], True)
        tri[:, rows16:padded] = jnp.zeros((count, padded - rows16, 3 * D), BF16)
        load_triple(w_refs, plan, wt, sem, idx[0], idx[1], False)

    for i in range(count):
        xhat, _ = ln_parts(pad_rows(tok[i].astype(F32), rows16))
        n1 = (xhat * norm[0:1] + norm[1:2]).astype(BF16)
        n1_out[i] = n1[:rows]
        t = mm(n1, wt[...]).astype(BF16)
        tri[i, 0:rows16, 0:D] = t[:, 0:D] * jnp.asarray(HEAD_DIM**-0.5, BF16)
        tri[i, 0:rows16, D:] = t[:, D:]
        tri_out[i] = tri[i, 0:rows]

    masks = head_masks()
    lane = lax.broadcasted_iota(jnp.int32, (1, QUAD), 1) % QB
    blocks = -(-rows // QB)
    chains = [
        (i, j, g * QUAD, g * blocks + j)
        for i in range(count) for j in range(blocks) for g in range(HEADS // 4)
    ]
    exts = [min(QB * (j + 1), rows16) for _, j, _, _ in chains]
    q4 = [stack_heads(tri[i, QB * j : QB * (j + 1), gl : gl + QUAD], masks) for i, j, gl, _ in chains]
    s = [mm(tri[i, 0:x, D + gl : D + gl + QUAD], q, NT) for (i, _, gl, _), x, q in zip(chains, exts, q4)]
    pb = []
    for (i, j, _, at), x, v in zip(chains, exts, s):
        kmax = jnp.minimum(lane + QB * j, lens[e * count + i] - 1)
        krow = lax.broadcasted_iota(jnp.int32, (x, QUAD), 0)
        v = jnp.where(krow <= kmax, v, MASKED)
        m = jnp.max(v, axis=0, keepdims=True)
        p = jnp.exp(v - m)
        total = jnp.sum(p, axis=0, keepdims=True)
        lse_out[i, pl.ds(at, 1), :] = m + jnp.log(total)
        pb.append((p * (1.0 / total)).astype(BF16))
    o = [mm(v, tri[i, 0:x, 2 * D + gl : 2 * D + gl + QUAD], TN) for (i, _, gl, _), x, v in zip(chains, exts, pb)]
    for (i, j, gl, _), v in zip(chains, o):
        live = min(QB, rows - QB * j)
        att_out[i, QB * j : QB * j + live, gl : gl + QUAD] = own_lanes(v).astype(BF16)[:live]


def put_rows(dst, at_index, at, src, row, rows):
    for q in range(src.shape[1] // QUAD):
        dst[(*at_index, slice(at, at + rows))] = src[pl.ds(row, rows), q * QUAD : (q + 1) * QUAD].astype(BF16)
        at += rows
    return at


def put_ff_grads(target, halves, pos, idx, acc_e, acc_r, wr, acc_m=None):
    hm = D // len(pos) // halves
    hr = wr.shape[0] // len(pos) // halves
    for c in range(wr.shape[0] // D):
        wr[c * D : c * D + D] = acc_r[:, c * D : c * D + D].T.astype(BF16)
    for p, rel in enumerate(pos):
        block = jnp.bitwise_xor(idx[0], rel)
        for c in range(halves):
            side = 0 if halves == 1 else c + 1
            dst, where = target(c, p)
            row, rowr = place(block, hm, side, idx[1]), place(block, hr, side, idx[1])
            at = put_rows(dst, where, 0, acc_e, row, hm)
            at = put_rows(dst, where, at, wr, rowr, hr)
            if acc_m is not None:
                put_rows(dst, where, at, acc_m, row, hm)


def ff_chunks(n2, glow, out, g2, we, wr, acc_e, acc_r):
    for c in range(we.shape[1] // D):
        cs = slice(c * D, c * D + D)
        ex = mm(n2, we[:, cs])
        phi = 0.5 + 0.5 * lax.erf(ex * 0.7071067811865476)
        act = (ex * phi).astype(BF16)
        gp = phi + ex * (jnp.exp(-0.5 * ex * ex) * 0.3989422804014327)
        out = out + mm(act, wr[cs])
        gact = mm(glow, wr[cs], NT)
        ge = (gp * gact).astype(BF16)
        back = mm(ge, we[:, cs], NT)
        g2 = back if g2 is None else g2 + back
        acc_r[:, cs] += mm(glow, act, TN)
        acc_e[:, cs] += mm(n2, ge, TN)
    return out, g2


def live_rows(cot, lens, rows, step):
    count = cot.shape[0] // rows
    row = lax.broadcasted_iota(jnp.int32, (cot.shape[0], 1), 0)
    live = None
    for i in range(count):
        inside = (row >= i * rows) & (row < i * rows + lens[step * count + i])
        live = inside if live is None else live | inside
    return cot * jnp.where(live, 1.0, 0.0).astype(BF16)


def f2a_kernel(plan, nw, pos, rows, idx, lens, att_ref, tok, cot, norm, *refs):
    w_refs, refs = refs[:nw], refs[nw:]
    hid_out, out_out, g2_out, n2_out, keep, send, wm, we, wr, acc_e, acc_r, sem = refs
    s = pl.program_id(0)

    @pl.when(s == 0)
    def _():
        load_mixer(w_refs, plan, wm, sem.at[0], idx[0], idx[1], True)
        load_ff(w_refs, plan, True, we, wr, sem.at[1], idx[0], idx[1], True)
        acc_e[...] = jnp.zeros_like(acc_e)
        acc_r[...] = jnp.zeros_like(acc_r)
        load_mixer(w_refs, plan, wm, sem.at[0], idx[0], idx[1], False)

    glow = live_rows(cot[...], lens, rows, s)
    hidden = tok[...].astype(F32) + mm(att_ref[...], wm[...])
    xhat, _ = ln_parts(hidden)
    n2 = (xhat * norm[2:3] + norm[3:4]).astype(BF16)
    hid_out[...] = hidden
    n2_out[...] = n2

    @pl.when(s == 0)
    def _():
        load_ff(w_refs, plan, True, we, wr, sem.at[1], idx[0], idx[1], False)

    out, g2 = ff_chunks(n2, glow, hidden, None, we, wr, acc_e, acc_r)
    out_out[...] = out
    g2_out[...] = g2

    @pl.when(s == pl.num_programs(0) - 1)
    def _():
        half = len(pos) // 2
        target = lambda c, p: (keep if p < half else send, (c, p % half))
        put_ff_grads(target, keep.shape[0], pos, idx, acc_e, acc_r, wr)


def f2b_kernel(plan, nw, pos, nh, rows, idx, lens, att_ref, hid, out_ref, g2_ref, n2_ref, cot, norm, *refs):
    w_refs, b_refs, refs = refs[:nw], refs[nw : 2 * nw], refs[2 * nw :]
    (block_out, gh_out, ga_out), grads, refs = refs[:3], refs[3 : 3 + nh], refs[3 + nh :]
    ln_out, wm, we, wr, acc_e, acc_r, acc_m, sem = refs
    s = pl.program_id(0)

    @pl.when(s == 0)
    def _():
        load_ff(b_refs, plan, False, we, wr, sem.at[1], idx[0], idx[1], True)
        load_mixer(w_refs, plan, wm, sem.at[0], idx[0], idx[1], True)
        acc_e[...] = jnp.zeros_like(acc_e)
        acc_r[...] = jnp.zeros_like(acc_r)
        acc_m[...] = jnp.zeros_like(acc_m)
        ln_out[...] = jnp.zeros_like(ln_out)
        load_ff(b_refs, plan, False, we, wr, sem.at[1], idx[0], idx[1], False)

    gain = norm[2:3]
    glow = live_rows(cot[...], lens, rows, s)
    out, g2 = ff_chunks(n2_ref[...], glow, out_ref[...], g2_ref[...], we, wr, acc_e, acc_r)
    block_out[...] = out.astype(BF16)
    xhat, rstd = ln_parts(hid[...])
    gh = glow.astype(F32) + ln_back(g2, xhat, rstd, gain)
    ln_out[0:1] += jnp.sum(g2 * xhat, axis=0, keepdims=True)
    ln_out[1:2] += jnp.sum(g2, axis=0, keepdims=True)

    @pl.when(s == 0)
    def _():
        load_mixer(w_refs, plan, wm, sem.at[0], idx[0], idx[1], False)

    gb = gh.astype(BF16)
    gh_out[...] = gh
    acc_m[...] += mm(att_ref[...], gb, TN)
    ga_out[...] = mm(gb, wm[...], NT).astype(BF16)

    @pl.when(s == pl.num_programs(0) - 1)
    def _():
        put_ff_grads(lambda c, p: (grads[c], (p,)), nh, pos, idx, acc_e, acc_r, wr, acc_m)


def b1_kernel(pos, nh, idx, lens, tri_ref, ga_ref, lse, n1, gtri_out, *refs):
    grads, (tri, ga, gtri, dk, dv, acc, n1p, gtp) = refs[:nh], refs[nh:]
    e = pl.program_id(0)
    last = pl.num_programs(0) - 1
    count, rows = n1.shape[:2]
    padded = tri.shape[1]
    rows16 = -(-rows // 16) * 16
    low16 = rows // 16 * 16

    @pl.when(e == 0)
    def _():
        acc[...] = jnp.zeros_like(acc)
        tri[:, low16:padded] = jnp.zeros((count, padded - low16, 3 * D), BF16)
        ga[:, low16:padded] = jnp.zeros((count, padded - low16, D), BF16)

    for i in range(count):
        tri[i, 0:rows] = tri_ref[i]
        ga[i, 0:rows] = ga_ref[i]
    dk[...] = jnp.zeros_like(dk)
    dv[...] = jnp.zeros_like(dv)
    gtri[:, :, 0:D] = jnp.zeros((count, padded, D), BF16)

    lengths = [lens[e * count + i] for i in range(count)]
    masks = head_masks()
    lane = lax.broadcasted_iota(jnp.int32, (1, QUAD), 1) % QB
    blocks = -(-rows // QB)

    def run(chains):
        chains = [(i, j, g * QUAD, g * blocks + j) for i, j in chains for g in range(HEADS // 4)]
        exts = [min(QB * (j + 1), rows16) for _, j, _, _ in chains]
        q4 = [stack_heads(tri[i, QB * j : QB * (j + 1), gl : gl + QUAD], masks) for i, j, gl, _ in chains]
        do4 = [stack_heads(ga[i, QB * j : QB * (j + 1), gl : gl + QUAD], masks) for i, j, gl, _ in chains]
        s = [mm(tri[i, 0:x, D + gl : D + gl + QUAD], q, NT) for (i, _, gl, _), x, q in zip(chains, exts, q4)]
        dp = [mm(tri[i, 0:x, 2 * D + gl : 2 * D + gl + QUAD], d, NT) for (i, _, gl, _), x, d in zip(chains, exts, do4)]
        p = []
        for (i, j, _, at), x, v in zip(chains, exts, s):
            kmax = jnp.minimum(lane + QB * j, lengths[i] - 1)
            krow = lax.broadcasted_iota(jnp.int32, (x, QUAD), 0)
            p.append(jnp.exp(jnp.where(krow <= kmax, v - lse[i, pl.ds(at, 1), :], MASKED)))
        ds = []
        for v, w in zip(p, dp):
            delta = jnp.sum(v * w, axis=0, keepdims=True)
            ds.append((v * (w - delta)).astype(BF16))
        for (i, _, gl, _), x, v, d in zip(chains, exts, p, do4):
            dv[i, 0:x, gl : gl + QUAD] += mm(v.astype(BF16), d)
        dq = [mm(v, tri[i, 0:x, D + gl : D + gl + QUAD], TN) for (i, _, gl, _), x, v in zip(chains, exts, ds)]
        for (i, _, gl, _), x, v, q in zip(chains, exts, ds, q4):
            dk[i, 0:x, gl : gl + QUAD] += mm(v, q)
        for (i, j, gl, _), v in zip(chains, dq):
            gtri[i, QB * j : QB * (j + 1), gl : gl + QUAD] = (own_lanes(v) * HEAD_DIM**-0.5).astype(BF16)

    run([(i, j) for i in range(count) for j in range(min(2, blocks))])
    for i in range(count):
        for j in range(2, blocks, 2):

            @pl.when(lengths[i] > QB * j)
            def _(i=i, j=j):
                run([(i, k) for k in range(j, min(j + 2, blocks))])

    start = jnp.int32(0)
    for i in range(lens.shape[0] - count):
        start = start + jnp.where(i < e * count, (lens[i] + 15) // 16, 0)
    for i in range(count):
        gtri[i, 0:rows16, D : 2 * D] = dk[i].astype(BF16)
        gtri[i, 0:rows16, 2 * D :] = dv[i].astype(BF16)
        gtri_out[i] = gtri[i, 0:rows]
        at = pl.multiple_of(start * 16, 16)
        n1p[pl.ds(at, rows16)] = pad_rows(n1[i], rows16)
        gtp[pl.ds(at, rows16)] = gtri[i, 0:rows16]
        start = start + (lengths[i] + 15) // 16

    @pl.when(e == last)
    def _():
        end = pl.multiple_of(at + rows16, 16)
        n1p[pl.ds(end, PACK)] = jnp.zeros((PACK, D), BF16)
        gtp[pl.ds(end, PACK)] = jnp.zeros((PACK, 3 * D), BF16)

        def chunk(i, carry):
            row = pl.multiple_of(i * PACK, PACK)
            acc[...] += mm(n1p[pl.ds(row, PACK)], gtp[pl.ds(row, PACK)], TN)
            return carry

        lax.fori_loop(0, (start * 16 + PACK - 1) // PACK, chunk, 0)
        hm = D // len(pos) // nh
        for p, rel in enumerate(pos):
            block = jnp.bitwise_xor(idx[0], rel)
            for c in range(nh):
                side = 0 if nh == 1 else c + 1
                put_rows(grads[c], (p,), 0, acc, place(block, hm, side, idx[1]), hm)


def b2_kernel(plan, nw, first, idx, gtri, tok, gh, norm, *refs):
    w_refs, refs = refs[:nw], refs[nw:]
    if first:
        ig_out, ln_out, wt, sem = refs
    else:
        _, ln1_a, ln2, q_sum, q_top, ig_out, ln_out, wt, sem = refs
    s = pl.program_id(0)

    @pl.when(s == 0)
    def _():
        load_triple(w_refs, plan, wt, sem, idx[0], idx[1], True)
        ln_out[...] = jnp.zeros_like(ln_out)
        load_triple(w_refs, plan, wt, sem, idx[0], idx[1], False)

    g1 = mm(gtri[...], wt[...], NT)
    xhat, rstd = ln_parts(tok[...].astype(F32))
    ig_out[...] = (gh[...] + ln_back(g1, xhat, rstd, norm[0:1])).astype(BF16)
    ln_out[0:1] += jnp.sum(g1 * xhat, axis=0, keepdims=True)
    ln_out[1:2] += jnp.sum(g1, axis=0, keepdims=True)

    if not first:

        @pl.when(s == pl.num_programs(0) - 1)
        def _():
            ln_out[0:2] += ln1_a[0:2]
            ln_out[2:4] = ln2[0:2]
            ln_out[4:5, 0:16] = jnp.sum(q_sum[...].T, axis=0, keepdims=True)
            ln_out[5:6, 0:16] = jnp.max(q_top[...].T, axis=0, keepdims=True)


def q_kernel(total_rows, bo, vh, bins, cnt, sum_out, top_out):
    s = pl.program_id(0)
    block = bo.shape[0]

    @pl.when(s == 0)
    def _():
        sum_out[...] = jnp.zeros_like(sum_out)
        top_out[...] = jnp.full_like(top_out, MASKED)

    place = lax.broadcasted_iota(jnp.int32, (1, block), 1) + s * block
    counted = (cnt[...] > 0) & (place < total_rows)
    binrow = lax.broadcasted_iota(jnp.int32, (NBINS, block), 0)
    for a in range(ACT):
        sc = mm(vh[a * NBINS : (a + 1) * NBINS], bo[...], NT)
        picked = jnp.sum(jnp.where(binrow == bins[a : a + 1], sc, 0.0), axis=0, keepdims=True)
        sum_out[a : a + 1] += jnp.where(counted, picked, 0.0)
        top_out[a : a + 1] = jnp.maximum(top_out[a : a + 1], jnp.where(counted, picked, MASKED))
    sum_out[ACT : ACT + 1] += jnp.where(counted, 1.0, 0.0)


def lamb_moments(weight, gradient, moment_one, moment_two):
    first_new = BETA_FIRST * moment_one + (1.0 - BETA_FIRST) * gradient
    second_new = BETA_SECOND * moment_two + (1.0 - BETA_SECOND) * gradient * gradient
    update = (
        first_new
        * (1.0 / (1.0 - BETA_FIRST**STEP))
        / (jnp.sqrt(second_new * (1.0 / (1.0 - BETA_SECOND**STEP))) + ADAM_EPSILON)
        + WEIGHT_DECAY * weight
    )
    return (first_new, second_new, update)


class Squares:
    def __init__(self):
        self.total = jnp.zeros((8, 128), F32)

    def add(self, lane, weight, update):
        rows = lax.broadcasted_iota(jnp.int32, (8, 128), 0)
        lanes = lax.broadcasted_iota(jnp.int32, (8, 128), 1)
        for row, v in ((6, weight), (7, update)):
            one = jnp.sum(jnp.sum(v * v, axis=0, keepdims=True), axis=1, keepdims=True)
            self.total = self.total + jnp.where((rows == row) & (lanes == lane), one, 0.0)


def lamb_piece(state, outs, grad, rows, cols, squares, lane):
    weight = state[0][rows, cols]
    first_new, second_new, update = lamb_moments(weight, grad, state[1][rows, cols], state[2][rows, cols])
    for out, v in zip(outs, (first_new, second_new, update)):
        out[rows, cols] = v
    squares.add(lane, weight, update)


def core_halves(idx, parts):
    if len(parts) == 1:
        return [lambda rows: parts[0][rows]]
    own = idx[1] == 0
    return [
        lambda rows: jnp.where(own, parts[0][rows], parts[1][rows]),
        lambda rows: jnp.where(own, parts[1][rows], parts[0][rows]),
    ]


def lamb_mlp_kernel(n_f, nh, rows_a, idx, *refs):
    parts, refs = refs[:nh], refs[nh:]
    states = [refs[3 * i : 3 * i + 3] for i in range(3)]
    outs = [refs[9 + 3 * i : 12 + 3 * i] for i in range(3)]
    sq_out = refs[18]
    hm = D // n_f // nh
    h2 = FF // n_f // 2
    hr = h2 // nh
    ne, nd = FF // 2 // QUAD, D // QUAD
    squares = Squares()
    for c, take in enumerate(core_halves(idx, parts)):
        rows = slice(c * hm, c * hm + hm)
        for q in range(nd):
            at = 2 * rows_a + hm * q
            grad = take(slice(at, at + hm))
            lamb_piece(states[0], outs[0], grad, rows, slice(q * QUAD, (q + 1) * QUAD), squares, 1)
        for h in range(2):
            for q in range(ne):
                at = rows_a * h + hm * q
                grad = take(slice(at, at + hm))
                for k in range(QUAD // h2):
                    i = q * (QUAD // h2) + k
                    col = (2 * i + h) * h2
                    lamb_piece(
                        states[1], outs[1], grad[:, k * h2 : (k + 1) * h2], rows,
                        slice(col, col + h2), squares, 2,
                    )
            for q in range(nd):
                at = rows_a * h + hm * ne + hr * q
                grad = take(slice(at, at + hr))
                row = h * h2 + c * hr
                lamb_piece(
                    states[2], outs[2], grad, slice(row, row + hr),
                    slice(q * QUAD, (q + 1) * QUAD), squares, 3,
                )
    sq_out[...] = squares.total


def lamb_triple_kernel(n_f, nh, idx, *refs):
    parts, refs = refs[:nh], refs[nh:]
    sq_in, state, outs, sq_out = refs[0], refs[1:4], refs[4:7], refs[7]
    hm = D // n_f // nh
    squares = Squares()
    for c, take in enumerate(core_halves(idx, parts)):
        for q in range(3 * D // QUAD):
            lamb_piece(
                state, outs, take(slice(hm * q, hm * q + hm)), slice(c * hm, c * hm + hm),
                slice(q * QUAD, (q + 1) * QUAD), squares, 0,
            )
    sq_out[...] = squares.total + sq_in[...]


def merge_small(mine, other):
    row = lax.broadcasted_iota(jnp.int32, mine.shape, 0)
    return jnp.where(row == 5, jnp.maximum(mine, other), mine + other)


def final_kernel(one, two, norms, firsts, seconds, *refs):
    masters, updates, news = refs[:4], refs[4:8], refs[8:12]
    norms_out, first_out, second_out, table_out, mean_out, peak_out = refs[12:]
    small = merge_small(one[...], two[...])
    roots = jnp.sqrt(small[6:8, 0:128])
    for i in range(4):
        ratio = roots[0:1, i : i + 1] / (roots[1:2, i : i + 1] + RATIO_EPSILON)
        news[i][...] = masters[i][...] - LEARNING_RATE * ratio * updates[i][...]
    weight = norms[...]
    first_new, second_new, update = lamb_moments(weight, small[0:4], firsts[...], seconds[...])
    weight_norm = jnp.sqrt(jnp.sum(weight * weight, axis=1, keepdims=True))
    update_norm = jnp.sqrt(jnp.sum(update * update, axis=1, keepdims=True))
    norms_out[...] = weight - LEARNING_RATE * (weight_norm / (update_norm + RATIO_EPSILON)) * update
    first_out[...] = first_new
    second_out[...] = second_new
    row = lax.broadcasted_iota(jnp.int32, (4, 128), 0)
    lane = lax.broadcasted_iota(jnp.int32, (4, 128), 1)
    low = lax.broadcasted_iota(jnp.int32, (1, 128), 1) < 4
    for k, v in enumerate((weight_norm, update_norm)):
        spread = jnp.sum(jnp.where(lane == row + 4, v, 0.0), axis=0, keepdims=True)
        table_out[k : k + 1] = jnp.where(low, roots[k : k + 1], spread)[:, 0:8]
    sums = small[4:5, 0:128]
    mean_out[...] = (sums / jnp.maximum(sums[:, ACT : ACT + 1], 1.0))[:, 0:ACT]
    peak_out[...] = small[5:6, 0:ACT]


def xor_step(v, axis, size, bit):
    return lax.ppermute(v, axis, [(i, i ^ bit) for i in range(size)])


def axis_bits(size):
    bits = []
    b = 1
    while b < size:
        bits.append(b)
        b *= 2
    return bits


def sync(*vs):
    return lax.optimization_barrier(vs)


def halving_positions(order):
    rels = [0]
    for b in reversed(order):
        rels = rels + [r ^ b for r in rels]
    return rels


def add_low(a, b):
    return (a.astype(F32) + b.astype(F32)).astype(BF16)


def const_spec(shape):
    return pl.BlockSpec(shape, lambda *a: (0,) * len(shape))


SMEM = pl.BlockSpec(memory_space=pltpu.SMEM)
ANY = pl.BlockSpec(memory_space=pl.ANY)


def kernel_call(kernel, name, grid, in_specs, out, scratch, mib, args, **more):
    return pl.pallas_call(
        kernel,
        grid=grid,
        in_specs=in_specs,
        out_specs=[spec for spec, _ in out],
        out_shape=[shape for _, shape in out],
        scratch_shapes=scratch,
        compiler_params=pltpu.CompilerParams(
            dimension_semantics=("arbitrary",) * len(grid), vmem_limit_bytes=mib * MIB
        ),
        cost_estimate=pl.CostEstimate(flops=1, bytes_accessed=1, transcendentals=0),
        name=name,
        **more,
    )(*args)


def body(n_d, n_f, *args):
    (
        tokens, cotangent, lengths, valid_mask, action_bins, value_head,
        w_triple, w_mixer, w_expand, w_reduce, norm_params,
        first_triple, first_mixer, first_expand, first_reduce, first_norms,
        second_triple, second_mixer, second_expand, second_reduce, second_norms,
    ) = args
    ep, rows, _ = tokens.shape
    flat = ep * rows
    rows16 = -(-rows // 16) * 16
    padded = -(-rows // QB) * QB
    blocks = padded // QB
    me = lax.axis_index("fsdp")
    dp = lax.axis_index("dp")
    core = dp % 2
    idx = jnp.stack([me, core]).astype(jnp.int32)
    shard = D // n_f
    h2 = FF // n_f // 2
    half_ff = FF // 2
    nh = 2 if shard >= 32 else 1
    f_bits, d_bits = axis_bits(n_f), axis_bits(n_d)
    steps_f = lambda v, b: xor_step(v, "fsdp", n_f, b)
    steps_d = lambda v, b: xor_step(v, "dp", n_d, b)

    def own_half(w):
        n = w.shape[0] // nh
        return lax.dynamic_slice_in_dim(w, core * n, n, 0) if nh == 2 else w

    def ff_half(w, h):
        return jnp.concatenate([w[:, (2 * i + h) * h2 : (2 * i + h + 1) * h2] for i in range(n_f)], axis=1)

    def under(w):
        return [w[:, q * D : (q + 1) * D] for q in range(w.shape[1] // D)]

    own_t = own_half(w_triple).astype(BF16)

    def own_piece(expand, reduce, h, first):
        rows_h = slice(h * h2, (h + 1) * h2)
        return jnp.concatenate(
            first + under(ff_half(own_half(expand), h).astype(BF16)) + [own_half(reduce[rows_h]).astype(BF16)],
            axis=0,
        )

    norm_t = norm_params.T
    norm = jnp.concatenate([norm_t, jnp.zeros((4, D), F32)], axis=0)
    ep_block = lambda width: pl.BlockSpec((1, rows, width), lambda e: (e, 0, 0))
    eps = 2 if ep % 2 == 0 else 1
    eps_block = lambda width: pl.BlockSpec((eps, rows, width), lambda e: (e, 0, 0))
    ep_shape = lambda width, dtype: jax.ShapeDtypeStruct((ep, rows, width), dtype)
    low = lambda width: (ep_block(width), ep_shape(width, BF16))
    wide = lambda width: (ep_block(width), ep_shape(width, F32))
    whole = lambda shape: (const_spec(shape), jax.ShapeDtypeStruct(shape, F32))
    norm_spec = const_spec((8, D))
    lse_spec = pl.BlockSpec((1, 16, QUAD), lambda e: (e, 0, 0))
    dma = pltpu.SemaphoreType.DMA
    wt_scratch = pltpu.VMEM((D, 3 * D), BF16)

    near = f_bits[0]
    rels_a = [0]
    for b in f_bits[1:]:
        rels_a = rels_a + [r ^ b for r in rels_a]
    rels_b = [r ^ near for r in rels_a]
    own_t, w_mixer_0, w_expand_0, w_reduce_0 = sync(own_t, w_mixer, w_expand, w_reduce)
    t_got = [steps_f(own_t, r) for r in rels_a[1:]]
    own_a = own_piece(w_expand_0, w_reduce_0, 0, [own_half(w_mixer_0).astype(BF16)])
    own_b = own_piece(w_expand_0, w_reduce_0, 1, [])
    a_near = steps_f(own_a, near)
    t_one = jnp.stack([own_t, *t_got])
    t_one, idx, norm, own_a, own_b, a_near = sync(t_one, idx, norm, own_a, own_b, a_near)
    t_two = steps_f(t_one, near)
    t_refs, t_plan = [t_one], [(rels_a, nh - 1)]
    if nh == 2:
        t_refs.append(steps_d(t_one, 1))
        t_plan.append((rels_a, 2))
    t_two, own_b = sync(t_two, own_b)
    b_near = steps_f(own_b, near)
    a_pair, b_pair = jnp.stack([own_a, a_near]), jnp.stack([own_b, b_near])
    a_got = [steps_f(a_pair, r) for r in rels_a[1:]]
    t_refs.append(t_two)
    t_plan.append((rels_b, nh - 1))
    if nh == 2:
        for i in range(0, len(rels_b), 2):
            t_refs.append(steps_d(t_two[i : i + 2], 1))
            t_plan.append((rels_b[i : i + 2], 2))
    nw = len(t_refs)
    pair_plan = [([0, near], nh - 1)]
    got_plan = [([r, r ^ near], nh - 1) for r in rels_a[1:]]
    a_refs, a_plan = [a_pair], pair_plan + got_plan
    norm, b_pair, *t_refs = sync(norm, b_pair, *t_refs)
    b_refs, b_got = [b_pair], [steps_f(b_pair, r) for r in rels_a[1:]]
    triple, n1, attended, lse = kernel_call(
        functools.partial(f1_kernel, t_plan, nw), "f1", (ep // eps,),
        [SMEM, SMEM, eps_block(D), norm_spec] + [ANY] * nw,
        [
            (eps_block(3 * D), ep_shape(3 * D, BF16)), (eps_block(D), ep_shape(D, BF16)),
            (eps_block(D), ep_shape(D, BF16)),
            (pl.BlockSpec((eps, 16, QUAD), lambda e: (e, 0, 0)), jax.ShapeDtypeStruct((ep, 16, QUAD), F32)),
        ],
        [wt_scratch, pltpu.VMEM((eps, padded, 3 * D), BF16), dma], 60,
        (idx, lengths, tokens, norm, *t_refs),
    )
    attended, *a_got = sync(attended, *a_got)
    a_refs += a_got
    if nh == 2:
        a_refs += [steps_d(v, 1) for v in [a_pair, *a_got]]
        a_plan = a_plan + [(rels, 2) for rels, _ in a_plan]
    na = len(a_refs)
    attended, *a_refs = sync(attended, *a_refs)

    order = f_bits[1:2] + f_bits[:1] + f_bits[2:]
    late = order[2:]
    pos = halving_positions(order)
    hm, hr = shard // nh, h2 // nh
    rows_a = hm * (half_ff // QUAD) + hr * (D // QUAD)
    rows_b = rows_a + hm * (D // QUAD)
    rows_t = 6 * hm
    half = n_f // 2
    low_out = lambda *shape: (const_spec(shape), jax.ShapeDtypeStruct(shape, BF16))
    ff_scratch = [
        pltpu.VMEM((D, D), BF16), pltpu.VMEM((D, half_ff), BF16), pltpu.VMEM((half_ff, D), BF16),
        pltpu.VMEM((D, half_ff), F32), pltpu.VMEM((D, half_ff), F32),
    ]
    fl = flat // 3 if flat % 48 == 0 else rows
    fl_steps = flat // fl
    fl_block = lambda width, at=0: pl.BlockSpec((fl, width), lambda i: (i + at, 0))
    fl_low = lambda width: (fl_block(width), jax.ShapeDtypeStruct((flat, width), BF16))
    fl_wide = lambda width: (fl_block(width), jax.ShapeDtypeStruct((flat, width), F32))
    tok_flat = tokens.reshape(flat, D)
    cot_flat = cotangent.reshape(flat, D)
    attended = attended.reshape(flat, D)
    hidden, out_part, g2_part, n2, keep_a, send_a = kernel_call(
        functools.partial(f2a_kernel, a_plan, na, pos, rows), "f2a", (fl_steps,),
        [SMEM, SMEM] + [fl_block(D)] * 3 + [norm_spec] + [ANY] * na,
        [fl_wide(D)] * 3 + [fl_low(D)] + [low_out(nh, half, rows_a, QUAD)] * 2,
        ff_scratch + [pltpu.SemaphoreType.DMA((2,))], 60, (idx, lengths, attended, tok_flat, cot_flat, norm, *a_refs),
    )

    def halves(keep, got):
        n = keep.shape[-3] // 2
        return add_low(keep[..., :n, :, :], got[..., :n, :, :]), add_low(keep[..., n:, :, :], got[..., n:, :, :])

    def core_pair(total):
        return (total[0], steps_d(total[1], 1)) if nh == 2 else (total[0], None)

    def core_halves_of(pair):
        mine, other = pair
        n = mine.shape[0] // 2
        return halves(mine, other) if other is not None else (mine[:n], mine[n:])

    def core_add(pair):
        return add_low(*pair) if pair[1] is not None else pair[0]

    n2, keep_a, send_a, *b_got = sync(n2, keep_a, send_a, *b_got)
    b_refs += b_got
    if nh == 2:
        b_refs += [steps_d(v, 1) for v in [b_pair, *b_got]]
    n2, keep_a, send_a, *b_refs = sync(n2, keep_a, send_a, *b_refs)
    got_a = steps_f(send_a, order[0])
    block_out, gh, ga, *rest = kernel_call(
        functools.partial(f2b_kernel, a_plan, na, pos, nh, rows), "f2b", (fl_steps,),
        [SMEM, SMEM] + [fl_block(D)] * 6 + [norm_spec] + [ANY] * (2 * na),
        [fl_low(D), fl_wide(D), fl_low(D)] + [low_out(n_f, rows_b, QUAD)] * nh + [whole((8, D))],
        ff_scratch + [pltpu.VMEM((D, D), F32), pltpu.SemaphoreType.DMA((2,))], 54,
        (idx, lengths, attended, hidden, out_part, g2_part, n2, cot_flat, norm, *a_refs, *b_refs),
    )
    grads_b, ln2 = rest[:nh], rest[nh]
    ga, valid_mask, action_bins, keep_a, got_a, *grads_b = sync(
        ga, valid_mask, action_bins, keep_a, got_a, *grads_b
    )
    pair_b = core_pair(grads_b)
    places = jnp.arange(rows)
    inside = places[None, :] < lengths[:, None]
    counted = ((valid_mask == 1) & inside).astype(jnp.int32).reshape(1, flat)
    bins_t = action_bins.reshape(flat, ACT).T
    sum_a = add_low(keep_a, got_a)
    pair_a = core_pair(sum_a)
    keep_b, send_b = core_halves_of(pair_b)
    keep_a, send_a = core_halves_of(pair_a)
    ga, counted, bins_t, keep_a, send_a, keep_b, send_b = sync(ga, counted, bins_t, keep_a, send_a, keep_b, send_b)

    got_b = steps_f(send_b, order[0])
    got_a = steps_f(send_a, order[1])
    pack_rows = ep * rows16 + PACK
    gtri, *grads_t = kernel_call(
        functools.partial(b1_kernel, pos, nh), "b1", (ep // eps,),
        [SMEM, SMEM, eps_block(3 * D), eps_block(D), pl.BlockSpec((eps, 16, QUAD), lambda e: (e, 0, 0)), eps_block(D)],
        [(eps_block(3 * D), ep_shape(3 * D, BF16))] + [low_out(n_f, rows_t, QUAD)] * nh,
        [
            pltpu.VMEM((eps, padded, 3 * D), BF16), pltpu.VMEM((eps, padded, D), BF16),
            pltpu.VMEM((eps, padded, 3 * D), BF16), pltpu.VMEM((eps, rows16, D), F32),
            pltpu.VMEM((eps, rows16, D), F32), pltpu.VMEM((D, 3 * D), F32),
            pltpu.VMEM((pack_rows, D), BF16), pltpu.VMEM((pack_rows, 3 * D), BF16),
        ],
        48, (idx, lengths, triple, ga.reshape(ep, rows, D), lse, n1),
    )
    gtri, keep_a, got_a, keep_b, got_b, *grads_t = sync(gtri, keep_a, got_a, keep_b, got_b, *grads_t)

    mine_t, other_t = core_pair(grads_t)
    keep_b, send_b = halves(keep_b, got_b)
    if late:
        keep_a, send_a = halves(keep_a, got_a)
    else:
        keep_a, send_a = add_low(keep_a, got_a), keep_a
    mine_t, other_t, keep_a, send_a, keep_b, send_b = sync(mine_t, other_t, keep_a, send_a, keep_b, send_b)
    keep_t, send_t = core_halves_of((mine_t, other_t))
    block_out, keep_t, send_t, keep_a, send_a, keep_b, send_b = sync(
        block_out, keep_t, send_t, keep_a, send_a, keep_b, send_b
    )
    got_t = steps_f(send_t, order[0])
    got_b = steps_f(send_b, order[1])
    if late:
        got_a = steps_f(send_a, late[0])

    qb = 256
    steps = -(-flat // qb)
    q_sum, q_top = kernel_call(
        functools.partial(q_kernel, flat), "qstat", (steps,),
        [
            pl.BlockSpec((qb, D), lambda i: (i, 0)), const_spec((ACT * NBINS, D)),
            pl.BlockSpec((ACT, qb), lambda i: (0, i)), pl.BlockSpec((1, qb), lambda i: (0, i)),
        ],
        [whole((16, qb))] * 2, [], 20, (block_out, value_head, bins_t, counted),
    )
    gtri, q_sum, keep_t, got_t, keep_b, got_b = sync(gtri, q_sum, keep_t, got_t, keep_b, got_b)

    def b2_call(at, n, gtri, prior, more_in):
        extra = [] if prior is None else [prior, *more_in]
        specs = [] if prior is None else [ANY] + [const_spec(v.shape) for v in more_in]
        more = {} if prior is None else {"input_output_aliases": {5 + nw: 0}}
        return kernel_call(
            functools.partial(b2_kernel, t_plan, nw, prior is None), "b2", (n,),
            [SMEM, fl_block(3 * D, at), fl_block(D, at), fl_block(D, at), norm_spec] + [ANY] * nw + specs,
            [(fl_block(D, at), jax.ShapeDtypeStruct((flat, D), BF16)), whole((8, D))],
            [wt_scratch, dma], 28, (idx, gtri, tok_flat, gh, norm, *t_refs, *extra), **more,
        )

    keep_t, send_t = halves(keep_t, got_t)
    if late:
        keep_b, send_b = halves(keep_b, got_b)
    else:
        keep_b, send_b = add_low(keep_b, got_b), keep_b
    gtri_flat = gtri.reshape(flat, 3 * D)
    gtri_flat, keep_t, send_t, keep_b, send_b = sync(gtri_flat, keep_t, send_t, keep_b, send_b)
    got_t = steps_f(send_t, order[1])
    if late:
        got_b = steps_f(send_b, late[0])
    cut = (fl_steps + 1) // 2
    ig_part, ln1_a = b2_call(0, cut, gtri_flat, None, ())
    ig_part, keep_t, got_t, keep_b, *got_b = sync(ig_part, keep_t, got_t, keep_b, *([got_b] if late else []))

    def finish(keep, bits):
        for b in bits:
            n = keep.shape[0] // 2
            keep = add_low(keep[:n], steps_f(keep[n:], b))
        return keep[0]

    x_bits = d_bits[nh - 1 :]
    if late:
        keep_t, send_t = halves(keep_t, got_t)
        keep_b, keep_a = add_low(keep_b, got_b[0]), add_low(keep_a, got_a)
    else:
        keep_t = add_low(keep_t, got_t)
    red = jnp.concatenate([finish(keep_a, late[1:]), finish(keep_b, late[1:])], axis=0)
    for b in x_bits[:-1]:
        red = add_low(red, steps_d(red, b))
    red, keep_t, ig_part = sync(red, keep_t, ig_part)
    if late:
        got_t = steps_f(send_t, late[0])
    got_red = steps_d(red, x_bits[-1])
    input_grad, small = b2_call(cut, fl_steps - cut, gtri_flat, ig_part, (ln1_a, ln2, q_sum, q_top))
    small, red, got_red, keep_t, *got_t = sync(small, red, got_red, keep_t, *([got_t] if late else []))

    red_t = finish(add_low(keep_t, got_t[0]) if late else keep_t, late[1:])
    for b in x_bits[:-1]:
        red_t = add_low(red_t, steps_d(red_t, b))
    got_rt = steps_d(red_t, x_bits[-1])
    red = red.astype(F32) + got_red.astype(F32)
    red_parts = [red] + ([steps_d(red, 1)] if nh == 2 else [])
    small_core = steps_d(small, d_bits[0])
    red_t, *red_parts = sync(red_t, *red_parts)
    like = lambda w: whole(w.shape)
    full = lambda *ws: [pl.BlockSpec(memory_space=pltpu.VMEM)] * len(ws)
    mlp_state = (
        w_mixer, first_mixer, second_mixer, w_expand, first_expand, second_expand,
        w_reduce, first_reduce, second_reduce,
    )
    *mlp_out, sq_mlp = kernel_call(
        functools.partial(lamb_mlp_kernel, n_f, nh, rows_a), "lamb_mlp", (1,),
        [SMEM] + full(*red_parts, *mlp_state),
        [like(w) for w in (w_mixer, w_expand, w_reduce) for _ in range(3)] + [whole((8, 128))],
        [], 20, (idx, *red_parts, *mlp_state),
    )
    small, small_core, sq_mlp, red_t, got_rt = sync(small, small_core, sq_mlp, red_t, got_rt)
    small = merge_small(small, small_core)
    for b in d_bits[1:]:
        small = merge_small(small, steps_d(small, b))
    red_t = red_t.astype(F32) + got_rt.astype(F32)
    parts_t = [red_t] + ([steps_d(red_t, 1)] if nh == 2 else [])
    tri_state = (w_triple, first_triple, second_triple)
    *tri_out, squares = kernel_call(
        functools.partial(lamb_triple_kernel, n_f, nh), "lamb_triple", (1,),
        [SMEM] + full(*parts_t, sq_mlp, *tri_state),
        [like(w_triple)] * 3 + [whole((8, 128))],
        [], 12, (idx, *parts_t, sq_mlp, *tri_state),
    )

    small = small + jnp.pad(squares, ((0, 0), (0, D - 128)))
    for b in f_bits[:-1]:
        small = merge_small(small, steps_f(small, b))
    small_two = steps_f(small, f_bits[-1])
    masters = (w_triple, w_mixer, w_expand, w_reduce)
    updates = (tri_out[2], mlp_out[2], mlp_out[5], mlp_out[8])
    firsts_t, seconds_t = first_norms.T, second_norms.T
    *news, norms_out, first_out, second_out, norm_table, mean, peak = kernel_call(
        final_kernel, "final", (1,),
        full(small, small_two, norm_t, firsts_t, seconds_t, *masters, *updates),
        [like(w) for w in masters]
        + [whole((4, D))] * 3 + [whole((2, 8)), whole((1, ACT)), whole((1, ACT))],
        [], 16, (small, small_two, norm_t, firsts_t, seconds_t, *masters, *updates),
    )
    return (
        block_out.reshape(ep, rows, D), input_grad.reshape(ep, rows, D), *news,
        tri_out[0], mlp_out[0], mlp_out[3], mlp_out[6],
        tri_out[1], mlp_out[1], mlp_out[4], mlp_out[7],
        norms_out.T, first_out.T, second_out.T, norm_table, mean.reshape(ACT), peak.reshape(ACT),
    )


def solution(mesh):
    n_d, n_f = mesh.shape["dp"], mesh.shape["fsdp"]
    both = ("dp", "fsdp")
    row, rep = P("fsdp", None), P()
    in_specs = (
        P(both, None, None), P(both, None, None), P(both), P(both, None), P(both, None, None), rep,
        row, row, row, row, rep,
        row, row, row, row, rep,
        row, row, row, row, rep,
    )
    out_specs = (
        (P(both, None, None),) * 2 + (row,) * 12 + (rep,) * 6
    )
    return jax.shard_map(
        functools.partial(body, n_d, n_f), mesh=mesh, in_specs=in_specs, out_specs=out_specs,
        check_vma=False,
    )
```

```python
import functools

import jax
import jax.numpy as jnp
from jax import lax
from jax.experimental import pallas as pl
from jax.experimental.pallas import tpu as pltpu
from jax.sharding import PartitionSpec as P

HEADS = 8
HEAD_DIM = 64
ACT = 11
NBINS = 256
STEP = 5

NORM_EPSILON = 1e-05
BETA_FIRST = 0.9
BETA_SECOND = 0.999
ADAM_EPSILON = 1e-06
RATIO_EPSILON = 1e-06
WEIGHT_DECAY = 0.01
LEARNING_RATE = 0.5
MASKED = -1e30

D = 512
FF = 2048
QB = 64
PACK = 256
QUAD = 256
F32 = jnp.float32
BF16 = jnp.bfloat16
MIB = 1024 * 1024

NT = (((1,), (1,)), ((), ()))
NN = (((1,), (0,)), ((), ()))
TN = (((0,), (0,)), ((), ()))


def mm(a, b, dims=NN):
    return lax.dot_general(a, b, dims, preferred_element_type=F32)


def pad_rows(v, rows):
    if v.shape[0] == rows:
        return v
    return jnp.concatenate([v, jnp.zeros((rows - v.shape[0], v.shape[1]), v.dtype)], axis=0)


def ln_parts(x):
    center = x - jnp.mean(x, axis=-1, keepdims=True)
    spread = jnp.mean(center * center, axis=-1, keepdims=True)
    rstd = lax.rsqrt(spread + NORM_EPSILON)
    return center * rstd, rstd


def ln_back(grad, xhat, rstd, gain):
    t = grad * gain
    m1 = jnp.mean(t, axis=-1, keepdims=True)
    m2 = jnp.mean(t * xhat, axis=-1, keepdims=True)
    return rstd * (t - m1 - xhat * m2)


def head_masks():
    lane = lax.broadcasted_iota(jnp.int32, (1, QUAD), 1)
    return [jnp.where(lane // HEAD_DIM == h, 1.0, 0.0).astype(BF16) for h in range(4)]


def stack_heads(block, masks):
    return jnp.concatenate([block * m for m in masks], axis=0)


def own_lanes(t):
    head = lax.broadcasted_iota(jnp.int32, (QB, QUAD), 1) // HEAD_DIM
    out = t[0:QB]
    for h in range(1, 4):
        out = jnp.where(head == h, t[QB * h : QB * (h + 1)], out)
    return out


def place(block, size, side, core):
    if side == 0:
        return pl.multiple_of(block * size, size)
    c = core if side == 1 else 1 - core
    return pl.multiple_of(block * (2 * size) + c * size, size)


def run_copies(copies, start):
    for copy in copies:
        copy.start() if start else copy.wait()


def load_triple(refs, plan, dst, sem, me, core, start):
    for ref, (rels, side) in zip(refs, plan):
        half = ref.shape[1]
        for p, rel in enumerate(rels):
            row = place(jnp.bitwise_xor(me, rel), half, side, core)
            run_copies([pltpu.make_async_copy(ref.at[p], dst.at[pl.ds(row, half)], sem)], start)


def load_mixer(refs, plan, wm, sem, me, core, start):
    for ref, (rels, side) in zip(refs, plan):
        hm = D // wm_blocks(plan) // (1 if side == 0 else 2)
        for p, rel in enumerate(rels):
            row = place(jnp.bitwise_xor(me, rel), hm, side, core)
            run_copies([pltpu.make_async_copy(ref.at[p, pl.ds(0, hm)], wm.at[pl.ds(row, hm)], sem)], start)


def wm_blocks(plan):
    return sum(len(rels) for rels, side in plan if side != 2)


def load_ff(refs, plan, at_mixer, we, wr, sem, me, core, start):
    for ref, (rels, side) in zip(refs, plan):
        halves = 1 if side == 0 else 2
        hm = D // wm_blocks(plan) // halves
        hr = wr.shape[0] // wm_blocks(plan) // halves
        nc = we.shape[1] // D
        at = hm if at_mixer else 0
        for p, rel in enumerate(rels):
            block = jnp.bitwise_xor(me, rel)
            row, rowr = place(block, hm, side, core), place(block, hr, side, core)
            copies = []
            for q in range(nc):
                copies.append(
                    pltpu.make_async_copy(
                        ref.at[p, pl.ds(at + hm * q, hm)],
                        we.at[pl.ds(row, hm), pl.ds(q * D, D)],
                        sem,
                    )
                )
            copies.append(
                pltpu.make_async_copy(ref.at[p, pl.ds(at + hm * nc, hr)], wr.at[pl.ds(rowr, hr)], sem)
            )
            run_copies(copies, start)


def f1_kernel(plan, nw, idx, lens, tok, norm, *refs):
    w_refs, (tri_out, n1_out, att_out, lse_out, wt, tri, sem) = refs[:nw], refs[nw:]
    e = pl.program_id(0)
    count, rows = tok.shape[:2]
    padded = tri.shape[1]
    rows16 = -(-rows // 16) * 16

    @pl.when(e == 0)
    def _():
        load_triple(w_refs, plan, wt, sem, idx[0], idx[1], True)
        tri[:, rows16:padded] = jnp.zeros((count, padded - rows16, 3 * D), BF16)
        load_triple(w_refs, plan, wt, sem, idx[0], idx[1], False)

    for i in range(count):
        xhat, _ = ln_parts(pad_rows(tok[i].astype(F32), rows16))
        n1 = (xhat * norm[0:1] + norm[1:2]).astype(BF16)
        n1_out[i] = n1[:rows]
        t = mm(n1, wt[...]).astype(BF16)
        tri[i, 0:rows16, 0:D] = t[:, 0:D] * jnp.asarray(HEAD_DIM**-0.5, BF16)
        tri[i, 0:rows16, D:] = t[:, D:]
        tri_out[i] = tri[i, 0:rows]

    masks = head_masks()
    lane = lax.broadcasted_iota(jnp.int32, (1, QUAD), 1) % QB
    blocks = -(-rows // QB)
    chains = [
        (i, j, g * QUAD, g * blocks + j)
        for i in range(count) for j in range(blocks) for g in range(HEADS // 4)
    ]
    exts = [min(QB * (j + 1), rows16) for _, j, _, _ in chains]
    q4 = [stack_heads(tri[i, QB * j : QB * (j + 1), gl : gl + QUAD], masks) for i, j, gl, _ in chains]
    s = [mm(tri[i, 0:x, D + gl : D + gl + QUAD], q, NT) for (i, _, gl, _), x, q in zip(chains, exts, q4)]
    pb = []
    for (i, j, _, at), x, v in zip(chains, exts, s):
        kmax = jnp.minimum(lane + QB * j, lens[e * count + i] - 1)
        krow = lax.broadcasted_iota(jnp.int32, (x, QUAD), 0)
        v = jnp.where(krow <= kmax, v, MASKED)
        m = jnp.max(v, axis=0, keepdims=True)
        p = jnp.exp(v - m)
        total = jnp.sum(p, axis=0, keepdims=True)
        lse_out[i, pl.ds(at, 1), :] = m + jnp.log(total)
        pb.append((p * (1.0 / total)).astype(BF16))
    o = [mm(v, tri[i, 0:x, 2 * D + gl : 2 * D + gl + QUAD], TN) for (i, _, gl, _), x, v in zip(chains, exts, pb)]
    for (i, j, gl, _), v in zip(chains, o):
        live = min(QB, rows - QB * j)
        att_out[i, QB * j : QB * j + live, gl : gl + QUAD] = own_lanes(v).astype(BF16)[:live]


def put_rows(dst, at_index, at, src, row, rows):
    for q in range(src.shape[1] // QUAD):
        dst[(*at_index, slice(at, at + rows))] = src[pl.ds(row, rows), q * QUAD : (q + 1) * QUAD].astype(BF16)
        at += rows
    return at


def put_ff_grads(target, halves, pos, idx, acc_e, acc_r, wr, acc_m=None):
    hm = D // len(pos) // halves
    hr = wr.shape[0] // len(pos) // halves
    for c in range(wr.shape[0] // D):
        wr[c * D : c * D + D] = acc_r[:, c * D : c * D + D].T.astype(BF16)
    for p, rel in enumerate(pos):
        block = jnp.bitwise_xor(idx[0], rel)
        for c in range(halves):
            side = 0 if halves == 1 else c + 1
            dst, where = target(c, p)
            row, rowr = place(block, hm, side, idx[1]), place(block, hr, side, idx[1])
            at = put_rows(dst, where, 0, acc_e, row, hm)
            at = put_rows(dst, where, at, wr, rowr, hr)
            if acc_m is not None:
                put_rows(dst, where, at, acc_m, row, hm)


def ff_chunks(n2, glow, out, g2, we, wr, acc_e, acc_r):
    for c in range(we.shape[1] // D):
        cs = slice(c * D, c * D + D)
        ex = mm(n2, we[:, cs])
        phi = 0.5 + 0.5 * lax.erf(ex * 0.7071067811865476)
        act = (ex * phi).astype(BF16)
        gp = phi + ex * (jnp.exp(-0.5 * ex * ex) * 0.3989422804014327)
        out = out + mm(act, wr[cs])
        gact = mm(glow, wr[cs], NT)
        ge = (gp * gact).astype(BF16)
        back = mm(ge, we[:, cs], NT)
        g2 = back if g2 is None else g2 + back
        acc_r[:, cs] += mm(glow, act, TN)
        acc_e[:, cs] += mm(n2, ge, TN)
    return out, g2


def live_rows(cot, lens, rows, step):
    count = cot.shape[0] // rows
    row = lax.broadcasted_iota(jnp.int32, (cot.shape[0], 1), 0)
    live = None
    for i in range(count):
        inside = (row >= i * rows) & (row < i * rows + lens[step * count + i])
        live = inside if live is None else live | inside
    return cot * jnp.where(live, 1.0, 0.0).astype(BF16)


def f2a_kernel(plan, nw, pos, rows, idx, lens, att_ref, tok, cot, norm, *refs):
    w_refs, refs = refs[:nw], refs[nw:]
    hid_out, out_out, g2_out, n2_out, keep, send, wm, we, wr, acc_e, acc_r, sem = refs
    s = pl.program_id(0)

    @pl.when(s == 0)
    def _():
        load_mixer(w_refs, plan, wm, sem.at[0], idx[0], idx[1], True)
        load_ff(w_refs, plan, True, we, wr, sem.at[1], idx[0], idx[1], True)
        acc_e[...] = jnp.zeros_like(acc_e)
        acc_r[...] = jnp.zeros_like(acc_r)
        load_mixer(w_refs, plan, wm, sem.at[0], idx[0], idx[1], False)

    glow = live_rows(cot[...], lens, rows, s)
    hidden = tok[...].astype(F32) + mm(att_ref[...], wm[...])
    xhat, _ = ln_parts(hidden)
    n2 = (xhat * norm[2:3] + norm[3:4]).astype(BF16)
    hid_out[...] = hidden
    n2_out[...] = n2

    @pl.when(s == 0)
    def _():
        load_ff(w_refs, plan, True, we, wr, sem.at[1], idx[0], idx[1], False)

    out, g2 = ff_chunks(n2, glow, hidden, None, we, wr, acc_e, acc_r)
    out_out[...] = out
    g2_out[...] = g2

    @pl.when(s == pl.num_programs(0) - 1)
    def _():
        half = len(pos) // 2
        target = lambda c, p: (keep if p < half else send, (c, p % half))
        put_ff_grads(target, keep.shape[0], pos, idx, acc_e, acc_r, wr)


def f2b_kernel(plan, nw, pos, nh, rows, idx, lens, att_ref, hid, out_ref, g2_ref, n2_ref, cot, norm, *refs):
    w_refs, b_refs, refs = refs[:nw], refs[nw : 2 * nw], refs[2 * nw :]
    (block_out, gh_out, ga_out), grads, refs = refs[:3], refs[3 : 3 + nh], refs[3 + nh :]
    ln_out, wm, we, wr, acc_e, acc_r, acc_m, sem = refs
    s = pl.program_id(0)

    @pl.when(s == 0)
    def _():
        load_ff(b_refs, plan, False, we, wr, sem.at[1], idx[0], idx[1], True)
        load_mixer(w_refs, plan, wm, sem.at[0], idx[0], idx[1], True)
        acc_e[...] = jnp.zeros_like(acc_e)
        acc_r[...] = jnp.zeros_like(acc_r)
        acc_m[...] = jnp.zeros_like(acc_m)
        ln_out[...] = jnp.zeros_like(ln_out)
        load_ff(b_refs, plan, False, we, wr, sem.at[1], idx[0], idx[1], False)

    gain = norm[2:3]
    glow = live_rows(cot[...], lens, rows, s)
    out, g2 = ff_chunks(n2_ref[...], glow, out_ref[...], g2_ref[...], we, wr, acc_e, acc_r)
    block_out[...] = out.astype(BF16)
    xhat, rstd = ln_parts(hid[...])
    gh = glow.astype(F32) + ln_back(g2, xhat, rstd, gain)
    ln_out[0:1] += jnp.sum(g2 * xhat, axis=0, keepdims=True)
    ln_out[1:2] += jnp.sum(g2, axis=0, keepdims=True)

    @pl.when(s == 0)
    def _():
        load_mixer(w_refs, plan, wm, sem.at[0], idx[0], idx[1], False)

    gb = gh.astype(BF16)
    gh_out[...] = gh
    acc_m[...] += mm(att_ref[...], gb, TN)
    ga_out[...] = mm(gb, wm[...], NT).astype(BF16)

    @pl.when(s == pl.num_programs(0) - 1)
    def _():
        put_ff_grads(lambda c, p: (grads[c], (p,)), nh, pos, idx, acc_e, acc_r, wr, acc_m)


def b1_kernel(pos, nh, idx, lens, tri_ref, ga_ref, lse, n1, gtri_out, *refs):
    grads, (tri, ga, gtri, dk, dv, acc, n1p, gtp) = refs[:nh], refs[nh:]
    e = pl.program_id(0)
    last = pl.num_programs(0) - 1
    count, rows = n1.shape[:2]
    padded = tri.shape[1]
    rows16 = -(-rows // 16) * 16
    low16 = rows // 16 * 16

    @pl.when(e == 0)
    def _():
        acc[...] = jnp.zeros_like(acc)
        tri[:, low16:padded] = jnp.zeros((count, padded - low16, 3 * D), BF16)
        ga[:, low16:padded] = jnp.zeros((count, padded - low16, D), BF16)

    for i in range(count):
        tri[i, 0:rows] = tri_ref[i]
        ga[i, 0:rows] = ga_ref[i]
    dk[...] = jnp.zeros_like(dk)
    dv[...] = jnp.zeros_like(dv)
    gtri[:, :, 0:D] = jnp.zeros((count, padded, D), BF16)

    lengths = [lens[e * count + i] for i in range(count)]
    masks = head_masks()
    lane = lax.broadcasted_iota(jnp.int32, (1, QUAD), 1) % QB
    blocks = -(-rows // QB)

    def run(chains):
        chains = [(i, j, g * QUAD, g * blocks + j) for i, j in chains for g in range(HEADS // 4)]
        exts = [min(QB * (j + 1), rows16) for _, j, _, _ in chains]
        q4 = [stack_heads(tri[i, QB * j : QB * (j + 1), gl : gl + QUAD], masks) for i, j, gl, _ in chains]
        do4 = [stack_heads(ga[i, QB * j : QB * (j + 1), gl : gl + QUAD], masks) for i, j, gl, _ in chains]
        s = [mm(tri[i, 0:x, D + gl : D + gl + QUAD], q, NT) for (i, _, gl, _), x, q in zip(chains, exts, q4)]
        dp = [mm(tri[i, 0:x, 2 * D + gl : 2 * D + gl + QUAD], d, NT) for (i, _, gl, _), x, d in zip(chains, exts, do4)]
        p = []
        for (i, j, _, at), x, v in zip(chains, exts, s):
            kmax = jnp.minimum(lane + QB * j, lengths[i] - 1)
            krow = lax.broadcasted_iota(jnp.int32, (x, QUAD), 0)
            p.append(jnp.exp(jnp.where(krow <= kmax, v - lse[i, pl.ds(at, 1), :], MASKED)))
        ds = []
        for v, w in zip(p, dp):
            delta = jnp.sum(v * w, axis=0, keepdims=True)
            ds.append((v * (w - delta)).astype(BF16))
        for (i, _, gl, _), x, v, d in zip(chains, exts, p, do4):
            dv[i, 0:x, gl : gl + QUAD] += mm(v.astype(BF16), d)
        dq = [mm(v, tri[i, 0:x, D + gl : D + gl + QUAD], TN) for (i, _, gl, _), x, v in zip(chains, exts, ds)]
        for (i, _, gl, _), x, v, q in zip(chains, exts, ds, q4):
            dk[i, 0:x, gl : gl + QUAD] += mm(v, q)
        for (i, j, gl, _), v in zip(chains, dq):
            gtri[i, QB * j : QB * (j + 1), gl : gl + QUAD] = (own_lanes(v) * HEAD_DIM**-0.5).astype(BF16)

    run([(i, j) for i in range(count) for j in range(min(2, blocks))])
    for i in range(count):
        for j in range(2, blocks, 2):

            @pl.when(lengths[i] > QB * j)
            def _(i=i, j=j):
                run([(i, k) for k in range(j, min(j + 2, blocks))])

    start = jnp.int32(0)
    for i in range(lens.shape[0] - count):
        start = start + jnp.where(i < e * count, (lens[i] + 15) // 16, 0)
    for i in range(count):
        gtri[i, 0:rows16, D : 2 * D] = dk[i].astype(BF16)
        gtri[i, 0:rows16, 2 * D :] = dv[i].astype(BF16)
        gtri_out[i] = gtri[i, 0:rows]
        at = pl.multiple_of(start * 16, 16)
        n1p[pl.ds(at, rows16)] = pad_rows(n1[i], rows16)
        gtp[pl.ds(at, rows16)] = gtri[i, 0:rows16]
        start = start + (lengths[i] + 15) // 16

    @pl.when(e == last)
    def _():
        end = pl.multiple_of(at + rows16, 16)
        n1p[pl.ds(end, PACK)] = jnp.zeros((PACK, D), BF16)
        gtp[pl.ds(end, PACK)] = jnp.zeros((PACK, 3 * D), BF16)

        def chunk(i, carry):
            row = pl.multiple_of(i * PACK, PACK)
            acc[...] += mm(n1p[pl.ds(row, PACK)], gtp[pl.ds(row, PACK)], TN)
            return carry

        lax.fori_loop(0, (start * 16 + PACK - 1) // PACK, chunk, 0)
        hm = D // len(pos) // nh
        for p, rel in enumerate(pos):
            block = jnp.bitwise_xor(idx[0], rel)
            for c in range(nh):
                side = 0 if nh == 1 else c + 1
                put_rows(grads[c], (p,), 0, acc, place(block, hm, side, idx[1]), hm)


def b2_kernel(plan, nw, first, idx, gtri, tok, gh, norm, *refs):
    w_refs, refs = refs[:nw], refs[nw:]
    if first:
        ig_out, ln_out, wt, sem = refs
    else:
        _, ln1_a, ln2, q_sum, q_top, ig_out, ln_out, wt, sem = refs
    s = pl.program_id(0)

    @pl.when(s == 0)
    def _():
        load_triple(w_refs, plan, wt, sem, idx[0], idx[1], True)
        ln_out[...] = jnp.zeros_like(ln_out)
        load_triple(w_refs, plan, wt, sem, idx[0], idx[1], False)

    g1 = mm(gtri[...], wt[...], NT)
    xhat, rstd = ln_parts(tok[...].astype(F32))
    ig_out[...] = (gh[...] + ln_back(g1, xhat, rstd, norm[0:1])).astype(BF16)
    ln_out[0:1] += jnp.sum(g1 * xhat, axis=0, keepdims=True)
    ln_out[1:2] += jnp.sum(g1, axis=0, keepdims=True)

    if not first:

        @pl.when(s == pl.num_programs(0) - 1)
        def _():
            ln_out[0:2] += ln1_a[0:2]
            ln_out[2:4] = ln2[0:2]
            ln_out[4:5, 0:16] = jnp.sum(q_sum[...].T, axis=0, keepdims=True)
            ln_out[5:6, 0:16] = jnp.max(q_top[...].T, axis=0, keepdims=True)


def q_kernel(total_rows, bo, vh, bins, cnt, sum_out, top_out):
    s = pl.program_id(0)
    block = bo.shape[0]

    @pl.when(s == 0)
    def _():
        sum_out[...] = jnp.zeros_like(sum_out)
        top_out[...] = jnp.full_like(top_out, MASKED)

    place = lax.broadcasted_iota(jnp.int32, (1, block), 1) + s * block
    counted = (cnt[...] > 0) & (place < total_rows)
    binrow = lax.broadcasted_iota(jnp.int32, (NBINS, block), 0)
    for a in range(ACT):
        sc = mm(vh[a * NBINS : (a + 1) * NBINS], bo[...], NT)
        picked = jnp.sum(jnp.where(binrow == bins[a : a + 1], sc, 0.0), axis=0, keepdims=True)
        sum_out[a : a + 1] += jnp.where(counted, picked, 0.0)
        top_out[a : a + 1] = jnp.maximum(top_out[a : a + 1], jnp.where(counted, picked, MASKED))
    sum_out[ACT : ACT + 1] += jnp.where(counted, 1.0, 0.0)


def lamb_moments(weight, gradient, moment_one, moment_two):
    first_new = BETA_FIRST * moment_one + (1.0 - BETA_FIRST) * gradient
    second_new = BETA_SECOND * moment_two + (1.0 - BETA_SECOND) * gradient * gradient
    update = (
        first_new
        * (1.0 / (1.0 - BETA_FIRST**STEP))
        / (jnp.sqrt(second_new * (1.0 / (1.0 - BETA_SECOND**STEP))) + ADAM_EPSILON)
        + WEIGHT_DECAY * weight
    )
    return (first_new, second_new, update)


class Squares:
    def __init__(self):
        self.total = jnp.zeros((8, 128), F32)

    def add(self, lane, weight, update):
        rows = lax.broadcasted_iota(jnp.int32, (8, 128), 0)
        lanes = lax.broadcasted_iota(jnp.int32, (8, 128), 1)
        for row, v in ((6, weight), (7, update)):
            one = jnp.sum(jnp.sum(v * v, axis=0, keepdims=True), axis=1, keepdims=True)
            self.total = self.total + jnp.where((rows == row) & (lanes == lane), one, 0.0)


def lamb_piece(state, outs, grad, rows, cols, squares, lane):
    weight = state[0][rows, cols]
    first_new, second_new, update = lamb_moments(weight, grad, state[1][rows, cols], state[2][rows, cols])
    for out, v in zip(outs, (first_new, second_new, update)):
        out[rows, cols] = v
    squares.add(lane, weight, update)


def core_halves(idx, parts):
    if len(parts) == 1:
        return [lambda rows: parts[0][rows]]
    own = idx[1] == 0
    return [
        lambda rows: jnp.where(own, parts[0][rows], parts[1][rows]),
        lambda rows: jnp.where(own, parts[1][rows], parts[0][rows]),
    ]


def lamb_mlp_kernel(n_f, nh, rows_a, idx, *refs):
    parts, refs = refs[:nh], refs[nh:]
    states = [refs[3 * i : 3 * i + 3] for i in range(3)]
    outs = [refs[9 + 3 * i : 12 + 3 * i] for i in range(3)]
    sq_out = refs[18]
    hm = D // n_f // nh
    h2 = FF // n_f // 2
    hr = h2 // nh
    ne, nd = FF // 2 // QUAD, D // QUAD
    squares = Squares()
    for c, take in enumerate(core_halves(idx, parts)):
        rows = slice(c * hm, c * hm + hm)
        for q in range(nd):
            at = 2 * rows_a + hm * q
            grad = take(slice(at, at + hm))
            lamb_piece(states[0], outs[0], grad, rows, slice(q * QUAD, (q + 1) * QUAD), squares, 1)
        for h in range(2):
            for q in range(ne):
                at = rows_a * h + hm * q
                grad = take(slice(at, at + hm))
                for k in range(QUAD // h2):
                    i = q * (QUAD // h2) + k
                    col = (2 * i + h) * h2
                    lamb_piece(
                        states[1], outs[1], grad[:, k * h2 : (k + 1) * h2], rows,
                        slice(col, col + h2), squares, 2,
                    )
            for q in range(nd):
                at = rows_a * h + hm * ne + hr * q
                grad = take(slice(at, at + hr))
                row = h * h2 + c * hr
                lamb_piece(
                    states[2], outs[2], grad, slice(row, row + hr),
                    slice(q * QUAD, (q + 1) * QUAD), squares, 3,
                )
    sq_out[...] = squares.total


def lamb_triple_kernel(n_f, nh, idx, *refs):
    parts, refs = refs[:nh], refs[nh:]
    sq_in, state, outs, sq_out = refs[0], refs[1:4], refs[4:7], refs[7]
    hm = D // n_f // nh
    squares = Squares()
    for c, take in enumerate(core_halves(idx, parts)):
        for q in range(3 * D // QUAD):
            lamb_piece(
                state, outs, take(slice(hm * q, hm * q + hm)), slice(c * hm, c * hm + hm),
                slice(q * QUAD, (q + 1) * QUAD), squares, 0,
            )
    sq_out[...] = squares.total + sq_in[...]


def merge_small(mine, other):
    row = lax.broadcasted_iota(jnp.int32, mine.shape, 0)
    return jnp.where(row == 5, jnp.maximum(mine, other), mine + other)


def final_kernel(count, *refs):
    parts, (norms, firsts, seconds), refs = refs[:count], refs[count : count + 3], refs[count + 3 :]
    masters, updates, news = refs[:4], refs[4:8], refs[8:12]
    norms_out, first_out, second_out, table_out, mean_out, peak_out = refs[12:]
    level = [part[...] for part in parts]
    while len(level) > 1:
        level = [merge_small(level[i], level[i + 1]) for i in range(0, len(level), 2)]
    small = level[0]
    roots = jnp.sqrt(small[6:8, 0:128])
    for i in range(4):
        ratio = roots[0:1, i : i + 1] / (roots[1:2, i : i + 1] + RATIO_EPSILON)
        news[i][...] = masters[i][...] - LEARNING_RATE * ratio * updates[i][...]
    weight = norms[...]
    first_new, second_new, update = lamb_moments(weight, small[0:4], firsts[...], seconds[...])
    weight_norm = jnp.sqrt(jnp.sum(weight * weight, axis=1, keepdims=True))
    update_norm = jnp.sqrt(jnp.sum(update * update, axis=1, keepdims=True))
    norms_out[...] = weight - LEARNING_RATE * (weight_norm / (update_norm + RATIO_EPSILON)) * update
    first_out[...] = first_new
    second_out[...] = second_new
    row = lax.broadcasted_iota(jnp.int32, (4, 128), 0)
    lane = lax.broadcasted_iota(jnp.int32, (4, 128), 1)
    low = lax.broadcasted_iota(jnp.int32, (1, 128), 1) < 4
    for k, v in enumerate((weight_norm, update_norm)):
        spread = jnp.sum(jnp.where(lane == row + 4, v, 0.0), axis=0, keepdims=True)
        table_out[k : k + 1] = jnp.where(low, roots[k : k + 1], spread)[:, 0:8]
    sums = small[4:5, 0:128]
    mean_out[...] = (sums / jnp.maximum(sums[:, ACT : ACT + 1], 1.0))[:, 0:ACT]
    peak_out[...] = small[5:6, 0:ACT]


def xor_step(v, axis, size, bit):
    return lax.ppermute(v, axis, [(i, i ^ bit) for i in range(size)])


def axis_bits(size):
    bits = []
    b = 1
    while b < size:
        bits.append(b)
        b *= 2
    return bits


def sync(*vs):
    return lax.optimization_barrier(vs)


def halving_positions(order):
    rels = [0]
    for b in reversed(order):
        rels = rels + [r ^ b for r in rels]
    return rels


def add_low(a, b):
    return (a.astype(F32) + b.astype(F32)).astype(BF16)


def const_spec(shape):
    return pl.BlockSpec(shape, lambda *a: (0,) * len(shape))


SMEM = pl.BlockSpec(memory_space=pltpu.SMEM)
ANY = pl.BlockSpec(memory_space=pl.ANY)


def kernel_call(kernel, name, grid, in_specs, out, scratch, mib, args, **more):
    return pl.pallas_call(
        kernel,
        grid=grid,
        in_specs=in_specs,
        out_specs=[spec for spec, _ in out],
        out_shape=[shape for _, shape in out],
        scratch_shapes=scratch,
        compiler_params=pltpu.CompilerParams(
            dimension_semantics=("arbitrary",) * len(grid), vmem_limit_bytes=mib * MIB
        ),
        cost_estimate=pl.CostEstimate(flops=1, bytes_accessed=1, transcendentals=0),
        name=name,
        **more,
    )(*args)


def body(n_d, n_f, *args):
    (
        tokens, cotangent, lengths, valid_mask, action_bins, value_head,
        w_triple, w_mixer, w_expand, w_reduce, norm_params,
        first_triple, first_mixer, first_expand, first_reduce, first_norms,
        second_triple, second_mixer, second_expand, second_reduce, second_norms,
    ) = args
    ep, rows, _ = tokens.shape
    flat = ep * rows
    rows16 = -(-rows // 16) * 16
    padded = -(-rows // QB) * QB
    blocks = padded // QB
    me = lax.axis_index("fsdp")
    dp = lax.axis_index("dp")
    core = dp % 2
    idx = jnp.stack([me, core]).astype(jnp.int32)
    shard = D // n_f
    h2 = FF // n_f // 2
    half_ff = FF // 2
    nh = 2 if shard >= 32 else 1
    f_bits, d_bits = axis_bits(n_f), axis_bits(n_d)
    steps_f = lambda v, b: xor_step(v, "fsdp", n_f, b)
    steps_d = lambda v, b: xor_step(v, "dp", n_d, b)

    def own_half(w):
        n = w.shape[0] // nh
        return lax.dynamic_slice_in_dim(w, core * n, n, 0) if nh == 2 else w

    def ff_half(w, h):
        return jnp.concatenate([w[:, (2 * i + h) * h2 : (2 * i + h + 1) * h2] for i in range(n_f)], axis=1)

    def under(w):
        return [w[:, q * D : (q + 1) * D] for q in range(w.shape[1] // D)]

    own_t = own_half(w_triple).astype(BF16)

    def own_piece(expand, reduce, h, first):
        rows_h = slice(h * h2, (h + 1) * h2)
        return jnp.concatenate(
            first + under(ff_half(own_half(expand), h).astype(BF16)) + [own_half(reduce[rows_h]).astype(BF16)],
            axis=0,
        )

    norm_t = norm_params.T
    norm = jnp.concatenate([norm_t, jnp.zeros((4, D), F32)], axis=0)
    ep_block = lambda width: pl.BlockSpec((1, rows, width), lambda e: (e, 0, 0))
    eps = 2 if ep % 2 == 0 else 1
    eps_block = lambda width: pl.BlockSpec((eps, rows, width), lambda e: (e, 0, 0))
    ep_shape = lambda width, dtype: jax.ShapeDtypeStruct((ep, rows, width), dtype)
    low = lambda width: (ep_block(width), ep_shape(width, BF16))
    wide = lambda width: (ep_block(width), ep_shape(width, F32))
    whole = lambda shape: (const_spec(shape), jax.ShapeDtypeStruct(shape, F32))
    norm_spec = const_spec((8, D))
    lse_spec = pl.BlockSpec((1, 16, QUAD), lambda e: (e, 0, 0))
    dma = pltpu.SemaphoreType.DMA
    wt_scratch = pltpu.VMEM((D, 3 * D), BF16)

    near = f_bits[0]
    rels_a = [0]
    for b in f_bits[1:]:
        rels_a = rels_a + [r ^ b for r in rels_a]
    rels_b = [r ^ near for r in rels_a]
    own_t, w_mixer_0, w_expand_0, w_reduce_0 = sync(own_t, w_mixer, w_expand, w_reduce)
    t_got = [steps_f(own_t, r) for r in rels_a[1:]]
    own_a = own_piece(w_expand_0, w_reduce_0, 0, [own_half(w_mixer_0).astype(BF16)])
    own_b = own_piece(w_expand_0, w_reduce_0, 1, [])
    a_near = steps_f(own_a, near)
    t_one = jnp.stack([own_t, *t_got])
    t_one, idx, norm, own_a, own_b, a_near = sync(t_one, idx, norm, own_a, own_b, a_near)
    t_two = steps_f(t_one, near)
    t_refs, t_plan = [t_one], [(rels_a, nh - 1)]
    if nh == 2:
        t_refs.append(steps_d(t_one, 1))
        t_plan.append((rels_a, 2))
    t_two, own_b = sync(t_two, own_b)
    b_near = steps_f(own_b, near)
    a_pair, b_pair = jnp.stack([own_a, a_near]), jnp.stack([own_b, b_near])
    a_got = [steps_f(a_pair, r) for r in rels_a[1:]]
    t_refs.append(t_two)
    t_plan.append((rels_b, nh - 1))
    if nh == 2:
        for i in range(0, len(rels_b), 2):
            t_refs.append(steps_d(t_two[i : i + 2], 1))
            t_plan.append((rels_b[i : i + 2], 2))
    nw = len(t_refs)
    pair_plan = [([0, near], nh - 1)]
    got_plan = [([r, r ^ near], nh - 1) for r in rels_a[1:]]
    a_refs, a_plan = [a_pair], pair_plan + got_plan
    norm, b_pair, *t_refs = sync(norm, b_pair, *t_refs)
    b_refs, b_got = [b_pair], [steps_f(b_pair, r) for r in rels_a[1:]]
    triple, n1, attended, lse = kernel_call(
        functools.partial(f1_kernel, t_plan, nw), "f1", (ep // eps,),
        [SMEM, SMEM, eps_block(D), norm_spec] + [ANY] * nw,
        [
            (eps_block(3 * D), ep_shape(3 * D, BF16)), (eps_block(D), ep_shape(D, BF16)),
            (eps_block(D), ep_shape(D, BF16)),
            (pl.BlockSpec((eps, 16, QUAD), lambda e: (e, 0, 0)), jax.ShapeDtypeStruct((ep, 16, QUAD), F32)),
        ],
        [wt_scratch, pltpu.VMEM((eps, padded, 3 * D), BF16), dma], 60,
        (idx, lengths, tokens, norm, *t_refs),
    )
    attended, *a_got = sync(attended, *a_got)
    a_refs += a_got
    if nh == 2:
        a_refs += [steps_d(v, 1) for v in [a_pair, *a_got]]
        a_plan = a_plan + [(rels, 2) for rels, _ in a_plan]
    na = len(a_refs)
    attended, *a_refs = sync(attended, *a_refs)

    order = f_bits[1:2] + f_bits[:1] + f_bits[2:]
    late = order[2:]
    pos = halving_positions(order)
    hm, hr = shard // nh, h2 // nh
    rows_a = hm * (half_ff // QUAD) + hr * (D // QUAD)
    rows_b = rows_a + hm * (D // QUAD)
    rows_t = 6 * hm
    half = n_f // 2
    low_out = lambda *shape: (const_spec(shape), jax.ShapeDtypeStruct(shape, BF16))
    ff_scratch = [
        pltpu.VMEM((D, D), BF16), pltpu.VMEM((D, half_ff), BF16), pltpu.VMEM((half_ff, D), BF16),
        pltpu.VMEM((D, half_ff), F32), pltpu.VMEM((D, half_ff), F32),
    ]
    fl = flat // 3 if flat % 48 == 0 else rows
    fl_steps = flat // fl
    fl_block = lambda width, at=0: pl.BlockSpec((fl, width), lambda i: (i + at, 0))
    fl_low = lambda width: (fl_block(width), jax.ShapeDtypeStruct((flat, width), BF16))
    fl_wide = lambda width: (fl_block(width), jax.ShapeDtypeStruct((flat, width), F32))
    tok_flat = tokens.reshape(flat, D)
    cot_flat = cotangent.reshape(flat, D)
    attended = attended.reshape(flat, D)
    hidden, out_part, g2_part, n2, keep_a, send_a = kernel_call(
        functools.partial(f2a_kernel, a_plan, na, pos, rows), "f2a", (fl_steps,),
        [SMEM, SMEM] + [fl_block(D)] * 3 + [norm_spec] + [ANY] * na,
        [fl_wide(D)] * 3 + [fl_low(D)] + [low_out(nh, half, rows_a, QUAD)] * 2,
        ff_scratch + [pltpu.SemaphoreType.DMA((2,))], 60, (idx, lengths, attended, tok_flat, cot_flat, norm, *a_refs),
    )

    def halves(keep, got):
        n = keep.shape[-3] // 2
        return add_low(keep[..., :n, :, :], got[..., :n, :, :]), add_low(keep[..., n:, :, :], got[..., n:, :, :])

    def core_pair(total):
        return (total[0], steps_d(total[1], 1)) if nh == 2 else (total[0], None)

    def core_halves_of(pair):
        mine, other = pair
        n = mine.shape[0] // 2
        return halves(mine, other) if other is not None else (mine[:n], mine[n:])

    def core_add(pair):
        return add_low(*pair) if pair[1] is not None else pair[0]

    n2, keep_a, send_a, *b_got = sync(n2, keep_a, send_a, *b_got)
    b_refs += b_got
    if nh == 2:
        b_refs += [steps_d(v, 1) for v in [b_pair, *b_got]]
    n2, keep_a, send_a, *b_refs = sync(n2, keep_a, send_a, *b_refs)
    got_a = steps_f(send_a, order[0])
    block_out, gh, ga, *rest = kernel_call(
        functools.partial(f2b_kernel, a_plan, na, pos, nh, rows), "f2b", (fl_steps,),
        [SMEM, SMEM] + [fl_block(D)] * 6 + [norm_spec] + [ANY] * (2 * na),
        [fl_low(D), fl_wide(D), fl_low(D)] + [low_out(n_f, rows_b, QUAD)] * nh + [whole((8, D))],
        ff_scratch + [pltpu.VMEM((D, D), F32), pltpu.SemaphoreType.DMA((2,))], 54,
        (idx, lengths, attended, hidden, out_part, g2_part, n2, cot_flat, norm, *a_refs, *b_refs),
    )
    grads_b, ln2 = rest[:nh], rest[nh]
    ga, valid_mask, action_bins, keep_a, got_a, *grads_b = sync(
        ga, valid_mask, action_bins, keep_a, got_a, *grads_b
    )
    pair_b = core_pair(grads_b)
    places = jnp.arange(rows)
    inside = places[None, :] < lengths[:, None]
    counted = ((valid_mask == 1) & inside).astype(jnp.int32).reshape(1, flat)
    bins_t = action_bins.reshape(flat, ACT).T
    sum_a = add_low(keep_a, got_a)
    pair_a = core_pair(sum_a)
    keep_b, send_b = core_halves_of(pair_b)
    keep_a, send_a = core_halves_of(pair_a)
    ga, counted, bins_t, keep_a, send_a, keep_b, send_b = sync(ga, counted, bins_t, keep_a, send_a, keep_b, send_b)

    got_b = steps_f(send_b, order[0])
    got_a = steps_f(send_a, order[1])
    pack_rows = ep * rows16 + PACK
    gtri, *grads_t = kernel_call(
        functools.partial(b1_kernel, pos, nh), "b1", (ep // eps,),
        [SMEM, SMEM, eps_block(3 * D), eps_block(D), pl.BlockSpec((eps, 16, QUAD), lambda e: (e, 0, 0)), eps_block(D)],
        [(eps_block(3 * D), ep_shape(3 * D, BF16))] + [low_out(n_f, rows_t, QUAD)] * nh,
        [
            pltpu.VMEM((eps, padded, 3 * D), BF16), pltpu.VMEM((eps, padded, D), BF16),
            pltpu.VMEM((eps, padded, 3 * D), BF16), pltpu.VMEM((eps, rows16, D), F32),
            pltpu.VMEM((eps, rows16, D), F32), pltpu.VMEM((D, 3 * D), F32),
            pltpu.VMEM((pack_rows, D), BF16), pltpu.VMEM((pack_rows, 3 * D), BF16),
        ],
        48, (idx, lengths, triple, ga.reshape(ep, rows, D), lse, n1),
    )
    gtri, keep_a, got_a, keep_b, got_b, *grads_t = sync(gtri, keep_a, got_a, keep_b, got_b, *grads_t)

    mine_t, other_t = core_pair(grads_t)
    keep_b, send_b = halves(keep_b, got_b)
    if late:
        keep_a, send_a = halves(keep_a, got_a)
    else:
        keep_a, send_a = add_low(keep_a, got_a), keep_a
    mine_t, other_t, keep_a, send_a, keep_b, send_b = sync(mine_t, other_t, keep_a, send_a, keep_b, send_b)
    keep_t, send_t = core_halves_of((mine_t, other_t))
    block_out, keep_t, send_t, keep_a, send_a, keep_b, send_b = sync(
        block_out, keep_t, send_t, keep_a, send_a, keep_b, send_b
    )
    got_t = steps_f(send_t, order[0])
    got_b = steps_f(send_b, order[1])
    if late:
        got_a = steps_f(send_a, late[0])

    qb = 256
    steps = -(-flat // qb)
    q_sum, q_top = kernel_call(
        functools.partial(q_kernel, flat), "qstat", (steps,),
        [
            pl.BlockSpec((qb, D), lambda i: (i, 0)), const_spec((ACT * NBINS, D)),
            pl.BlockSpec((ACT, qb), lambda i: (0, i)), pl.BlockSpec((1, qb), lambda i: (0, i)),
        ],
        [whole((16, qb))] * 2, [], 20, (block_out, value_head, bins_t, counted),
    )
    gtri, q_sum, keep_t, got_t, keep_b, got_b = sync(gtri, q_sum, keep_t, got_t, keep_b, got_b)

    def b2_call(at, n, gtri, prior, more_in):
        extra = [] if prior is None else [prior, *more_in]
        specs = [] if prior is None else [ANY] + [const_spec(v.shape) for v in more_in]
        more = {} if prior is None else {"input_output_aliases": {5 + nw: 0}}
        return kernel_call(
            functools.partial(b2_kernel, t_plan, nw, prior is None), "b2", (n,),
            [SMEM, fl_block(3 * D, at), fl_block(D, at), fl_block(D, at), norm_spec] + [ANY] * nw + specs,
            [(fl_block(D, at), jax.ShapeDtypeStruct((flat, D), BF16)), whole((8, D))],
            [wt_scratch, dma], 28, (idx, gtri, tok_flat, gh, norm, *t_refs, *extra), **more,
        )

    keep_t, send_t = halves(keep_t, got_t)
    if late:
        keep_b, send_b = halves(keep_b, got_b)
    else:
        keep_b, send_b = add_low(keep_b, got_b), keep_b
    gtri_flat = gtri.reshape(flat, 3 * D)

    def finish(keep, bits):
        for b in bits:
            n = keep.shape[0] // 2
            keep = add_low(keep[:n], steps_f(keep[n:], b))
        return keep[0]

    x_bits = d_bits[nh - 1 :]

    def before_x(keep):
        red = finish(keep, late[1:])
        for b in x_bits[:-1]:
            red = add_low(red, steps_d(red, b))
        return red

    if late:
        keep_a = add_low(keep_a, got_a)
    red_a = before_x(keep_a)
    gtri_flat, keep_t, send_t, keep_b, send_b, red_a = sync(gtri_flat, keep_t, send_t, keep_b, send_b, red_a)
    got_t = steps_f(send_t, order[1])
    if late:
        got_b = steps_f(send_b, late[0])
    cut = (fl_steps + 1) // 2
    got_ra = steps_d(red_a, x_bits[-1])
    ig_part, ln1_a = b2_call(0, cut, gtri_flat, None, ())
    ig_part, keep_t, got_t, got_ra, keep_b, *got_b = sync(
        ig_part, keep_t, got_t, got_ra, keep_b, *([got_b] if late else [])
    )
    if late:
        keep_t, send_t = halves(keep_t, got_t)
        keep_b = add_low(keep_b, got_b[0])
    else:
        keep_t = add_low(keep_t, got_t)
    red_b = before_x(keep_b)
    red_b, keep_t, ig_part = sync(red_b, keep_t, ig_part)
    if late:
        got_t = steps_f(send_t, late[0])
    got_rb = steps_d(red_b, x_bits[-1])
    input_grad, small = b2_call(cut, fl_steps - cut, gtri_flat, ig_part, (ln1_a, ln2, q_sum, q_top))
    small, red_a, got_ra, red_b, got_rb, keep_t, *got_t = sync(
        small, red_a, got_ra, red_b, got_rb, keep_t, *([got_t] if late else [])
    )

    red_t = before_x(add_low(keep_t, got_t[0]) if late else keep_t)
    got_rt = steps_d(red_t, x_bits[-1])
    both_sum = lambda a, b: a.astype(F32) + b.astype(F32)
    red = jnp.concatenate([both_sum(red_a, got_ra), both_sum(red_b, got_rb)], axis=0)
    red_parts = [red] + ([steps_d(red, 1)] if nh == 2 else [])
    small_core = steps_d(small, d_bits[0])
    red_t, *red_parts = sync(red_t, *red_parts)
    like = lambda w: whole(w.shape)
    full = lambda *ws: [pl.BlockSpec(memory_space=pltpu.VMEM)] * len(ws)
    mlp_state = (
        w_mixer, first_mixer, second_mixer, w_expand, first_expand, second_expand,
        w_reduce, first_reduce, second_reduce,
    )
    *mlp_out, sq_mlp = kernel_call(
        functools.partial(lamb_mlp_kernel, n_f, nh, rows_a), "lamb_mlp", (1,),
        [SMEM] + full(*red_parts, *mlp_state),
        [like(w) for w in (w_mixer, w_expand, w_reduce) for _ in range(3)] + [whole((8, 128))],
        [], 20, (idx, *red_parts, *mlp_state),
    )
    small, small_core, sq_mlp, red_t, got_rt = sync(small, small_core, sq_mlp, red_t, got_rt)
    small = merge_small(small, small_core)
    for b in d_bits[1:]:
        small = merge_small(small, steps_d(small, b))
    red_t = red_t.astype(F32) + got_rt.astype(F32)
    parts_t = [red_t] + ([steps_d(red_t, 1)] if nh == 2 else [])
    tri_state = (w_triple, first_triple, second_triple)
    *tri_out, squares = kernel_call(
        functools.partial(lamb_triple_kernel, n_f, nh), "lamb_triple", (1,),
        [SMEM] + full(*parts_t, sq_mlp, *tri_state),
        [like(w_triple)] * 3 + [whole((8, 128))],
        [], 12, (idx, *parts_t, sq_mlp, *tri_state),
    )

    small = small + jnp.pad(squares, ((0, 0), (0, D - 128)))
    for b in f_bits[:-2]:
        small = merge_small(small, steps_f(small, b))
    far = [0]
    for b in f_bits[-2:]:
        far = far + [r ^ b for r in far]
    smalls = [small] + [steps_f(small, r) for r in far[1:]]
    masters = (w_triple, w_mixer, w_expand, w_reduce)
    updates = (tri_out[2], mlp_out[2], mlp_out[5], mlp_out[8])
    firsts_t, seconds_t = first_norms.T, second_norms.T
    *news, norms_out, first_out, second_out, norm_table, mean, peak = kernel_call(
        functools.partial(final_kernel, len(smalls)), "final", (1,),
        full(*smalls, norm_t, firsts_t, seconds_t, *masters, *updates),
        [like(w) for w in masters]
        + [whole((4, D))] * 3 + [whole((2, 8)), whole((1, ACT)), whole((1, ACT))],
        [], 16, (*smalls, norm_t, firsts_t, seconds_t, *masters, *updates),
    )
    return (
        block_out.reshape(ep, rows, D), input_grad.reshape(ep, rows, D), *news,
        tri_out[0], mlp_out[0], mlp_out[3], mlp_out[6],
        tri_out[1], mlp_out[1], mlp_out[4], mlp_out[7],
        norms_out.T, first_out.T, second_out.T, norm_table, mean.reshape(ACT), peak.reshape(ACT),
    )


def solution(mesh):
    n_d, n_f = mesh.shape["dp"], mesh.shape["fsdp"]
    both = ("dp", "fsdp")
    row, rep = P("fsdp", None), P()
    in_specs = (
        P(both, None, None), P(both, None, None), P(both), P(both, None), P(both, None, None), rep,
        row, row, row, row, rep,
        row, row, row, row, rep,
        row, row, row, row, rep,
    )
    out_specs = (
        (P(both, None, None),) * 2 + (row,) * 12 + (rep,) * 6
    )
    return jax.shard_map(
        functools.partial(body, n_d, n_f), mesh=mesh, in_specs=in_specs, out_specs=out_specs,
        check_vma=False,
    )
```

```python
import functools

import jax
import jax.numpy as jnp
from jax import lax
from jax.experimental import pallas as pl
from jax.experimental.pallas import tpu as pltpu
from jax.sharding import PartitionSpec as P

HEADS = 8
HEAD_DIM = 64
ACT = 11
NBINS = 256
STEP = 5

NORM_EPSILON = 1e-05
BETA_FIRST = 0.9
BETA_SECOND = 0.999
ADAM_EPSILON = 1e-06
RATIO_EPSILON = 1e-06
WEIGHT_DECAY = 0.01
LEARNING_RATE = 0.5
MASKED = -1e30

D = 512
FF = 2048
QB = 64
PACK = 256
QUAD = 256
F32 = jnp.float32
BF16 = jnp.bfloat16
MIB = 1024 * 1024

NT = (((1,), (1,)), ((), ()))
NN = (((1,), (0,)), ((), ()))
TN = (((0,), (0,)), ((), ()))


def mm(a, b, dims=NN):
    return lax.dot_general(a, b, dims, preferred_element_type=F32)


def pad_rows(v, rows):
    if v.shape[0] == rows:
        return v
    return jnp.concatenate([v, jnp.zeros((rows - v.shape[0], v.shape[1]), v.dtype)], axis=0)


def ln_parts(x):
    center = x - jnp.mean(x, axis=-1, keepdims=True)
    spread = jnp.mean(center * center, axis=-1, keepdims=True)
    rstd = lax.rsqrt(spread + NORM_EPSILON)
    return center * rstd, rstd


def ln_back(grad, xhat, rstd, gain):
    t = grad * gain
    m1 = jnp.mean(t, axis=-1, keepdims=True)
    m2 = jnp.mean(t * xhat, axis=-1, keepdims=True)
    return rstd * (t - m1 - xhat * m2)


def head_masks():
    lane = lax.broadcasted_iota(jnp.int32, (1, QUAD), 1)
    return [jnp.where(lane // HEAD_DIM == h, 1.0, 0.0).astype(BF16) for h in range(4)]


def stack_heads(block, masks):
    return jnp.concatenate([block * m for m in masks], axis=0)


def own_lanes(t):
    head = lax.broadcasted_iota(jnp.int32, (QB, QUAD), 1) // HEAD_DIM
    out = t[0:QB]
    for h in range(1, 4):
        out = jnp.where(head == h, t[QB * h : QB * (h + 1)], out)
    return out


def place(block, size, side, core):
    if side == 0:
        return pl.multiple_of(block * size, size)
    c = core if side == 1 else 1 - core
    return pl.multiple_of(block * (2 * size) + c * size, size)


def run_copies(copies, start):
    for copy in copies:
        copy.start() if start else copy.wait()


def load_triple(refs, plan, dst, sem, me, core, start):
    for ref, (rels, side) in zip(refs, plan):
        half = ref.shape[1]
        for p, rel in enumerate(rels):
            row = place(jnp.bitwise_xor(me, rel), half, side, core)
            run_copies([pltpu.make_async_copy(ref.at[p], dst.at[pl.ds(row, half)], sem)], start)


def load_mixer(refs, plan, wm, sem, me, core, start):
    for ref, (rels, side) in zip(refs, plan):
        hm = D // wm_blocks(plan) // (1 if side == 0 else 2)
        for p, rel in enumerate(rels):
            row = place(jnp.bitwise_xor(me, rel), hm, side, core)
            run_copies([pltpu.make_async_copy(ref.at[p, pl.ds(0, hm)], wm.at[pl.ds(row, hm)], sem)], start)


def wm_blocks(plan):
    return sum(len(rels) for rels, side in plan if side != 2)


def load_ff(refs, plan, at_mixer, we, wr, sem, me, core, start):
    for ref, (rels, side) in zip(refs, plan):
        halves = 1 if side == 0 else 2
        hm = D // wm_blocks(plan) // halves
        hr = wr.shape[0] // wm_blocks(plan) // halves
        nc = we.shape[1] // D
        at = hm if at_mixer else 0
        for p, rel in enumerate(rels):
            block = jnp.bitwise_xor(me, rel)
            row, rowr = place(block, hm, side, core), place(block, hr, side, core)
            copies = []
            for q in range(nc):
                copies.append(
                    pltpu.make_async_copy(
                        ref.at[p, pl.ds(at + hm * q, hm)],
                        we.at[pl.ds(row, hm), pl.ds(q * D, D)],
                        sem,
                    )
                )
            copies.append(
                pltpu.make_async_copy(ref.at[p, pl.ds(at + hm * nc, hr)], wr.at[pl.ds(rowr, hr)], sem)
            )
            run_copies(copies, start)


def f1_kernel(plan, nw, idx, lens, tok, norm, *refs):
    w_refs, (tri_out, n1_out, att_out, lse_out, wt, tri, sem) = refs[:nw], refs[nw:]
    e = pl.program_id(0)
    count, rows = tok.shape[:2]
    padded = tri.shape[1]
    rows16 = -(-rows // 16) * 16

    @pl.when(e == 0)
    def _():
        load_triple(w_refs, plan, wt, sem, idx[0], idx[1], True)
        tri[:, rows16:padded] = jnp.zeros((count, padded - rows16, 3 * D), BF16)
        load_triple(w_refs, plan, wt, sem, idx[0], idx[1], False)

    for i in range(count):
        xhat, _ = ln_parts(pad_rows(tok[i].astype(F32), rows16))
        n1 = (xhat * norm[0:1] + norm[1:2]).astype(BF16)
        n1_out[i] = n1[:rows]
        t = mm(n1, wt[...]).astype(BF16)
        tri[i, 0:rows16, 0:D] = t[:, 0:D] * jnp.asarray(HEAD_DIM**-0.5, BF16)
        tri[i, 0:rows16, D:] = t[:, D:]
        tri_out[i] = tri[i, 0:rows]

    masks = head_masks()
    lane = lax.broadcasted_iota(jnp.int32, (1, QUAD), 1) % QB
    blocks = -(-rows // QB)
    chains = [
        (i, j, g * QUAD, g * blocks + j)
        for i in range(count) for j in range(blocks) for g in range(HEADS // 4)
    ]
    exts = [min(QB * (j + 1), rows16) for _, j, _, _ in chains]
    q4 = [stack_heads(tri[i, QB * j : QB * (j + 1), gl : gl + QUAD], masks) for i, j, gl, _ in chains]
    s = [mm(tri[i, 0:x, D + gl : D + gl + QUAD], q, NT) for (i, _, gl, _), x, q in zip(chains, exts, q4)]
    pb = []
    for (i, j, _, at), x, v in zip(chains, exts, s):
        kmax = jnp.minimum(lane + QB * j, lens[e * count + i] - 1)
        krow = lax.broadcasted_iota(jnp.int32, (x, QUAD), 0)
        v = jnp.where(krow <= kmax, v, MASKED)
        m = jnp.max(v, axis=0, keepdims=True)
        p = jnp.exp(v - m)
        total = jnp.sum(p, axis=0, keepdims=True)
        lse_out[i, pl.ds(at, 1), :] = m + jnp.log(total)
        pb.append((p * (1.0 / total)).astype(BF16))
    o = [mm(v, tri[i, 0:x, 2 * D + gl : 2 * D + gl + QUAD], TN) for (i, _, gl, _), x, v in zip(chains, exts, pb)]
    for (i, j, gl, _), v in zip(chains, o):
        live = min(QB, rows - QB * j)
        att_out[i, QB * j : QB * j + live, gl : gl + QUAD] = own_lanes(v).astype(BF16)[:live]


def put_rows(dst, at_index, at, src, row, rows):
    for q in range(src.shape[1] // QUAD):
        dst[(*at_index, slice(at, at + rows))] = src[pl.ds(row, rows), q * QUAD : (q + 1) * QUAD].astype(BF16)
        at += rows
    return at


def put_ff_grads(target, halves, pos, idx, acc_e, acc_r, wr, acc_m=None):
    hm = D // len(pos) // halves
    hr = wr.shape[0] // len(pos) // halves
    for c in range(wr.shape[0] // D):
        wr[c * D : c * D + D] = acc_r[:, c * D : c * D + D].T.astype(BF16)
    for p, rel in enumerate(pos):
        block = jnp.bitwise_xor(idx[0], rel)
        for c in range(halves):
            side = 0 if halves == 1 else c + 1
            dst, where = target(c, p)
            row, rowr = place(block, hm, side, idx[1]), place(block, hr, side, idx[1])
            at = put_rows(dst, where, 0, acc_e, row, hm)
            at = put_rows(dst, where, at, wr, rowr, hr)
            if acc_m is not None:
                put_rows(dst, where, at, acc_m, row, hm)


def ff_chunks(n2, glow, out, g2, we, wr, acc_e, acc_r):
    for c in range(we.shape[1] // D):
        cs = slice(c * D, c * D + D)
        ex = mm(n2, we[:, cs])
        phi = 0.5 + 0.5 * lax.erf(ex * 0.7071067811865476)
        act = (ex * phi).astype(BF16)
        gp = phi + ex * (jnp.exp(-0.5 * ex * ex) * 0.3989422804014327)
        out = out + mm(act, wr[cs])
        gact = mm(glow, wr[cs], NT)
        ge = (gp * gact).astype(BF16)
        back = mm(ge, we[:, cs], NT)
        g2 = back if g2 is None else g2 + back
        acc_r[:, cs] += mm(glow, act, TN)
        acc_e[:, cs] += mm(n2, ge, TN)
    return out, g2


def live_rows(cot, lens, rows, step):
    count = cot.shape[0] // rows
    row = lax.broadcasted_iota(jnp.int32, (cot.shape[0], 1), 0)
    live = None
    for i in range(count):
        inside = (row >= i * rows) & (row < i * rows + lens[step * count + i])
        live = inside if live is None else live | inside
    return cot * jnp.where(live, 1.0, 0.0).astype(BF16)


def f2a_kernel(plan, nw, pos, rows, idx, lens, att_ref, tok, cot, norm, *refs):
    w_refs, refs = refs[:nw], refs[nw:]
    hid_out, out_out, g2_out, n2_out, keep, send, wm, we, wr, acc_e, acc_r, sem = refs
    s = pl.program_id(0)

    @pl.when(s == 0)
    def _():
        load_mixer(w_refs, plan, wm, sem.at[0], idx[0], idx[1], True)
        load_ff(w_refs, plan, True, we, wr, sem.at[1], idx[0], idx[1], True)
        acc_e[...] = jnp.zeros_like(acc_e)
        acc_r[...] = jnp.zeros_like(acc_r)
        load_mixer(w_refs, plan, wm, sem.at[0], idx[0], idx[1], False)

    glow = live_rows(cot[...], lens, rows, s)
    hidden = tok[...].astype(F32) + mm(att_ref[...], wm[...])
    xhat, _ = ln_parts(hidden)
    n2 = (xhat * norm[2:3] + norm[3:4]).astype(BF16)
    hid_out[...] = hidden
    n2_out[...] = n2

    @pl.when(s == 0)
    def _():
        load_ff(w_refs, plan, True, we, wr, sem.at[1], idx[0], idx[1], False)

    out, g2 = ff_chunks(n2, glow, hidden, None, we, wr, acc_e, acc_r)
    out_out[...] = out
    g2_out[...] = g2

    @pl.when(s == pl.num_programs(0) - 1)
    def _():
        half = len(pos) // 2
        target = lambda c, p: (keep if p < half else send, (c, p % half))
        put_ff_grads(target, keep.shape[0], pos, idx, acc_e, acc_r, wr)


def f2b_kernel(plan, nw, pos, nh, rows, idx, lens, att_ref, hid, out_ref, g2_ref, n2_ref, cot, norm, *refs):
    w_refs, b_refs, refs = refs[:nw], refs[nw : 2 * nw], refs[2 * nw :]
    (block_out, gh_out, ga_out), grads, refs = refs[:3], refs[3 : 3 + nh], refs[3 + nh :]
    ln_out, wm, we, wr, acc_e, acc_r, acc_m, sem = refs
    s = pl.program_id(0)

    @pl.when(s == 0)
    def _():
        load_ff(b_refs, plan, False, we, wr, sem.at[1], idx[0], idx[1], True)
        load_mixer(w_refs, plan, wm, sem.at[0], idx[0], idx[1], True)
        acc_e[...] = jnp.zeros_like(acc_e)
        acc_r[...] = jnp.zeros_like(acc_r)
        acc_m[...] = jnp.zeros_like(acc_m)
        ln_out[...] = jnp.zeros_like(ln_out)
        load_ff(b_refs, plan, False, we, wr, sem.at[1], idx[0], idx[1], False)

    gain = norm[2:3]
    glow = live_rows(cot[...], lens, rows, s)
    out, g2 = ff_chunks(n2_ref[...], glow, out_ref[...], g2_ref[...], we, wr, acc_e, acc_r)
    block_out[...] = out.astype(BF16)
    xhat, rstd = ln_parts(hid[...])
    gh = glow.astype(F32) + ln_back(g2, xhat, rstd, gain)
    ln_out[0:1] += jnp.sum(g2 * xhat, axis=0, keepdims=True)
    ln_out[1:2] += jnp.sum(g2, axis=0, keepdims=True)

    @pl.when(s == 0)
    def _():
        load_mixer(w_refs, plan, wm, sem.at[0], idx[0], idx[1], False)

    gb = gh.astype(BF16)
    gh_out[...] = gh
    acc_m[...] += mm(att_ref[...], gb, TN)
    ga_out[...] = mm(gb, wm[...], NT).astype(BF16)

    @pl.when(s == pl.num_programs(0) - 1)
    def _():
        put_ff_grads(lambda c, p: (grads[c], (p,)), nh, pos, idx, acc_e, acc_r, wr, acc_m)


def b1_kernel(pos, nh, idx, lens, tri_ref, ga_ref, lse, n1, gtri_out, *refs):
    grads, (tri, ga, gtri, dk, dv, acc, n1p, gtp) = refs[:nh], refs[nh:]
    e = pl.program_id(0)
    last = pl.num_programs(0) - 1
    count, rows = n1.shape[:2]
    padded = tri.shape[1]
    rows16 = -(-rows // 16) * 16
    low16 = rows // 16 * 16

    @pl.when(e == 0)
    def _():
        acc[...] = jnp.zeros_like(acc)
        tri[:, low16:padded] = jnp.zeros((count, padded - low16, 3 * D), BF16)
        ga[:, low16:padded] = jnp.zeros((count, padded - low16, D), BF16)

    for i in range(count):
        tri[i, 0:rows] = tri_ref[i]
        ga[i, 0:rows] = ga_ref[i]
    dk[...] = jnp.zeros_like(dk)
    dv[...] = jnp.zeros_like(dv)
    gtri[:, :, 0:D] = jnp.zeros((count, padded, D), BF16)

    lengths = [lens[e * count + i] for i in range(count)]
    masks = head_masks()
    lane = lax.broadcasted_iota(jnp.int32, (1, QUAD), 1) % QB
    blocks = -(-rows // QB)

    def run(chains):
        chains = [(i, j, g * QUAD, g * blocks + j) for i, j in chains for g in range(HEADS // 4)]
        exts = [min(QB * (j + 1), rows16) for _, j, _, _ in chains]
        q4 = [stack_heads(tri[i, QB * j : QB * (j + 1), gl : gl + QUAD], masks) for i, j, gl, _ in chains]
        do4 = [stack_heads(ga[i, QB * j : QB * (j + 1), gl : gl + QUAD], masks) for i, j, gl, _ in chains]
        s = [mm(tri[i, 0:x, D + gl : D + gl + QUAD], q, NT) for (i, _, gl, _), x, q in zip(chains, exts, q4)]
        dp = [mm(tri[i, 0:x, 2 * D + gl : 2 * D + gl + QUAD], d, NT) for (i, _, gl, _), x, d in zip(chains, exts, do4)]
        p = []
        for (i, j, _, at), x, v in zip(chains, exts, s):
            kmax = jnp.minimum(lane + QB * j, lengths[i] - 1)
            krow = lax.broadcasted_iota(jnp.int32, (x, QUAD), 0)
            p.append(jnp.exp(jnp.where(krow <= kmax, v - lse[i, pl.ds(at, 1), :], MASKED)))
        ds = []
        for v, w in zip(p, dp):
            delta = jnp.sum(v * w, axis=0, keepdims=True)
            ds.append((v * (w - delta)).astype(BF16))
        for (i, _, gl, _), x, v, d in zip(chains, exts, p, do4):
            dv[i, 0:x, gl : gl + QUAD] += mm(v.astype(BF16), d)
        dq = [mm(v, tri[i, 0:x, D + gl : D + gl + QUAD], TN) for (i, _, gl, _), x, v in zip(chains, exts, ds)]
        for (i, _, gl, _), x, v, q in zip(chains, exts, ds, q4):
            dk[i, 0:x, gl : gl + QUAD] += mm(v, q)
        for (i, j, gl, _), v in zip(chains, dq):
            gtri[i, QB * j : QB * (j + 1), gl : gl + QUAD] = (own_lanes(v) * HEAD_DIM**-0.5).astype(BF16)

    run([(i, j) for i in range(count) for j in range(min(2, blocks))])
    for i in range(count):
        for j in range(2, blocks, 2):

            @pl.when(lengths[i] > QB * j)
            def _(i=i, j=j):
                run([(i, k) for k in range(j, min(j + 2, blocks))])

    start = jnp.int32(0)
    for i in range(lens.shape[0] - count):
        start = start + jnp.where(i < e * count, (lens[i] + 15) // 16, 0)
    for i in range(count):
        gtri[i, 0:rows16, D : 2 * D] = dk[i].astype(BF16)
        gtri[i, 0:rows16, 2 * D :] = dv[i].astype(BF16)
        gtri_out[i] = gtri[i, 0:rows]
        at = pl.multiple_of(start * 16, 16)
        n1p[pl.ds(at, rows16)] = pad_rows(n1[i], rows16)
        gtp[pl.ds(at, rows16)] = gtri[i, 0:rows16]
        start = start + (lengths[i] + 15) // 16

    @pl.when(e == last)
    def _():
        end = pl.multiple_of(at + rows16, 16)
        n1p[pl.ds(end, PACK)] = jnp.zeros((PACK, D), BF16)
        gtp[pl.ds(end, PACK)] = jnp.zeros((PACK, 3 * D), BF16)

        def chunk(i, carry):
            row = pl.multiple_of(i * PACK, PACK)
            acc[...] += mm(n1p[pl.ds(row, PACK)], gtp[pl.ds(row, PACK)], TN)
            return carry

        lax.fori_loop(0, (start * 16 + PACK - 1) // PACK, chunk, 0)
        hm = D // len(pos) // nh
        for p, rel in enumerate(pos):
            block = jnp.bitwise_xor(idx[0], rel)
            for c in range(nh):
                side = 0 if nh == 1 else c + 1
                put_rows(grads[c], (p,), 0, acc, place(block, hm, side, idx[1]), hm)


def b2_kernel(plan, nw, first, idx, gtri, tok, gh, norm, *refs):
    w_refs, refs = refs[:nw], refs[nw:]
    if first:
        ig_out, ln_out, wt, sem = refs
    else:
        _, ln1_a, ln2, q_sum, q_top, ig_out, ln_out, wt, sem = refs
    s = pl.program_id(0)

    @pl.when(s == 0)
    def _():
        load_triple(w_refs, plan, wt, sem, idx[0], idx[1], True)
        ln_out[...] = jnp.zeros_like(ln_out)
        load_triple(w_refs, plan, wt, sem, idx[0], idx[1], False)

    g1 = mm(gtri[...], wt[...], NT)
    xhat, rstd = ln_parts(tok[...].astype(F32))
    ig_out[...] = (gh[...] + ln_back(g1, xhat, rstd, norm[0:1])).astype(BF16)
    ln_out[0:1] += jnp.sum(g1 * xhat, axis=0, keepdims=True)
    ln_out[1:2] += jnp.sum(g1, axis=0, keepdims=True)

    if not first:

        @pl.when(s == pl.num_programs(0) - 1)
        def _():
            ln_out[0:2] += ln1_a[0:2]
            ln_out[2:4] = ln2[0:2]
            ln_out[4:5, 0:16] = jnp.sum(q_sum[...].T, axis=0, keepdims=True)
            ln_out[5:6, 0:16] = jnp.max(q_top[...].T, axis=0, keepdims=True)


def q_kernel(total_rows, bo, vh, bins, cnt, sum_out, top_out):
    s = pl.program_id(0)
    block = bo.shape[0]

    @pl.when(s == 0)
    def _():
        sum_out[...] = jnp.zeros_like(sum_out)
        top_out[...] = jnp.full_like(top_out, MASKED)

    place = lax.broadcasted_iota(jnp.int32, (1, block), 1) + s * block
    counted = (cnt[...] > 0) & (place < total_rows)
    binrow = lax.broadcasted_iota(jnp.int32, (NBINS, block), 0)
    for a in range(ACT):
        sc = mm(vh[a * NBINS : (a + 1) * NBINS], bo[...], NT)
        picked = jnp.sum(jnp.where(binrow == bins[a : a + 1], sc, 0.0), axis=0, keepdims=True)
        sum_out[a : a + 1] += jnp.where(counted, picked, 0.0)
        top_out[a : a + 1] = jnp.maximum(top_out[a : a + 1], jnp.where(counted, picked, MASKED))
    sum_out[ACT : ACT + 1] += jnp.where(counted, 1.0, 0.0)


def lamb_moments(weight, gradient, moment_one, moment_two):
    first_new = BETA_FIRST * moment_one + (1.0 - BETA_FIRST) * gradient
    second_new = BETA_SECOND * moment_two + (1.0 - BETA_SECOND) * gradient * gradient
    update = (
        first_new
        * (1.0 / (1.0 - BETA_FIRST**STEP))
        / (jnp.sqrt(second_new * (1.0 / (1.0 - BETA_SECOND**STEP))) + ADAM_EPSILON)
        + WEIGHT_DECAY * weight
    )
    return (first_new, second_new, update)


class Squares:
    def __init__(self):
        self.total = jnp.zeros((8, 128), F32)

    def add(self, lane, weight, update):
        rows = lax.broadcasted_iota(jnp.int32, (8, 128), 0)
        lanes = lax.broadcasted_iota(jnp.int32, (8, 128), 1)
        for row, v in ((6, weight), (7, update)):
            one = jnp.sum(jnp.sum(v * v, axis=0, keepdims=True), axis=1, keepdims=True)
            self.total = self.total + jnp.where((rows == row) & (lanes == lane), one, 0.0)


def lamb_piece(state, outs, grad, rows, cols, squares, lane):
    weight = state[0][rows, cols]
    first_new, second_new, update = lamb_moments(weight, grad, state[1][rows, cols], state[2][rows, cols])
    for out, v in zip(outs, (first_new, second_new, update)):
        out[rows, cols] = v
    squares.add(lane, weight, update)


def core_halves(idx, parts):
    if len(parts) == 1:
        return [lambda rows: parts[0][rows]]
    own = idx[1] == 0
    return [
        lambda rows: jnp.where(own, parts[0][rows], parts[1][rows]),
        lambda rows: jnp.where(own, parts[1][rows], parts[0][rows]),
    ]


def lamb_mlp_kernel(n_f, nh, rows_a, idx, *refs):
    parts, refs = refs[:nh], refs[nh:]
    states = [refs[3 * i : 3 * i + 3] for i in range(3)]
    outs = [refs[9 + 3 * i : 12 + 3 * i] for i in range(3)]
    sq_out = refs[18]
    hm = D // n_f // nh
    h2 = FF // n_f // 2
    hr = h2 // nh
    ne, nd = FF // 2 // QUAD, D // QUAD
    squares = Squares()
    for c, take in enumerate(core_halves(idx, parts)):
        rows = slice(c * hm, c * hm + hm)
        for q in range(nd):
            at = 2 * rows_a + hm * q
            grad = take(slice(at, at + hm))
            lamb_piece(states[0], outs[0], grad, rows, slice(q * QUAD, (q + 1) * QUAD), squares, 1)
        for h in range(2):
            for q in range(ne):
                at = rows_a * h + hm * q
                grad = take(slice(at, at + hm))
                for k in range(QUAD // h2):
                    i = q * (QUAD // h2) + k
                    col = (2 * i + h) * h2
                    lamb_piece(
                        states[1], outs[1], grad[:, k * h2 : (k + 1) * h2], rows,
                        slice(col, col + h2), squares, 2,
                    )
            for q in range(nd):
                at = rows_a * h + hm * ne + hr * q
                grad = take(slice(at, at + hr))
                row = h * h2 + c * hr
                lamb_piece(
                    states[2], outs[2], grad, slice(row, row + hr),
                    slice(q * QUAD, (q + 1) * QUAD), squares, 3,
                )
    sq_out[...] = squares.total


def lamb_triple_kernel(n_f, nh, idx, *refs):
    parts, refs = refs[:nh], refs[nh:]
    sq_in, state, outs, sq_out = refs[0], refs[1:4], refs[4:7], refs[7]
    hm = D // n_f // nh
    squares = Squares()
    for c, take in enumerate(core_halves(idx, parts)):
        for q in range(3 * D // QUAD):
            lamb_piece(
                state, outs, take(slice(hm * q, hm * q + hm)), slice(c * hm, c * hm + hm),
                slice(q * QUAD, (q + 1) * QUAD), squares, 0,
            )
    sq_out[...] = squares.total + sq_in[...]


def merge_small(mine, other):
    row = lax.broadcasted_iota(jnp.int32, mine.shape, 0)
    return jnp.where(row == 5, jnp.maximum(mine, other), mine + other)


def final_kernel(count, *refs):
    parts, (norms, firsts, seconds), refs = refs[:count], refs[count : count + 3], refs[count + 3 :]
    masters, updates, news = refs[:4], refs[4:8], refs[8:12]
    norms_out, first_out, second_out, table_out, mean_out, peak_out = refs[12:]
    level = [part[...] for part in parts]
    while len(level) > 1:
        level = [merge_small(level[i], level[i + 1]) for i in range(0, len(level), 2)]
    small = level[0]
    roots = jnp.sqrt(small[6:8, 0:128])
    for i in range(4):
        ratio = roots[0:1, i : i + 1] / (roots[1:2, i : i + 1] + RATIO_EPSILON)
        news[i][...] = masters[i][...] - LEARNING_RATE * ratio * updates[i][...]
    weight = norms[...]
    first_new, second_new, update = lamb_moments(weight, small[0:4], firsts[...], seconds[...])
    weight_norm = jnp.sqrt(jnp.sum(weight * weight, axis=1, keepdims=True))
    update_norm = jnp.sqrt(jnp.sum(update * update, axis=1, keepdims=True))
    norms_out[...] = weight - LEARNING_RATE * (weight_norm / (update_norm + RATIO_EPSILON)) * update
    first_out[...] = first_new
    second_out[...] = second_new
    row = lax.broadcasted_iota(jnp.int32, (4, 128), 0)
    lane = lax.broadcasted_iota(jnp.int32, (4, 128), 1)
    low = lax.broadcasted_iota(jnp.int32, (1, 128), 1) < 4
    for k, v in enumerate((weight_norm, update_norm)):
        spread = jnp.sum(jnp.where(lane == row + 4, v, 0.0), axis=0, keepdims=True)
        table_out[k : k + 1] = jnp.where(low, roots[k : k + 1], spread)[:, 0:8]
    sums = small[4:5, 0:128]
    mean_out[...] = (sums / jnp.maximum(sums[:, ACT : ACT + 1], 1.0))[:, 0:ACT]
    peak_out[...] = small[5:6, 0:ACT]


def xor_step(v, axis, size, bit):
    return lax.ppermute(v, axis, [(i, i ^ bit) for i in range(size)])


def axis_bits(size):
    bits = []
    b = 1
    while b < size:
        bits.append(b)
        b *= 2
    return bits


def sync(*vs):
    return lax.optimization_barrier(vs)


def halving_positions(order):
    rels = [0]
    for b in reversed(order):
        rels = rels + [r ^ b for r in rels]
    return rels


def add_low(a, b):
    return (a.astype(F32) + b.astype(F32)).astype(BF16)


def const_spec(shape):
    return pl.BlockSpec(shape, lambda *a: (0,) * len(shape))


SMEM = pl.BlockSpec(memory_space=pltpu.SMEM)
ANY = pl.BlockSpec(memory_space=pl.ANY)


def kernel_call(kernel, name, grid, in_specs, out, scratch, mib, args, **more):
    return pl.pallas_call(
        kernel,
        grid=grid,
        in_specs=in_specs,
        out_specs=[spec for spec, _ in out],
        out_shape=[shape for _, shape in out],
        scratch_shapes=scratch,
        compiler_params=pltpu.CompilerParams(
            dimension_semantics=("arbitrary",) * len(grid), vmem_limit_bytes=mib * MIB
        ),
        cost_estimate=pl.CostEstimate(flops=1, bytes_accessed=1, transcendentals=0),
        name=name,
        **more,
    )(*args)


def body(n_d, n_f, *args):
    (
        tokens, cotangent, lengths, valid_mask, action_bins, value_head,
        w_triple, w_mixer, w_expand, w_reduce, norm_params,
        first_triple, first_mixer, first_expand, first_reduce, first_norms,
        second_triple, second_mixer, second_expand, second_reduce, second_norms,
    ) = args
    ep, rows, _ = tokens.shape
    flat = ep * rows
    rows16 = -(-rows // 16) * 16
    padded = -(-rows // QB) * QB
    blocks = padded // QB
    me = lax.axis_index("fsdp")
    dp = lax.axis_index("dp")
    core = dp % 2
    idx = jnp.stack([me, core]).astype(jnp.int32)
    shard = D // n_f
    h2 = FF // n_f // 2
    half_ff = FF // 2
    nh = 2 if shard >= 32 else 1
    f_bits, d_bits = axis_bits(n_f), axis_bits(n_d)
    steps_f = lambda v, b: xor_step(v, "fsdp", n_f, b)
    steps_d = lambda v, b: xor_step(v, "dp", n_d, b)

    def own_half(w):
        n = w.shape[0] // nh
        return lax.dynamic_slice_in_dim(w, core * n, n, 0) if nh == 2 else w

    def ff_half(w, h):
        return jnp.concatenate([w[:, (2 * i + h) * h2 : (2 * i + h + 1) * h2] for i in range(n_f)], axis=1)

    def under(w):
        return [w[:, q * D : (q + 1) * D] for q in range(w.shape[1] // D)]

    own_t = own_half(w_triple).astype(BF16)

    def own_piece(expand, reduce, h, first):
        rows_h = slice(h * h2, (h + 1) * h2)
        return jnp.concatenate(
            first + under(ff_half(own_half(expand), h).astype(BF16)) + [own_half(reduce[rows_h]).astype(BF16)],
            axis=0,
        )

    norm_t = norm_params.T
    norm = jnp.concatenate([norm_t, jnp.zeros((4, D), F32)], axis=0)
    ep_block = lambda width: pl.BlockSpec((1, rows, width), lambda e: (e, 0, 0))
    eps = 2 if ep % 2 == 0 else 1
    eps_block = lambda width: pl.BlockSpec((eps, rows, width), lambda e: (e, 0, 0))
    ep_shape = lambda width, dtype: jax.ShapeDtypeStruct((ep, rows, width), dtype)
    low = lambda width: (ep_block(width), ep_shape(width, BF16))
    wide = lambda width: (ep_block(width), ep_shape(width, F32))
    whole = lambda shape: (const_spec(shape), jax.ShapeDtypeStruct(shape, F32))
    norm_spec = const_spec((8, D))
    lse_spec = pl.BlockSpec((1, 16, QUAD), lambda e: (e, 0, 0))
    dma = pltpu.SemaphoreType.DMA
    wt_scratch = pltpu.VMEM((D, 3 * D), BF16)

    near = f_bits[0]
    rels_a = [0]
    for b in f_bits[1:]:
        rels_a = rels_a + [r ^ b for r in rels_a]
    rels_b = [r ^ near for r in rels_a]
    own_t, w_mixer_0, w_expand_0, w_reduce_0 = sync(own_t, w_mixer, w_expand, w_reduce)
    t_got = [steps_f(own_t, r) for r in rels_a[1:]]
    own_a = own_piece(w_expand_0, w_reduce_0, 0, [own_half(w_mixer_0).astype(BF16)])
    own_b = own_piece(w_expand_0, w_reduce_0, 1, [])
    a_near = steps_f(own_a, near)
    t_one = jnp.stack([own_t, *t_got])
    t_one, idx, norm, own_a, own_b, a_near = sync(t_one, idx, norm, own_a, own_b, a_near)
    t_two = steps_f(t_one, near)
    t_refs, t_plan = [t_one], [(rels_a, nh - 1)]
    if nh == 2:
        t_refs.append(steps_d(t_one, 1))
        t_plan.append((rels_a, 2))
    t_two, own_b = sync(t_two, own_b)
    b_near = steps_f(own_b, near)
    a_pair, b_pair = jnp.stack([own_a, a_near]), jnp.stack([own_b, b_near])
    a_got = [steps_f(a_pair, r) for r in rels_a[1:]]
    t_refs.append(t_two)
    t_plan.append((rels_b, nh - 1))
    if nh == 2:
        for i in range(0, len(rels_b), 2):
            t_refs.append(steps_d(t_two[i : i + 2], 1))
            t_plan.append((rels_b[i : i + 2], 2))
    nw = len(t_refs)
    pair_plan = [([0, near], nh - 1)]
    got_plan = [([r, r ^ near], nh - 1) for r in rels_a[1:]]
    a_refs, a_plan = [a_pair], pair_plan + got_plan
    norm, b_pair, *t_refs = sync(norm, b_pair, *t_refs)
    b_refs, b_got = [b_pair], [steps_f(b_pair, r) for r in rels_a[1:]]
    triple, n1, attended, lse = kernel_call(
        functools.partial(f1_kernel, t_plan, nw), "f1", (ep // eps,),
        [SMEM, SMEM, eps_block(D), norm_spec] + [ANY] * nw,
        [
            (eps_block(3 * D), ep_shape(3 * D, BF16)), (eps_block(D), ep_shape(D, BF16)),
            (eps_block(D), ep_shape(D, BF16)),
            (pl.BlockSpec((eps, 16, QUAD), lambda e: (e, 0, 0)), jax.ShapeDtypeStruct((ep, 16, QUAD), F32)),
        ],
        [wt_scratch, pltpu.VMEM((eps, padded, 3 * D), BF16), dma], 60,
        (idx, lengths, tokens, norm, *t_refs),
    )
    attended, *a_got = sync(attended, *a_got)
    a_refs += a_got
    if nh == 2:
        a_refs += [steps_d(v, 1) for v in [a_pair, *a_got]]
        a_plan = a_plan + [(rels, 2) for rels, _ in a_plan]
    na = len(a_refs)
    attended, *a_refs = sync(attended, *a_refs)

    order = f_bits[1:2] + f_bits[:1] + f_bits[2:]
    late = order[2:]
    pos = halving_positions(order)
    hm, hr = shard // nh, h2 // nh
    rows_a = hm * (half_ff // QUAD) + hr * (D // QUAD)
    rows_b = rows_a + hm * (D // QUAD)
    rows_t = 6 * hm
    half = n_f // 2
    low_out = lambda *shape: (const_spec(shape), jax.ShapeDtypeStruct(shape, BF16))
    ff_scratch = [
        pltpu.VMEM((D, D), BF16), pltpu.VMEM((D, half_ff), BF16), pltpu.VMEM((half_ff, D), BF16),
        pltpu.VMEM((D, half_ff), F32), pltpu.VMEM((D, half_ff), F32),
    ]
    fl = flat // 3 if flat % 48 == 0 else rows
    fl_steps = flat // fl
    fl_block = lambda width, at=0: pl.BlockSpec((fl, width), lambda i: (i + at, 0))
    fl_low = lambda width: (fl_block(width), jax.ShapeDtypeStruct((flat, width), BF16))
    fl_wide = lambda width: (fl_block(width), jax.ShapeDtypeStruct((flat, width), F32))
    tok_flat = tokens.reshape(flat, D)
    cot_flat = cotangent.reshape(flat, D)
    attended = attended.reshape(flat, D)
    hidden, out_part, g2_part, n2, keep_a, send_a = kernel_call(
        functools.partial(f2a_kernel, a_plan, na, pos, rows), "f2a", (fl_steps,),
        [SMEM, SMEM] + [fl_block(D)] * 3 + [norm_spec] + [ANY] * na,
        [fl_wide(D)] * 3 + [fl_low(D)] + [low_out(nh, half, rows_a, QUAD)] * 2,
        ff_scratch + [pltpu.SemaphoreType.DMA((2,))], 60, (idx, lengths, attended, tok_flat, cot_flat, norm, *a_refs),
    )

    def halves(keep, got):
        n = keep.shape[-3] // 2
        return add_low(keep[..., :n, :, :], got[..., :n, :, :]), add_low(keep[..., n:, :, :], got[..., n:, :, :])

    def core_pair(total):
        return (total[0], steps_d(total[1], 1)) if nh == 2 else (total[0], None)

    def core_halves_of(pair):
        mine, other = pair
        n = mine.shape[0] // 2
        return halves(mine, other) if other is not None else (mine[:n], mine[n:])

    def core_add(pair):
        return add_low(*pair) if pair[1] is not None else pair[0]

    n2, keep_a, send_a, *b_got = sync(n2, keep_a, send_a, *b_got)
    b_refs += b_got
    if nh == 2:
        b_refs += [steps_d(v, 1) for v in [b_pair, *b_got]]
    n2, keep_a, send_a, *b_refs = sync(n2, keep_a, send_a, *b_refs)
    got_a = steps_f(send_a, order[0])
    block_out, gh, ga, *rest = kernel_call(
        functools.partial(f2b_kernel, a_plan, na, pos, nh, rows), "f2b", (fl_steps,),
        [SMEM, SMEM] + [fl_block(D)] * 6 + [norm_spec] + [ANY] * (2 * na),
        [fl_low(D), fl_wide(D), fl_low(D)] + [low_out(n_f, rows_b, QUAD)] * nh + [whole((8, D))],
        ff_scratch + [pltpu.VMEM((D, D), F32), pltpu.SemaphoreType.DMA((2,))], 54,
        (idx, lengths, attended, hidden, out_part, g2_part, n2, cot_flat, norm, *a_refs, *b_refs),
    )
    grads_b, ln2 = rest[:nh], rest[nh]
    ga, valid_mask, action_bins, keep_a, got_a, *grads_b = sync(
        ga, valid_mask, action_bins, keep_a, got_a, *grads_b
    )
    pair_b = core_pair(grads_b)
    places = jnp.arange(rows)
    inside = places[None, :] < lengths[:, None]
    counted = ((valid_mask == 1) & inside).astype(jnp.int32).reshape(1, flat)
    bins_t = action_bins.reshape(flat, ACT).T
    sum_a = add_low(keep_a, got_a)
    pair_a = core_pair(sum_a)
    keep_b, send_b = core_halves_of(pair_b)
    keep_a, send_a = core_halves_of(pair_a)
    ga, counted, bins_t, keep_a, send_a, keep_b, send_b = sync(ga, counted, bins_t, keep_a, send_a, keep_b, send_b)

    got_b = steps_f(send_b, order[0])
    got_a = steps_f(send_a, order[1])
    pack_rows = ep * rows16 + PACK
    gtri, *grads_t = kernel_call(
        functools.partial(b1_kernel, pos, nh), "b1", (ep // eps,),
        [SMEM, SMEM, eps_block(3 * D), eps_block(D), pl.BlockSpec((eps, 16, QUAD), lambda e: (e, 0, 0)), eps_block(D)],
        [(eps_block(3 * D), ep_shape(3 * D, BF16))] + [low_out(n_f, rows_t, QUAD)] * nh,
        [
            pltpu.VMEM((eps, padded, 3 * D), BF16), pltpu.VMEM((eps, padded, D), BF16),
            pltpu.VMEM((eps, padded, 3 * D), BF16), pltpu.VMEM((eps, rows16, D), F32),
            pltpu.VMEM((eps, rows16, D), F32), pltpu.VMEM((D, 3 * D), F32),
            pltpu.VMEM((pack_rows, D), BF16), pltpu.VMEM((pack_rows, 3 * D), BF16),
        ],
        48, (idx, lengths, triple, ga.reshape(ep, rows, D), lse, n1),
    )
    gtri, keep_a, got_a, keep_b, got_b, *grads_t = sync(gtri, keep_a, got_a, keep_b, got_b, *grads_t)

    mine_t, other_t = core_pair(grads_t)
    keep_b, send_b = halves(keep_b, got_b)
    if late:
        keep_a, send_a = halves(keep_a, got_a)
    else:
        keep_a, send_a = add_low(keep_a, got_a), keep_a
    mine_t, other_t, keep_a, send_a, keep_b, send_b = sync(mine_t, other_t, keep_a, send_a, keep_b, send_b)
    keep_t, send_t = core_halves_of((mine_t, other_t))
    block_out, keep_t, send_t, keep_a, send_a, keep_b, send_b = sync(
        block_out, keep_t, send_t, keep_a, send_a, keep_b, send_b
    )
    got_t = steps_f(send_t, order[0])
    got_b = steps_f(send_b, order[1])
    if late:
        got_a = steps_f(send_a, late[0])

    qb = 256
    steps = -(-flat // qb)
    q_sum, q_top = kernel_call(
        functools.partial(q_kernel, flat), "qstat", (steps,),
        [
            pl.BlockSpec((qb, D), lambda i: (i, 0)), const_spec((ACT * NBINS, D)),
            pl.BlockSpec((ACT, qb), lambda i: (0, i)), pl.BlockSpec((1, qb), lambda i: (0, i)),
        ],
        [whole((16, qb))] * 2, [], 20, (block_out, value_head, bins_t, counted),
    )
    gtri, q_sum, keep_t, got_t, keep_b, got_b = sync(gtri, q_sum, keep_t, got_t, keep_b, got_b)

    def b2_call(at, n, gtri, prior, more_in):
        extra = [] if prior is None else [prior, *more_in]
        specs = [] if prior is None else [ANY] + [const_spec(v.shape) for v in more_in]
        more = {} if prior is None else {"input_output_aliases": {5 + nw: 0}}
        return kernel_call(
            functools.partial(b2_kernel, t_plan, nw, prior is None), "b2", (n,),
            [SMEM, fl_block(3 * D, at), fl_block(D, at), fl_block(D, at), norm_spec] + [ANY] * nw + specs,
            [(fl_block(D, at), jax.ShapeDtypeStruct((flat, D), BF16)), whole((8, D))],
            [wt_scratch, dma], 28, (idx, gtri, tok_flat, gh, norm, *t_refs, *extra), **more,
        )

    keep_t, send_t = halves(keep_t, got_t)
    if late:
        keep_b, send_b = halves(keep_b, got_b)
    else:
        keep_b, send_b = add_low(keep_b, got_b), keep_b
    gtri_flat = gtri.reshape(flat, 3 * D)

    def finish(keep, bits):
        for b in bits:
            n = keep.shape[0] // 2
            keep = add_low(keep[:n], steps_f(keep[n:], b))
        return keep[0]

    x_bits = d_bits[nh - 1 :]

    def before_x(keep):
        red = finish(keep, late[1:])
        for b in x_bits[:-1]:
            red = add_low(red, steps_d(red, b))
        return red

    if late:
        keep_a = add_low(keep_a, got_a)
    red_a = before_x(keep_a)
    gtri_flat, keep_t, send_t, keep_b, send_b, red_a = sync(gtri_flat, keep_t, send_t, keep_b, send_b, red_a)
    got_t = steps_f(send_t, order[1])
    if late:
        got_b = steps_f(send_b, late[0])
    cut = (fl_steps + 1) // 2
    got_ra = steps_d(red_a, x_bits[-1])
    ig_part, ln1_a = b2_call(0, cut, gtri_flat, None, ())
    ig_part, keep_t, got_t, got_ra = sync(ig_part, keep_t, got_t, got_ra)
    if late:
        keep_t, send_t = halves(keep_t, got_t)
        got_t = steps_f(send_t, late[0])
        keep_b = add_low(keep_b, got_b)
    else:
        keep_t = add_low(keep_t, got_t)
    red_b = before_x(keep_b)
    red_b, ig_part = sync(red_b, ig_part)
    got_rb = steps_d(red_b, x_bits[-1])
    input_grad, small = b2_call(cut, fl_steps - cut, gtri_flat, ig_part, (ln1_a, ln2, q_sum, q_top))
    small, red_a, got_ra, red_b, got_rb, keep_t, *got_t = sync(
        small, red_a, got_ra, red_b, got_rb, keep_t, *([got_t] if late else [])
    )

    red_t = before_x(add_low(keep_t, got_t[0]) if late else keep_t)
    got_rt = steps_d(red_t, x_bits[-1])
    both_sum = lambda a, b: a.astype(F32) + b.astype(F32)
    red = jnp.concatenate([both_sum(red_a, got_ra), both_sum(red_b, got_rb)], axis=0)
    red_parts = [red] + ([steps_d(red, 1)] if nh == 2 else [])
    small_core = steps_d(small, d_bits[0])
    red_t, *red_parts = sync(red_t, *red_parts)
    like = lambda w: whole(w.shape)
    full = lambda *ws: [pl.BlockSpec(memory_space=pltpu.VMEM)] * len(ws)
    mlp_state = (
        w_mixer, first_mixer, second_mixer, w_expand, first_expand, second_expand,
        w_reduce, first_reduce, second_reduce,
    )
    *mlp_out, sq_mlp = kernel_call(
        functools.partial(lamb_mlp_kernel, n_f, nh, rows_a), "lamb_mlp", (1,),
        [SMEM] + full(*red_parts, *mlp_state),
        [like(w) for w in (w_mixer, w_expand, w_reduce) for _ in range(3)] + [whole((8, 128))],
        [], 20, (idx, *red_parts, *mlp_state),
    )
    small, small_core, sq_mlp, red_t, got_rt = sync(small, small_core, sq_mlp, red_t, got_rt)
    small = merge_small(small, small_core)
    for b in d_bits[1:]:
        small = merge_small(small, steps_d(small, b))
    red_t = red_t.astype(F32) + got_rt.astype(F32)
    parts_t = [red_t] + ([steps_d(red_t, 1)] if nh == 2 else [])
    tri_state = (w_triple, first_triple, second_triple)
    *tri_out, squares = kernel_call(
        functools.partial(lamb_triple_kernel, n_f, nh), "lamb_triple", (1,),
        [SMEM] + full(*parts_t, sq_mlp, *tri_state),
        [like(w_triple)] * 3 + [whole((8, 128))],
        [], 12, (idx, *parts_t, sq_mlp, *tri_state),
    )

    small = small + jnp.pad(squares, ((0, 0), (0, D - 128)))
    for b in f_bits[:-2]:
        small = merge_small(small, steps_f(small, b))
    far = [0]
    for b in f_bits[-2:]:
        far = far + [r ^ b for r in far]
    smalls = [small] + [steps_f(small, r) for r in far[1:]]
    masters = (w_triple, w_mixer, w_expand, w_reduce)
    updates = (tri_out[2], mlp_out[2], mlp_out[5], mlp_out[8])
    firsts_t, seconds_t = first_norms.T, second_norms.T
    *news, norms_out, first_out, second_out, norm_table, mean, peak = kernel_call(
        functools.partial(final_kernel, len(smalls)), "final", (1,),
        full(*smalls, norm_t, firsts_t, seconds_t, *masters, *updates),
        [like(w) for w in masters]
        + [whole((4, D))] * 3 + [whole((2, 8)), whole((1, ACT)), whole((1, ACT))],
        [], 16, (*smalls, norm_t, firsts_t, seconds_t, *masters, *updates),
    )
    return (
        block_out.reshape(ep, rows, D), input_grad.reshape(ep, rows, D), *news,
        tri_out[0], mlp_out[0], mlp_out[3], mlp_out[6],
        tri_out[1], mlp_out[1], mlp_out[4], mlp_out[7],
        norms_out.T, first_out.T, second_out.T, norm_table, mean.reshape(ACT), peak.reshape(ACT),
    )


def solution(mesh):
    n_d, n_f = mesh.shape["dp"], mesh.shape["fsdp"]
    both = ("dp", "fsdp")
    row, rep = P("fsdp", None), P()
    in_specs = (
        P(both, None, None), P(both, None, None), P(both), P(both, None), P(both, None, None), rep,
        row, row, row, row, rep,
        row, row, row, row, rep,
        row, row, row, row, rep,
    )
    out_specs = (
        (P(both, None, None),) * 2 + (row,) * 12 + (rep,) * 6
    )
    return jax.shard_map(
        functools.partial(body, n_d, n_f), mesh=mesh, in_specs=in_specs, out_specs=out_specs,
        check_vma=False,
    )
```
